32 devices in a mesh: dp: 16 (over z, y, core), tensor: 2 (over x).
Axes of the slice: x: 2, y: 2, z: 4, core: 2. Of those that a mesh axis runs over, the one named last changes fastest.
Arguments:
- tokens: bfloat16 [32768, 1024], P('dp'), may hold values from -6 to 6
- cotangent: bfloat16 [32768, 1024], P('dp'), may hold values from -6 to 6
- segments: int32 [32768], P('dp'), may hold values from 0 to 2, as said below
- routes: int32 [32768, 8], P('dp'), may hold values from 0 to 31, as said below
- slot_index: int32 [32768, 8], P('dp'), may hold values from 0 to 256, as said below
- w_query: bfloat16 [1024, 1024], P(None, 'tensor'), may hold values from -0.1875 to 0.1875
- w_key: bfloat16 [1024, 512], P(None, 'tensor'), may hold values from -0.1875 to 0.1875
- w_value: bfloat16 [1024, 512], P(None, 'tensor'), may hold values from -0.1875 to 0.1875
- w_output: bfloat16 [1024, 1024], P('tensor'), may hold values from -1.5 to 1.5
- norm_attn: bfloat16 [1024], replicated, may hold values from 0.5 to 1.5
- norm_ffn: bfloat16 [1024], replicated, may hold values from 0.5 to 1.5
- w_router: bfloat16 [1024, 32], replicated, may hold values from -0.09375 to 0.09375
- w_gate: bfloat16 [4, 1024, 512], P(None, None, 'tensor'), may hold values from -0.1875 to 0.1875
- w_up: bfloat16 [4, 1024, 512], P(None, None, 'tensor'), may hold values from -0.1875 to 0.1875
- w_down: bfloat16 [4, 512, 1024], P(None, 'tensor'), may hold values from -1.5 to 1.5
Outputs:
- block_output: bfloat16 [32768, 1024], P('dp')
- token_grad: float32 [32768, 1024], P('dp')
- grad_query: float32 [1024, 1024], P(None, 'tensor')
- grad_key: float32 [1024, 512], P(None, 'tensor')
- grad_value: float32 [1024, 512], P(None, 'tensor')
- grad_output: float32 [1024, 1024], P('tensor')
- grad_norm_attn: float32 [1024], replicated
- grad_norm_ffn: float32 [1024], replicated
- grad_router: float32 [1024, 32], replicated
- grad_gate: float32 [4, 1024, 512], P(None, None, 'tensor')
- grad_up: float32 [4, 1024, 512], P(None, None, 'tensor')
- grad_down: float32 [4, 512, 1024], P(None, 'tensor')
The draws below stay inside these ranges and needn't reach their ends.
Inputs may be any that keep to these rules, and one draw needn't show every extreme that they name: `routes`: each token names 8 different experts. In every draw one expert below 4 is named by every token. slot_index[t, k] counts the routes to the same expert that come before (t, k) among the tokens of t's sequence of 1024 tokens, in token order and then route order; it is 256 where that count is 256 or more, and where routes[t, k] is 4 or more. `segments`: within each sequence of 1024 tokens the numbers start at 0 and never fall; every document has 256 tokens or more.
All inputs are finite; a program needn't handle non-finite values.
Results may differ from the reference program's by a relative error of at most 0.011.
The reference program's roundings to bfloat16 on the way count: a program that leaves them out, or rounds other values in their place, can miss the bound.
Values may be sent and summed in bfloat16 or wider, within the bound.
No kernel may reach another device: no remote copies, remote signals or barrier semaphores. Data moves between devices by JAX's collectives and lax.ppermute only.
A program may use at most 256 MiB of HBM per device.

```python
import jax
import jax.numpy as jnp
from jax import lax

D = 1024
HEADS = 16
KV_HEADS = 8
HEAD_DIM = 64
FF = 512
EXPERTS = 32
TOP = 8
EXP_WIN = 4
SEQ_LEN = 1024
SEQS = 2
CAP = 256
TOKENS = 32768
N_DP = 16


def route_table(key):
    first_key, second_key, third_key = jax.random.split(key, 3)
    busy_expert = jax.random.randint(first_key, (), 0, EXP_WIN)
    expert_ids = jnp.arange(EXPERTS, dtype=jnp.int32)
    scores = jax.random.randint(second_key, (TOKENS, EXPERTS), 0, 1 << 20) * EXPERTS + expert_ids[None, :]
    scores = jnp.where(expert_ids[None, :] == busy_expert, 1 << 30, scores)
    chosen = lax.top_k(scores, TOP)[1].astype(jnp.int32)
    shuffle = jax.random.randint(third_key, (TOKENS, TOP), 0, 1 << 20) * TOP + jnp.arange(TOP, dtype=jnp.int32)[None, :]
    ranking = jnp.argsort(shuffle, axis=1)
    return jnp.take_along_axis(chosen, ranking, axis=1).astype(jnp.int32)


def draw_routes(key, part):
    return route_table(key)


def draw_slot_index(key, part):
    routes = route_table(key)
    blocks = routes.reshape(N_DP * SEQS, SEQ_LEN * TOP)
    onehot = (blocks[:, :, None] == jnp.arange(EXPERTS, dtype=jnp.int32)[None, None, :]).astype(jnp.int32)
    before = jnp.cumsum(onehot, axis=1) - onehot
    position = jnp.sum(before * onehot, axis=2)
    inside = blocks < EXP_WIN
    slots = jnp.where(inside, jnp.minimum(position, CAP), CAP)
    return slots.reshape(TOKENS, TOP).astype(jnp.int32)


def draw_segments(key, part):
    key = jax.random.fold_in(key, 7)
    first_key, second_key = jax.random.split(key)
    count = N_DP * SEQS
    quarter = SEQ_LEN // 4
    first_cut = jax.random.randint(first_key, (count, 1), quarter, SEQ_LEN // 2)
    second_cut = jax.random.randint(second_key, (count, 1), first_cut + quarter, SEQ_LEN - quarter + 1)
    positions = jnp.arange(SEQ_LEN, dtype=jnp.int32)[None, :]
    numbers = (positions >= first_cut).astype(jnp.int32) + (positions >= second_cut).astype(jnp.int32)
    return numbers.reshape(TOKENS).astype(jnp.int32)


def strengthened(values, rng, source, target, shards_of, factor):
    owner, partner = [(jnp.arange(values.shape[dim]) // (values.shape[dim] // shards_of)).reshape([-1 if axis == dim else 1 for axis in range(values.ndim)]) for dim in (source, target)]
    chosen = jax.random.permutation(rng, shards_of)[partner]
    strong = (owner == chosen) | (owner == (partner + shards_of // 2) % shards_of)
    return jnp.where(strong, factor * values, values)


def steps_of(own_key, dims, cuts, low, high):
    def one(dim, blocks):
        steps = jax.random.uniform(jax.random.fold_in(jax.random.fold_in(own_key, 6), dim), (blocks,), jnp.float32, low / len(cuts), high / len(cuts))
        return jnp.repeat(jnp.exp(steps), dims[dim] // blocks).reshape((-1,) + (1,) * (len(dims) - dim - 1))

    factor_of = one(*cuts[0])
    for cut in cuts[1:]:
        factor_of = factor_of * one(*cut)
    return factor_of


def centred(own_key, dims, width, limit, cuts=(), held_as=jnp.bfloat16):
    entries = jax.random.normal(own_key, dims, jnp.float32) * width
    if len(cuts) > 0:
        entries = steps_of(own_key, dims, cuts, -0.22, 0.18) * entries
    return jnp.clip(entries, min=-limit, max=limit).astype(held_as)


def bell_draw_with(key, dims, width, most, cuts, heavy, kind=jnp.bfloat16):
    entries = width * jax.random.normal(key, dims, jnp.float32)
    if cuts:
        entries = entries * steps_of(key, dims, cuts, -0.22, 0.18)
    return jnp.clip(strengthened(entries, jax.random.fold_in(key, 3), *heavy), -most, most).astype(kind)


def setup_inputs(seed: int = 0) -> dict:
    key_of = jax.random.split(jax.random.key(seed), 16)
    tokens = centred(key_of[0], (TOKENS, D), 1.0, 6.0, ((0, 16),))
    cotangent = bell_draw_with(key_of[1], (TOKENS, D), 1.0, 6.0, ((0, 16),), (0, 1, 16, 2.0))
    segments = draw_segments(jax.random.fold_in(key_of[15], 71), 0)
    routes = draw_routes(jax.random.fold_in(key_of[15], 71), 0)
    slot_index = draw_slot_index(jax.random.fold_in(key_of[15], 71), 0)
    w_query = centred(key_of[5], (D, HEADS * HEAD_DIM), D ** -0.5, 0.1875, ((1, 2),))
    w_key = centred(key_of[6], (D, KV_HEADS * HEAD_DIM), D ** -0.5, 0.1875, ((1, 2),))
    w_value = centred(key_of[7], (D, KV_HEADS * HEAD_DIM), D ** -0.5, 0.1875, ((1, 2),))
    w_output = centred(key_of[8], (HEADS * HEAD_DIM, D), HEADS ** -0.5, 1.5, ((0, 2),))
    norm_attn = jnp.clip(1.0 + 0.1 * jax.random.normal(key_of[9], (D,), jnp.float32), 0.5, 1.5).astype(jnp.bfloat16)
    norm_ffn = jnp.clip(1.0 + 0.1 * jax.random.normal(key_of[10], (D,), jnp.float32), 0.5, 1.5).astype(jnp.bfloat16)
    w_router = centred(key_of[11], (D, EXPERTS), (4 * D) ** -0.5, 0.09375)
    w_gate = centred(key_of[12], (EXP_WIN, D, FF), D ** -0.5, 0.1875, ((2, 2),))
    w_up = centred(key_of[13], (EXP_WIN, D, FF), D ** -0.5, 0.1875, ((2, 2),))
    w_down = centred(key_of[14], (EXP_WIN, FF, D), (FF // 32) ** -0.5, 1.5, ((1, 2),))
    return dict(tokens=tokens, cotangent=cotangent, segments=segments, routes=routes, slot_index=slot_index, w_query=w_query, w_key=w_key, w_value=w_value, w_output=w_output, norm_attn=norm_attn, norm_ffn=norm_ffn, w_router=w_router, w_gate=w_gate, w_up=w_up, w_down=w_down)


EPS = 1e-06
THETA = 10000.0
NEG = -1e+30

@jax.custom_vjp
def low(v):
    return lax.optimization_barrier(v.astype(jnp.bfloat16)).astype(jnp.float32)

@jax.custom_vjp
def low_back(v):
    return v

def low_keep(v):
    return (low(v), None)

def low_pass(kept, grad):
    return (grad,)

def back_keep(v):
    return (v, None)

def back_low(kept, grad):
    return (low(grad),)
low.defvjp(low_keep, low_pass)
low_back.defvjp(back_keep, back_low)

def exact_dot(left, right):
    return jnp.dot(left, right, precision=lax.Precision.HIGHEST, preferred_element_type=jnp.float32)

def rmsnorm(values, gain_row):
    return values * lax.rsqrt(lax.optimization_barrier(jnp.mean(values * values, axis=-1, keepdims=True)) + EPS) * gain_row

def rotary_tables(segments, head_size):
    earlier = lax.optimization_barrier(jnp.sum((segments[None, :] < segments[:, None]).astype(jnp.int32), axis=1))
    positions = (jnp.arange(segments.shape[0], dtype=jnp.int32) - earlier).astype(jnp.float32)
    half_dim = head_size // 2
    frequency = THETA ** (-(2.0 * jnp.arange(half_dim, dtype=jnp.float32)) / head_size)
    angles = positions[:, None] * frequency[None, :]
    angles = jnp.concatenate([angles, angles], axis=1)
    return (jnp.cos(angles)[:, None, :], jnp.sin(angles)[:, None, :])

def rotate(values, cosine, sine):
    half_dim = values.shape[-1] // 2
    turned = jnp.concatenate([-values[..., half_dim:], values[..., :half_dim]], axis=-1)
    return values * cosine + turned * sine

def block_forward(inputs, w_query, w_key, w_value, w_output, norm_attn, norm_ffn, w_router, w_gate, w_up, w_down, segments, routes, slot_index):
    length = inputs.shape[0]
    model_width = inputs.shape[1]
    groups = HEADS // KV_HEADS
    first = low(rmsnorm(inputs, norm_attn))
    cosine, sine = rotary_tables(segments, HEAD_DIM)
    query_heads = low(rotate(low_back(exact_dot(first, w_query)).reshape(length, HEADS, HEAD_DIM), cosine, sine))
    key_heads = low(rotate(low_back(exact_dot(first, w_key)).reshape(length, KV_HEADS, HEAD_DIM), cosine, sine))
    value_heads = low(low_back(exact_dot(first, w_value))).reshape(length, KV_HEADS, HEAD_DIM)
    keys_all = jnp.repeat(key_heads, groups, axis=1)
    values_all = jnp.repeat(value_heads, groups, axis=1)
    raw_scores = low_back(jnp.einsum('qhd,shd->hqs', query_heads, keys_all, precision=lax.Precision.HIGHEST))
    positions = jnp.arange(length)
    allowed = (positions[None, :] <= positions[:, None]) & (segments[None, :] == segments[:, None])
    scores = jnp.where(allowed[None, :, :], raw_scores * HEAD_DIM ** (-0.5), NEG)
    row_max = lax.optimization_barrier(jnp.max(scores, axis=-1, keepdims=True))
    weights = jnp.exp(scores - row_max)
    probs_low = low(weights / lax.optimization_barrier(jnp.sum(weights, axis=-1, keepdims=True)))
    attended = jnp.einsum('hqs,shd->qhd', probs_low, values_all, precision=lax.Precision.HIGHEST).reshape(length, HEADS * HEAD_DIM)
    attended = low(low_back(attended))
    resid = inputs + low_back(exact_dot(attended, w_output))
    second = low(rmsnorm(resid, norm_ffn))
    logits = exact_dot(second, w_router)
    gate_values = jax.nn.softmax(jnp.take_along_axis(logits, routes, axis=1), axis=-1)
    in_window = (routes < EXP_WIN) & (slot_index < CAP)
    target = jnp.where(in_window, routes * CAP + slot_index, EXP_WIN * CAP).reshape(-1).astype(jnp.int32)
    route_count = length * TOP
    route_of = jnp.full((EXP_WIN * CAP + 1,), route_count, jnp.int32).at[target].set(jnp.arange(route_count, dtype=jnp.int32))[:EXP_WIN * CAP]
    token_of = route_of // TOP
    padded = jnp.concatenate([second, jnp.zeros((1, model_width), jnp.float32)], axis=0)
    expert_in = padded[token_of].reshape(EXP_WIN, CAP, model_width)
    gate_pre = low_back(jnp.einsum('ecd,edf->ecf', expert_in, w_gate, precision=lax.Precision.HIGHEST))
    up_pre = low_back(jnp.einsum('ecd,edf->ecf', expert_in, w_up, precision=lax.Precision.HIGHEST))
    hidden = low(jax.nn.silu(gate_pre) * up_pre)
    expert_out = low_back(jnp.einsum('ecf,efd->ecd', hidden, w_down, precision=lax.Precision.HIGHEST)).reshape(EXP_WIN * CAP, model_width)
    out_pad = jnp.concatenate([expert_out, jnp.zeros((1, model_width), jnp.float32)], axis=0)
    picked = out_pad[target].reshape(length, TOP, model_width)
    weighted = gate_values * in_window.astype(jnp.float32)
    return resid + lax.optimization_barrier(jnp.sum(weighted[:, :, None] * picked, axis=1))

def reference(tokens, cotangent, segments, routes, slot_index, w_query, w_key, w_value, w_output, norm_attn, norm_ffn, w_router, w_gate, w_up, w_down):
    params = (w_query.astype(jnp.float32), w_key.astype(jnp.float32), w_value.astype(jnp.float32), w_output.astype(jnp.float32), norm_attn.astype(jnp.float32), norm_ffn.astype(jnp.float32), w_router.astype(jnp.float32), w_gate.astype(jnp.float32), w_up.astype(jnp.float32), w_down.astype(jnp.float32))
    count = N_DP * SEQS
    block_inputs = tokens.astype(jnp.float32).reshape(count, SEQ_LEN, D)
    block_grads = cotangent.astype(jnp.float32).reshape(count, SEQ_LEN, D)
    block_segments = segments.reshape(count, SEQ_LEN)
    block_routes = routes.reshape(count, SEQ_LEN, TOP)
    block_slots = slot_index.reshape(count, SEQ_LEN, TOP)

    def one_block(totals, pieces):
        inputs, upstream, segs, route_rows, slot_rows = pieces

        def forward(inputs, wq, wk, wv, wo, gone, gtwo, wr, wg, wu, wd):
            return block_forward(inputs, wq, wk, wv, wo, gone, gtwo, wr, wg, wu, wd, segs, route_rows, slot_rows)
        output, backward = jax.vjp(forward, inputs, *params)
        cotangents = backward(upstream)
        updated = tuple((first + second for first, second in zip(totals, cotangents[1:])))
        return (updated, (output.astype(jnp.bfloat16), cotangents[0]))
    starting = tuple((jnp.zeros_like(entry) for entry in params))
    totals, (outputs, token_grads) = lax.scan(one_block, starting, (block_inputs, block_grads, block_segments, block_routes, block_slots))
    return (outputs.reshape(TOKENS, D), token_grads.reshape(TOKENS, D), totals[0], totals[1], totals[2], totals[3], totals[4], totals[5], totals[6], totals[7], totals[8], totals[9])
```

```python
from functools import partial

import jax
import jax.numpy as jnp
from jax import lax
from jax.experimental import pallas as pl
from jax.experimental.pallas import tpu as pltpu
from jax.sharding import PartitionSpec as P

HEAD_DIM = 64
SEQ_LEN = 1024
CAP = 256
EPS = 1e-06
THETA = 10000.0
NEG = -1e30
BLOCK = 256
LANES = 128
GROUP = 4 * HEAD_DIM

f32 = jnp.float32
bf16 = jnp.bfloat16


def nn(left, right):
    return lax.dot_general(left, right, (((1,), (0,)), ((), ())), preferred_element_type=f32)


def nt(left, right):
    return lax.dot_general(left, right, (((1,), (1,)), ((), ())), preferred_element_type=f32)


def tn(left, right):
    return lax.dot_general(left, right, (((0,), (0,)), ((), ())), preferred_element_type=f32)


def params(count=1):
    return pltpu.CompilerParams(
        dimension_semantics=("arbitrary",) * count, vmem_limit_bytes=56 * 1024 * 1024
    )


def whole(shape):
    return pl.BlockSpec(shape, lambda *_: (0,) * len(shape))


def lane_iota(rows, lanes=LANES):
    return lax.broadcasted_iota(jnp.int32, (rows, lanes), 1)


def prologue_kernel(x_ref, gain_ref, seg_ref, freq_ref, first_ref, first_t_ref, cos_ref, up_ref, down_ref):
    rows = x_ref.shape[0]
    values = x_ref[...].astype(f32)
    scale = lax.rsqrt(jnp.mean(values * values, axis=-1, keepdims=True) + EPS)
    normed = values * scale * gain_ref[...].astype(f32)
    first_ref[...] = normed.astype(bf16)
    first_t_ref[...] = normed.astype(bf16).T
    seg = seg_ref[...]
    zeros = jnp.sum((seg == 0).astype(f32), axis=1, keepdims=True)
    ones = jnp.sum((seg == 1).astype(f32), axis=1, keepdims=True)
    places = lax.broadcasted_iota(jnp.int32, (1, rows), 1).astype(f32)
    places = places - jnp.where(seg >= 1, zeros, 0.0) - jnp.where(seg >= 2, ones, 0.0)
    angles = freq_ref[:, 0:1] * places
    cosine = jnp.cos(angles)
    sine = jnp.sin(angles)
    cosine = jnp.concatenate([cosine] * 4, axis=0).T
    sine = jnp.concatenate([sine] * 4, axis=0).T
    lower = (lane_iota(rows) % HEAD_DIM) < HEAD_DIM // 2
    cos_ref[...] = cosine
    up_ref[...] = jnp.where(lower, -sine, 0.0)
    down_ref[...] = jnp.where(lower, 0.0, sine)


def prologue(x, gain, seg_row, freq):
    rows, width = x.shape
    table = jax.ShapeDtypeStruct((rows, LANES), f32)
    return pl.pallas_call(
        prologue_kernel,
        out_shape=(
            jax.ShapeDtypeStruct((rows, width), bf16),
            jax.ShapeDtypeStruct((width, rows), bf16),
            table,
            table,
            table,
        ),
        compiler_params=pltpu.CompilerParams(vmem_limit_bytes=56 * 1024 * 1024),
        name="prologue",
    )(x, gain, seg_row, freq)


def rotate(values, cosine, up, down):
    return (
        values * cosine
        + pltpu.roll(values, LANES - 32, 1) * up
        + pltpu.roll(values, 32, 1) * down
    )


def rotate_back(values, cosine, up, down):
    return (
        values * cosine
        - pltpu.roll(values, LANES - 32, 1) * up
        - pltpu.roll(values, 32, 1) * down
    )


def doubled(values):
    turned = pltpu.roll(values, HEAD_DIM, 1)
    left = lane_iota(values.shape[0]) < HEAD_DIM
    return (
        jnp.where(left, values, turned).astype(bf16),
        jnp.where(left, turned, values).astype(bf16),
    )


def halves_mask():
    left = (lane_iota(1) < HEAD_DIM).astype(f32)
    return left.astype(bf16), (1.0 - left).astype(bf16)


def attend_kernel(
    first_ref, wq_ref, wk_ref, wv_ref, cos_ref, up_ref, down_ref, segc_ref, segr_ref,
    q_ref, k_ref, v_ref, att_ref, lse_ref, bias_ref,
):
    rows = first_ref.shape[0]

    @pl.when(pl.program_id(0) == 0)
    def _():
        for start in range(0, rows, BLOCK):
            at_row = lax.broadcasted_iota(jnp.int32, (BLOCK, rows), 0) + start
            at_col = lax.broadcasted_iota(jnp.int32, (BLOCK, rows), 1)
            allowed = (at_col <= at_row) & (segc_ref[start : start + BLOCK, :] == segr_ref[...])
            bias_ref[start : start + BLOCK, :] = jnp.where(allowed, 0.0, NEG)

    first = first_ref[...]
    cosine, up, down = cos_ref[...], up_ref[...], down_ref[...]
    for tile in range(2):
        part = slice(tile * LANES, (tile + 1) * LANES)
        raw = nn(first, wq_ref[:, part])
        q_ref[:, part] = (rotate(raw, cosine, up, down) * HEAD_DIM**-0.5).astype(bf16)
    key = rotate(nn(first, wk_ref[...]), cosine, up, down)
    value = nn(first, wv_ref[...])
    k_ref[...] = key.astype(bf16)
    v_ref[...] = value.astype(bf16)
    keys, values = doubled(key), doubled(value)
    low, high = halves_mask()
    for start in range(0, rows, BLOCK):
        width = start + BLOCK
        mine = slice(start, width)
        bias = bias_ref[mine, :width]
        bias = jnp.concatenate([bias, bias], axis=0)
        logs = jnp.zeros((BLOCK, LANES), f32)
        lanes = lane_iota(BLOCK)
        for kv in range(2):
            part = slice(kv * LANES, (kv + 1) * LANES)
            query = q_ref[mine, part]
            query = jnp.concatenate([query * low, query * high], axis=0)
            scores = nt(query, keys[kv][:width]) + bias
            row_max = jnp.max(scores, axis=-1, keepdims=True)
            weights = jnp.exp(scores - row_max)
            total = jnp.sum(weights, axis=-1, keepdims=True)
            probs = (weights * (1.0 / total)).astype(bf16)
            out = nn(probs, values[kv][:width])
            att_ref[mine, part] = jnp.where(lanes < HEAD_DIM, out[:BLOCK], out[BLOCK:]).astype(bf16)
            log_total = row_max + jnp.log(total)
            logs = jnp.where(lanes == 2 * kv, log_total[:BLOCK], logs)
            logs = jnp.where(lanes == 2 * kv + 1, log_total[BLOCK:], logs)
        lse_ref[0, :, mine] = logs.T[:8]


def attend(first, wq, wk, wv, tables, seg_col, seg_row):
    rows, width = first.shape
    groups = wq.shape[1] // GROUP
    table = whole((rows, LANES))
    return pl.pallas_call(
        attend_kernel,
        grid=(groups,),
        in_specs=[
            whole((rows, width)),
            pl.BlockSpec((width, GROUP), lambda g: (0, g)),
            pl.BlockSpec((width, LANES), lambda g: (0, g)),
            pl.BlockSpec((width, LANES), lambda g: (0, g)),
            table,
            table,
            table,
            whole((rows, 1)),
            whole((1, rows)),
        ],
        out_specs=[
            pl.BlockSpec((rows, GROUP), lambda g: (0, g)),
            pl.BlockSpec((rows, LANES), lambda g: (0, g)),
            pl.BlockSpec((rows, LANES), lambda g: (0, g)),
            pl.BlockSpec((rows, GROUP), lambda g: (0, g)),
            pl.BlockSpec((1, 8, rows), lambda g: (g, 0, 0)),
        ],
        out_shape=(
            jax.ShapeDtypeStruct((rows, groups * GROUP), bf16),
            jax.ShapeDtypeStruct((rows, groups * LANES), bf16),
            jax.ShapeDtypeStruct((rows, groups * LANES), bf16),
            jax.ShapeDtypeStruct((rows, groups * GROUP), bf16),
            jax.ShapeDtypeStruct((groups, 8, rows), f32),
        ),
        scratch_shapes=[pltpu.VMEM((rows, rows), f32)],
        compiler_params=params(),
        name="attend",
    )(first, wq, wk, wv, *tables, seg_col, seg_row)


def router_kernel(
    x_ref, att_a_ref, att_b_ref, wo_a_ref, wo_b_ref, gain_ref, wr_ref, routes_ref, slots_ref,
    resid_ref, second_ref, gates_ref, places_ref,
):
    resid = x_ref[...].astype(f32) + (nn(att_a_ref[...], wo_a_ref[...]) + nn(att_b_ref[...], wo_b_ref[...]))
    resid_ref[...] = resid
    scale = lax.rsqrt(jnp.mean(resid * resid, axis=-1, keepdims=True) + EPS)
    second = (resid * scale * gain_ref[...].astype(f32)).astype(bf16)
    second_ref[...] = second
    logits = nt(wr_ref[...], second)
    experts, rows = logits.shape
    routes, slots = routes_ref[...], slots_ref[...]
    number = lax.broadcasted_iota(jnp.int32, (experts, rows), 0)
    chosen = jnp.zeros((experts, rows), f32)
    place = jnp.zeros((8, rows), jnp.int32)
    taken = jnp.zeros((8, rows), jnp.int32)
    for k in range(routes.shape[0]):
        hit = number == routes[k : k + 1, :]
        chosen = jnp.where(hit, 1.0, chosen)
        hit = number[:8] == routes[k : k + 1, :]
        place = jnp.where(hit, slots[k : k + 1, :], place)
        taken = jnp.where(hit, 1, taken)
    places_ref[...] = jnp.where(taken > 0, place, CAP)
    top = jnp.max(jnp.where(chosen > 0, logits, NEG), axis=0, keepdims=True)
    weights = jnp.where(chosen > 0, jnp.exp(logits - top), 0.0)
    gates_ref[...] = weights / jnp.sum(weights, axis=0, keepdims=True)


def router(x, att_a, att_b, wo_a, wo_b, gain, wr_t, routes_t, slots_t):
    rows, width = x.shape
    return pl.pallas_call(
        router_kernel,
        out_shape=(
            jax.ShapeDtypeStruct((rows, width), f32),
            jax.ShapeDtypeStruct((rows, width), bf16),
            jax.ShapeDtypeStruct((wr_t.shape[0], rows), f32),
            jax.ShapeDtypeStruct((8, rows), jnp.int32),
        ),
        compiler_params=pltpu.CompilerParams(vmem_limit_bytes=56 * 1024 * 1024),
        name="router",
    )(x, att_a, att_b, wo_a, wo_b, gain, wr_t, routes_t, slots_t)


def split_three(values):
    first = values.astype(bf16)
    rest = values - first.astype(f32)
    second = rest.astype(bf16)
    return first, second, (rest - second.astype(f32)).astype(bf16)


def experts_kernel(
    second_ref, cot_ref, resid_ref, gates_ref, places_ref, gain_ref, wr_ref,
    wg_a_ref, wg_b_ref, wu_a_ref, wu_b_ref, wd_a_ref, wd_b_ref,
    out_ref, low_ref, grad_ref, small_ref,
    gg_a_ref, gg_b_ref, gu_a_ref, gu_b_ref, gd_a_ref, gd_b_ref,
    moe_ref, back_ref, slot_grads_ref,
):
    e = pl.program_id(0)
    rows = second_ref.shape[0]
    second = second_ref[...]
    slots = lax.broadcasted_iota(jnp.int32, (CAP, rows), 0)
    hit = slots == places_ref[pl.ds(e, 1), :]
    gate_slot = jnp.sum(jnp.where(hit, gates_ref[pl.ds(e, 1), :], 0.0), axis=1, keepdims=True)
    onehot = jnp.where(hit, 1.0, 0.0).astype(bf16)
    expert_in = nn(onehot, second).astype(bf16)
    slot_grad = nn(onehot, cot_ref[...])
    out_grad = (gate_slot * slot_grad).astype(bf16)
    expert_out = None
    back = None
    for wg_ref, wu_ref, wd_ref, gg_ref, gu_ref, gd_ref in (
        (wg_a_ref, wu_a_ref, wd_a_ref, gg_a_ref, gu_a_ref, gd_a_ref),
        (wg_b_ref, wu_b_ref, wd_b_ref, gg_b_ref, gu_b_ref, gd_b_ref),
    ):
        wg, wu, wd = wg_ref[0], wu_ref[0], wd_ref[0]
        gate_pre = nn(expert_in, wg)
        up_pre = nn(expert_in, wu)
        sig = 1.0 / (1.0 + jnp.exp(-gate_pre))
        silu = gate_pre * sig
        hidden = (silu * up_pre).astype(bf16)
        part = nn(hidden, wd)
        expert_out = part if expert_out is None else expert_out + part
        hidden_grad = nt(out_grad, wd)
        gd_ref[0] = tn(hidden, out_grad).astype(bf16)
        gate_low = (hidden_grad * up_pre * sig * (1.0 + gate_pre * (1.0 - sig))).astype(bf16)
        up_low = (hidden_grad * silu).astype(bf16)
        gg_ref[0] = tn(expert_in, gate_low).astype(bf16)
        gu_ref[0] = tn(expert_in, up_low).astype(bf16)
        part = nt(gate_low, wg) + nt(up_low, wu)
        back = part if back is None else back + part
    slot_gate = jnp.sum(expert_out * slot_grad, axis=1, keepdims=True)
    gate_row = jnp.sum(jnp.where(hit, slot_gate, 0.0), axis=0, keepdims=True)
    moe = tn(onehot, (gate_slot * expert_out).astype(bf16))
    second_back = tn(onehot, back.astype(bf16))

    @pl.when(e == 0)
    def _():
        moe_ref[...] = moe
        back_ref[...] = second_back
        slot_grads_ref[...] = jnp.zeros_like(slot_grads_ref)

    @pl.when(e > 0)
    def _():
        moe_ref[...] += moe
        back_ref[...] += second_back

    slot_grads_ref[pl.ds(e, 1), :] = gate_row

    @pl.when(e == pl.num_programs(0) - 1)
    def _():
        gates = gates_ref[...]
        resid = resid_ref[...]
        out_ref[...] = (resid + moe_ref[...]).astype(bf16)
        gate_grad = slot_grads_ref[...]
        logit_grad = gates * (gate_grad - jnp.sum(gates * gate_grad, axis=0, keepdims=True))
        router_grad = None
        second_grad = back_ref[...]
        for piece in split_three(logit_grad):
            part = nn(piece, second)
            router_grad = part if router_grad is None else router_grad + part
            second_grad = second_grad + tn(piece, wr_ref[...])
        experts = gates.shape[0]
        small_ref[0:experts, :] = router_grad
        gain = gain_ref[...].astype(f32)
        scale = lax.rsqrt(jnp.mean(resid * resid, axis=-1, keepdims=True) + EPS)
        norm_grad = jnp.sum(second_grad * resid * scale, axis=0, keepdims=True)
        small_ref[experts : experts + 8, :] = jnp.where(
            lax.broadcasted_iota(jnp.int32, (8, resid.shape[1]), 0) == 0, norm_grad, 0.0
        )
        inner = jnp.mean(gain * second_grad * resid, axis=-1, keepdims=True)
        grad = scale * gain * second_grad - resid * (scale * scale * scale) * inner
        grad = grad + cot_ref[...].astype(f32)
        grad_ref[...] = grad
        low_ref[...] = grad.astype(bf16)


def experts_layer(second, cot, resid, gates, places, gain, wr_t, weights):
    rows, width = second.shape
    experts = gates.shape[0]
    window, _, hidden = weights[0].shape
    wide = pl.BlockSpec((1, width, hidden), lambda e: (e, 0, 0))
    tall = pl.BlockSpec((1, hidden, width), lambda e: (e, 0, 0))
    wide_out = jax.ShapeDtypeStruct((window, width, hidden), bf16)
    tall_out = jax.ShapeDtypeStruct((window, hidden, width), bf16)
    return pl.pallas_call(
        experts_kernel,
        grid=(window,),
        in_specs=[
            whole((rows, width)),
            whole((rows, width)),
            whole((rows, width)),
            whole((experts, rows)),
            whole((8, rows)),
            whole((1, width)),
            whole((experts, width)),
            wide,
            wide,
            wide,
            wide,
            tall,
            tall,
        ],
        out_specs=[
            whole((rows, width)),
            whole((rows, width)),
            whole((rows, width)),
            whole((experts + 8, width)),
            wide,
            wide,
            wide,
            wide,
            tall,
            tall,
        ],
        out_shape=(
            jax.ShapeDtypeStruct((rows, width), bf16),
            jax.ShapeDtypeStruct((rows, width), bf16),
            jax.ShapeDtypeStruct((rows, width), f32),
            jax.ShapeDtypeStruct((experts + 8, width), f32),
            wide_out,
            wide_out,
            wide_out,
            wide_out,
            tall_out,
            tall_out,
        ),
        scratch_shapes=[
            pltpu.VMEM((rows, width), f32),
            pltpu.VMEM((rows, width), f32),
            pltpu.VMEM((experts, rows), f32),
        ],
        compiler_params=params(),
        name="experts",
    )(second, cot, resid, gates, places, gain, wr_t, *weights)


def attend_back_kernel(
    final,
    q_ref, k_ref, v_ref, att_ref, lse_ref, cos_ref, up_ref, down_ref, segc_ref, segr_ref,
    low_ref, wo_ref, first_t_ref, wq_ref, wk_ref, wv_ref, *rest,
):
    if final:
        (before_ref, x_ref, gain_ref, grad_ref, gq_ref, gk_ref, gv_ref, go_ref, token_ref, norm_ref,
         bias_ref, sum_ref, dq_ref, dk_ref, dv_ref) = rest
    else:
        gq_ref, gk_ref, gv_ref, go_ref, sum_ref, bias_ref, dq_ref, dk_ref, dv_ref = rest
    rows = q_ref.shape[0]
    g = pl.program_id(0)

    @pl.when(g == 0)
    def _():
        for start in range(0, rows, BLOCK):
            at_key = lax.broadcasted_iota(jnp.int32, (BLOCK, rows), 0) + start
            at_query = lax.broadcasted_iota(jnp.int32, (BLOCK, rows), 1)
            allowed = (at_key <= at_query) & (segc_ref[start : start + BLOCK, :] == segr_ref[...])
            bias_ref[start : start + BLOCK, :] = jnp.where(allowed, 0.0, NEG)
        if final:
            sum_ref[...] = before_ref[...]
        else:
            sum_ref[...] = jnp.zeros_like(sum_ref)

    low_grad = low_ref[...]
    go_ref[...] = tn(att_ref[...], low_grad).astype(bf16)
    upward = nt(low_grad, wo_ref[...]).astype(bf16)
    keys = doubled(k_ref[...].astype(f32))
    values = doubled(v_ref[...].astype(f32))
    low, high = halves_mask()
    dk_ref[...] = jnp.zeros_like(dk_ref)
    dv_ref[...] = jnp.zeros_like(dv_ref)
    lanes = lane_iota(BLOCK)
    for start in range(0, rows, BLOCK):
        width = start + BLOCK
        mine = slice(start, width)
        bias = bias_ref[:width, mine]
        bias = jnp.concatenate([bias, bias], axis=1)
        for kv in range(2):
            part = slice(kv * LANES, (kv + 1) * LANES)
            query = q_ref[mine, part]
            query = jnp.concatenate([query * low, query * high], axis=0)
            upper = upward[mine, part]
            upper = jnp.concatenate([upper * low, upper * high], axis=0)
            logs = jnp.concatenate(
                [lse_ref[0, 2 * kv : 2 * kv + 1, mine], lse_ref[0, 2 * kv + 1 : 2 * kv + 2, mine]], axis=1
            )
            key = keys[kv][:width]
            probs = jnp.exp(nt(key, query) + bias - logs)
            prob_grad = nt(values[kv][:width], upper)
            product = probs * prob_grad
            delta = jnp.sum(product, axis=0, keepdims=True)
            raw = (product - probs * delta).astype(bf16)
            dv_ref[kv, :width, :] += nn(probs.astype(bf16), upper)
            dk_ref[kv, :width, :] += nn(raw, query)
            back = tn(raw, key)
            dq_ref[mine, part] = jnp.where(lanes < HEAD_DIM, back[:BLOCK], back[BLOCK:])
    cosine, up, down = cos_ref[...], up_ref[...], down_ref[...]
    left = lane_iota(rows) < HEAD_DIM

    def both(ref):
        one, two = ref[0], ref[1]
        one = one + pltpu.roll(one, HEAD_DIM, 1)
        two = two + pltpu.roll(two, HEAD_DIM, 1)
        return jnp.where(left, one, two)

    first_t = first_t_ref[...]
    key_back = rotate_back(both(dk_ref), cosine, up, down).astype(bf16)
    value_back = both(dv_ref).astype(bf16)
    query_back = jnp.concatenate(
        [
            (rotate_back(dq_ref[:, :LANES], cosine, up, down) * HEAD_DIM**-0.5).astype(bf16),
            (rotate_back(dq_ref[:, LANES:], cosine, up, down) * HEAD_DIM**-0.5).astype(bf16),
        ],
        axis=1,
    )
    gq_ref[...] = nn(first_t, query_back).astype(bf16)
    gk_ref[...] = nn(first_t, key_back).astype(bf16)
    gv_ref[...] = nn(first_t, value_back).astype(bf16)
    sum_ref[...] += nt(query_back, wq_ref[...]) + nt(key_back, wk_ref[...]) + nt(value_back, wv_ref[...])

    if final:

        @pl.when(g == pl.num_programs(0) - 1)
        def _():
            values = x_ref[...].astype(f32)
            first_grad = sum_ref[...]
            gain = gain_ref[...].astype(f32)
            scale = lax.rsqrt(jnp.mean(values * values, axis=-1, keepdims=True) + EPS)
            norm_ref[...] = jnp.broadcast_to(
                jnp.sum(first_grad * values * scale, axis=0, keepdims=True), norm_ref.shape
            )
            inner = jnp.mean(gain * first_grad * values, axis=-1, keepdims=True)
            grad = scale * gain * first_grad - values * (scale * scale * scale) * inner
            token_ref[...] = (grad + grad_ref[...]).astype(bf16)


def attend_back(saved, tables, seg_col, seg_row, low_grad, wo, first_t, wq, wk, wv, final=None):
    query, key, value, att, logs = saved
    rows = query.shape[0]
    width = wq.shape[0]
    groups = query.shape[1] // GROUP
    table = whole((rows, LANES))
    wide = pl.BlockSpec((rows, GROUP), lambda g: (0, g))
    thin = pl.BlockSpec((rows, LANES), lambda g: (0, g))
    wide_w = pl.BlockSpec((width, GROUP), lambda g: (0, g))
    thin_w = pl.BlockSpec((width, LANES), lambda g: (0, g))
    tall_w = pl.BlockSpec((GROUP, width), lambda g: (g, 0))
    square = whole((rows, width))
    in_specs = [
        wide, thin, thin, wide, pl.BlockSpec((1, 8, rows), lambda g: (g, 0, 0)),
        table, table, table, whole((rows, 1)), whole((1, rows)),
        square, tall_w, whole((width, rows)), wide_w, thin_w, thin_w,
    ]
    out_specs = [wide_w, thin_w, thin_w, tall_w]
    out_shape = [
        jax.ShapeDtypeStruct((width, groups * GROUP), bf16),
        jax.ShapeDtypeStruct((width, groups * LANES), bf16),
        jax.ShapeDtypeStruct((width, groups * LANES), bf16),
        jax.ShapeDtypeStruct((groups * GROUP, width), bf16),
    ]
    scratch = [pltpu.VMEM((rows, rows), f32)]
    extra = ()
    if final is None:
        out_specs.append(square)
        out_shape.append(jax.ShapeDtypeStruct((rows, width), f32))
    else:
        extra = final
        in_specs += [square, square, whole((1, width)), square]
        out_specs += [square, whole((8, width))]
        out_shape += [
            jax.ShapeDtypeStruct((rows, width), bf16),
            jax.ShapeDtypeStruct((8, width), f32),
        ]
        scratch.append(pltpu.VMEM((rows, width), f32))
    scratch += [
        pltpu.VMEM((rows, GROUP), f32),
        pltpu.VMEM((2, rows, LANES), f32),
        pltpu.VMEM((2, rows, LANES), f32),
    ]
    return pl.pallas_call(
        partial(attend_back_kernel, final is not None),
        grid=(groups,),
        in_specs=in_specs,
        out_specs=out_specs,
        out_shape=tuple(out_shape),
        scratch_shapes=scratch,
        compiler_params=params(),
        name="attend_back_final" if final is not None else "attend_back",
    )(query, key, value, att, logs, *tables, seg_col, seg_row, low_grad, wo, first_t, wq, wk, wv, *extra)


def swap_tensor(values):
    return lax.ppermute(values, "tensor", [(0, 1), (1, 0)])


def swap_dp(values, bit):
    count = lax.axis_size("dp")
    return lax.ppermute(values, "dp", [(i, i ^ bit) for i in range(count)])


def after(values, earlier):
    return lax.optimization_barrier((values, earlier))[0]


def fetch_half(weights, core):
    pieces = [
        lax.dynamic_slice_in_dim(w, core * (w.shape[0] // 2), w.shape[0] // 2, 0) for w in weights
    ]
    got = [swap_tensor(p) for p in pieces]
    return got


def join_cores(got, core):
    other = [swap_dp(p, 1) for p in got]
    return [
        jnp.where(core == 0, jnp.concatenate([a, b], 0), jnp.concatenate([b, a], 0))
        for a, b in zip(got, other)
    ]


def per_device(
    tokens, cotangent, segments, routes, slot_index,
    w_query, w_key, w_value, w_output, norm_attn, norm_ffn, w_router, w_gate, w_up, w_down,
):
    length, width = tokens.shape
    side = lax.axis_index("tensor")
    core = lax.axis_index("dp") % 2
    rows = SEQ_LEN

    def own(values):
        return lax.dynamic_slice_in_dim(values, side * rows, rows, 0)

    got_one = fetch_half((w_query, w_key, w_value), core)
    r_query, r_key, r_value = join_cores(got_one, core)
    got_two = fetch_half(after((w_output,), got_one[0]), core)
    (r_output,) = join_cores(got_two, core)
    got_three = fetch_half(after((w_gate, w_up, w_down), got_two[0]), core)
    r_gate, r_up, r_down = join_cores(got_three, core)

    x = own(tokens)
    cot = own(cotangent)
    seg = own(segments)
    seg_row, seg_col = seg[None, :], seg[:, None]
    routes_t = own(routes).T
    slots_t = own(slot_index).T
    wr_t = w_router.T
    gain_one, gain_two = norm_attn[None, :], norm_ffn[None, :]
    half_dim = HEAD_DIM // 2
    frequency = THETA ** (-(2.0 * jnp.arange(half_dim, dtype=f32)) / HEAD_DIM)
    freq = jnp.broadcast_to(frequency[:, None], (half_dim, LANES))

    first, first_t, *tables = prologue(x, gain_one, seg_row, freq)
    saved_a = attend(first, w_query, w_key, w_value, tables, seg_col, seg_row)
    saved_b = attend(first, r_query, r_key, r_value, tables, seg_col, seg_row)
    resid, second, gates, places = router(
        x, saved_a[3], saved_b[3], w_output, r_output, gain_two, wr_t, routes_t, slots_t
    )
    (out, low_grad, resid_grad, small, gg_a, gg_b, gu_a, gu_b, gd_a, gd_b) = experts_layer(
        second, cot, resid, gates, places, gain_two, wr_t,
        (w_gate, r_gate, w_up, r_up, w_down, r_down),
    )

    def finish(mine, theirs):
        total = mine.astype(f32) + swap_tensor(theirs).astype(f32)
        return lax.psum(total.astype(bf16), "dp").astype(f32)

    grad_gate = finish(gg_a, gg_b)
    grad_up = finish(gu_a, gu_b)
    grad_down = finish(gd_a, gd_b)
    out_other = swap_tensor(out)

    gq_b, gk_b, gv_b, go_b, partial_sum = attend_back(
        saved_b, tables, seg_col, seg_row, low_grad, r_output, first_t, r_query, r_key, r_value
    )
    gq_a, gk_a, gv_a, go_a, token, norm_one = attend_back(
        saved_a, tables, seg_col, seg_row, low_grad, w_output, first_t, w_query, w_key, w_value,
        final=(partial_sum, x, gain_one, resid_grad),
    )
    token_other = swap_tensor(token)
    grad_query = finish(gq_a, gq_b)
    grad_key = finish(gk_a, gk_b)
    grad_value = finish(gv_a, gv_b)
    grad_output = finish(go_a, go_b)
    packed = lax.psum(jnp.concatenate([small, norm_one], 0), ("dp", "tensor"))
    experts = w_router.shape[1]
    grad_router = packed[:experts].T
    grad_norm_ffn = packed[experts]
    grad_norm_attn = packed[experts + 8]

    def both(mine, other):
        return jnp.where(side == 0, jnp.concatenate([mine, other], 0), jnp.concatenate([other, mine], 0))

    return (
        both(out, out_other),
        both(token, token_other).astype(f32),
        grad_query,
        grad_key,
        grad_value,
        grad_output,
        grad_norm_attn,
        grad_norm_ffn,
        grad_router,
        grad_gate,
        grad_up,
        grad_down,
    )


def solution(mesh):
    placed = (
        P("dp", None), P("dp", None), P("dp"), P("dp", None), P("dp", None),
        P(None, "tensor"), P(None, "tensor"), P(None, "tensor"), P("tensor", None),
        P(), P(), P(),
        P(None, None, "tensor"), P(None, None, "tensor"), P(None, "tensor", None),
    )
    return jax.shard_map(
        per_device,
        mesh=mesh,
        in_specs=placed,
        out_specs=(
            P("dp", None), P("dp", None),
            P(None, "tensor"), P(None, "tensor"), P(None, "tensor"), P("tensor", None),
            P(), P(), P(),
            P(None, None, "tensor"), P(None, None, "tensor"), P(None, "tensor", None),
        ),
        check_vma=False,
    )
```

```python
from functools import partial

import jax
import jax.numpy as jnp
from jax import lax
from jax.experimental import pallas as pl
from jax.experimental.pallas import tpu as pltpu
from jax.sharding import PartitionSpec as P

HEAD_DIM = 64
SEQ_LEN = 1024
CAP = 256
EPS = 1e-06
THETA = 10000.0
NEG = -1e30
BLOCK = 256
LANES = 128
GROUP = 4 * HEAD_DIM

f32 = jnp.float32
bf16 = jnp.bfloat16


def nn(left, right):
    return lax.dot_general(left, right, (((1,), (0,)), ((), ())), preferred_element_type=f32)


def nt(left, right):
    return lax.dot_general(left, right, (((1,), (1,)), ((), ())), preferred_element_type=f32)


def tn(left, right):
    return lax.dot_general(left, right, (((0,), (0,)), ((), ())), preferred_element_type=f32)


def params(count=1):
    return pltpu.CompilerParams(
        dimension_semantics=("arbitrary",) * count if count else None,
        vmem_limit_bytes=56 * 1024 * 1024,
    )


def cost(micros):
    return pl.CostEstimate(flops=int(micros * 1.1e9), bytes_accessed=1 << 20, transcendentals=0)


def whole(shape):
    return pl.BlockSpec(shape, lambda *_: (0,) * len(shape))


def lane_iota(rows, lanes=LANES):
    return lax.broadcasted_iota(jnp.int32, (rows, lanes), 1)


def prologue_kernel(x_ref, gain_ref, seg_ref, freq_ref, first_ref, first_t_ref, cos_ref, up_ref, down_ref):
    rows = x_ref.shape[0]
    values = x_ref[...].astype(f32)
    scale = lax.rsqrt(jnp.mean(values * values, axis=-1, keepdims=True) + EPS)
    normed = values * scale * gain_ref[...].astype(f32)
    first_ref[...] = normed.astype(bf16)
    first_t_ref[...] = normed.astype(bf16).T
    seg = seg_ref[...]
    zeros = jnp.sum((seg == 0).astype(f32), axis=1, keepdims=True)
    ones = jnp.sum((seg == 1).astype(f32), axis=1, keepdims=True)
    places = lax.broadcasted_iota(jnp.int32, (1, rows), 1).astype(f32)
    places = places - jnp.where(seg >= 1, zeros, 0.0) - jnp.where(seg >= 2, ones, 0.0)
    angles = freq_ref[:, 0:1] * places
    cosine = jnp.cos(angles)
    sine = jnp.sin(angles)
    cosine = jnp.concatenate([cosine] * 4, axis=0).T
    sine = jnp.concatenate([sine] * 4, axis=0).T
    lower = (lane_iota(rows) % HEAD_DIM) < HEAD_DIM // 2
    cos_ref[...] = cosine
    up_ref[...] = jnp.where(lower, -sine, 0.0)
    down_ref[...] = jnp.where(lower, 0.0, sine)


def prologue(x, gain, seg_row, freq):
    rows, width = x.shape
    table = jax.ShapeDtypeStruct((rows, LANES), f32)
    return pl.pallas_call(
        prologue_kernel,
        out_shape=(
            jax.ShapeDtypeStruct((rows, width), bf16),
            jax.ShapeDtypeStruct((width, rows), bf16),
            table,
            table,
            table,
        ),
        compiler_params=params(0),
        cost_estimate=cost(5),
        name="prologue",
    )(x, gain, seg_row, freq)


def rotate(values, cosine, up, down):
    return (
        values * cosine
        + pltpu.roll(values, LANES - 32, 1) * up
        + pltpu.roll(values, 32, 1) * down
    )


def rotate_back(values, cosine, up, down):
    return (
        values * cosine
        - pltpu.roll(values, LANES - 32, 1) * up
        - pltpu.roll(values, 32, 1) * down
    )


def doubled(values):
    turned = pltpu.roll(values, HEAD_DIM, 1)
    left = lane_iota(values.shape[0]) < HEAD_DIM
    return (
        jnp.where(left, values, turned).astype(bf16),
        jnp.where(left, turned, values).astype(bf16),
    )


def halves_mask():
    left = (lane_iota(1) < HEAD_DIM).astype(f32)
    return left.astype(bf16), (1.0 - left).astype(bf16)


def attend_kernel(
    first_ref, wq_ref, wk_ref, wv_ref, cos_ref, up_ref, down_ref, segc_ref, segr_ref,
    q_ref, k_ref, v_ref, att_ref, lse_ref, bias_ref,
):
    rows = first_ref.shape[0]

    @pl.when(pl.program_id(0) == 0)
    def _():
        for start in range(0, rows, BLOCK):
            at_row = lax.broadcasted_iota(jnp.int32, (BLOCK, rows), 0) + start
            at_col = lax.broadcasted_iota(jnp.int32, (BLOCK, rows), 1)
            allowed = (at_col <= at_row) & (segc_ref[start : start + BLOCK, :] == segr_ref[...])
            bias_ref[start : start + BLOCK, :] = jnp.where(allowed, 0.0, NEG)

    first = first_ref[...]
    cosine, up, down = cos_ref[...], up_ref[...], down_ref[...]
    for tile in range(2):
        part = slice(tile * LANES, (tile + 1) * LANES)
        raw = nn(first, wq_ref[:, part])
        q_ref[:, part] = (rotate(raw, cosine, up, down) * HEAD_DIM**-0.5).astype(bf16)
    key = rotate(nn(first, wk_ref[...]), cosine, up, down)
    value = nn(first, wv_ref[...])
    k_ref[...] = key.astype(bf16)
    v_ref[...] = value.astype(bf16)
    keys, values = doubled(key), doubled(value)
    low, high = halves_mask()
    for start in range(0, rows, BLOCK):
        width = start + BLOCK
        mine = slice(start, width)
        bias = bias_ref[mine, :width]
        bias = jnp.concatenate([bias, bias], axis=0)
        logs = jnp.zeros((BLOCK, LANES), f32)
        lanes = lane_iota(BLOCK)
        for kv in range(2):
            part = slice(kv * LANES, (kv + 1) * LANES)
            query = q_ref[mine, part]
            query = jnp.concatenate([query * low, query * high], axis=0)
            scores = nt(query, keys[kv][:width]) + bias
            row_max = jnp.max(scores, axis=-1, keepdims=True)
            weights = jnp.exp(scores - row_max)
            total = jnp.sum(weights, axis=-1, keepdims=True)
            probs = (weights * (1.0 / total)).astype(bf16)
            out = nn(probs, values[kv][:width])
            att_ref[mine, part] = jnp.where(lanes < HEAD_DIM, out[:BLOCK], out[BLOCK:]).astype(bf16)
            log_total = row_max + jnp.log(total)
            logs = jnp.where(lanes == 2 * kv, log_total[:BLOCK], logs)
            logs = jnp.where(lanes == 2 * kv + 1, log_total[BLOCK:], logs)
        lse_ref[0, :, mine] = logs.T[:8]


def attend(first, wq, wk, wv, tables, seg_col, seg_row):
    rows, width = first.shape
    groups = wq.shape[1] // GROUP
    table = whole((rows, LANES))
    return pl.pallas_call(
        attend_kernel,
        grid=(groups,),
        in_specs=[
            whole((rows, width)),
            pl.BlockSpec((width, GROUP), lambda g: (0, g)),
            pl.BlockSpec((width, LANES), lambda g: (0, g)),
            pl.BlockSpec((width, LANES), lambda g: (0, g)),
            table,
            table,
            table,
            whole((rows, 1)),
            whole((1, rows)),
        ],
        out_specs=[
            pl.BlockSpec((rows, GROUP), lambda g: (0, g)),
            pl.BlockSpec((rows, LANES), lambda g: (0, g)),
            pl.BlockSpec((rows, LANES), lambda g: (0, g)),
            pl.BlockSpec((rows, GROUP), lambda g: (0, g)),
            pl.BlockSpec((1, 8, rows), lambda g: (g, 0, 0)),
        ],
        out_shape=(
            jax.ShapeDtypeStruct((rows, groups * GROUP), bf16),
            jax.ShapeDtypeStruct((rows, groups * LANES), bf16),
            jax.ShapeDtypeStruct((rows, groups * LANES), bf16),
            jax.ShapeDtypeStruct((rows, groups * GROUP), bf16),
            jax.ShapeDtypeStruct((groups, 8, rows), f32),
        ),
        scratch_shapes=[pltpu.VMEM((rows, rows), f32)],
        compiler_params=params(),
        cost_estimate=cost(10 * groups),
        name="attend",
    )(first, wq, wk, wv, *tables, seg_col, seg_row)


def router_kernel(
    x_ref, att_a_ref, att_b_ref, att_c_ref, wo_a_ref, wo_b_ref, wo_c_ref, gain_ref, wr_ref, routes_ref, slots_ref,
    resid_ref, second_ref, gates_ref, places_ref,
):
    mixed = nn(att_a_ref[...], wo_a_ref[...])
    mixed = mixed + nn(att_b_ref[...], wo_b_ref[...])
    mixed = mixed + nn(att_c_ref[...], wo_c_ref[...])
    resid = x_ref[...].astype(f32) + mixed
    resid_ref[...] = resid
    scale = lax.rsqrt(jnp.mean(resid * resid, axis=-1, keepdims=True) + EPS)
    second = (resid * scale * gain_ref[...].astype(f32)).astype(bf16)
    second_ref[...] = second
    logits = nt(wr_ref[...], second)
    experts, rows = logits.shape
    routes, slots = routes_ref[...], slots_ref[...]
    number = lax.broadcasted_iota(jnp.int32, (experts, rows), 0)
    chosen = jnp.zeros((experts, rows), f32)
    place = jnp.zeros((8, rows), jnp.int32)
    taken = jnp.zeros((8, rows), jnp.int32)
    for k in range(routes.shape[0]):
        hit = number == routes[k : k + 1, :]
        chosen = jnp.where(hit, 1.0, chosen)
        hit = number[:8] == routes[k : k + 1, :]
        place = jnp.where(hit, slots[k : k + 1, :], place)
        taken = jnp.where(hit, 1, taken)
    places_ref[...] = jnp.where(taken > 0, place, CAP)
    top = jnp.max(jnp.where(chosen > 0, logits, NEG), axis=0, keepdims=True)
    weights = jnp.where(chosen > 0, jnp.exp(logits - top), 0.0)
    gates_ref[...] = weights / jnp.sum(weights, axis=0, keepdims=True)


def router(x, attended, outputs, gain, wr_t, routes_t, slots_t):
    rows, width = x.shape
    return pl.pallas_call(
        router_kernel,
        out_shape=(
            jax.ShapeDtypeStruct((rows, width), f32),
            jax.ShapeDtypeStruct((rows, width), bf16),
            jax.ShapeDtypeStruct((wr_t.shape[0], rows), f32),
            jax.ShapeDtypeStruct((8, rows), jnp.int32),
        ),
        compiler_params=params(0),
        cost_estimate=cost(8),
        name="router",
    )(x, *attended, *outputs, gain, wr_t, routes_t, slots_t)


def split_three(values):
    first = values.astype(bf16)
    rest = values - first.astype(f32)
    second = rest.astype(bf16)
    return first, second, (rest - second.astype(f32)).astype(bf16)


def experts_kernel(
    order_ref, second_ref, cot_ref, resid_ref, gates_ref, places_ref, gain_ref, wr_ref,
    wg_a_ref, wg_b_ref, wu_a_ref, wu_b_ref, wd_a_ref, wd_b_ref,
    out_ref, low_ref, grad_ref, small_ref,
    gg_a_ref, gg_b_ref, gu_a_ref, gu_b_ref, gd_a_ref, gd_b_ref,
    moe_ref, back_ref, slot_grads_ref,
):
    step = pl.program_id(0)
    e = step ^ order_ref[0]
    rows = second_ref.shape[0]
    second = second_ref[...]
    slots = lax.broadcasted_iota(jnp.int32, (CAP, rows), 0)
    hit = slots == places_ref[pl.ds(e, 1), :]
    gate_slot = jnp.sum(jnp.where(hit, gates_ref[pl.ds(e, 1), :], 0.0), axis=1, keepdims=True)
    onehot = jnp.where(hit, 1.0, 0.0).astype(bf16)
    expert_in = nn(onehot, second).astype(bf16)
    slot_grad = nn(onehot, cot_ref[...])
    out_grad = (gate_slot * slot_grad).astype(bf16)
    expert_out = None
    back = None
    for wg_ref, wu_ref, wd_ref, gg_ref, gu_ref, gd_ref in (
        (wg_a_ref, wu_a_ref, wd_a_ref, gg_a_ref, gu_a_ref, gd_a_ref),
        (wg_b_ref, wu_b_ref, wd_b_ref, gg_b_ref, gu_b_ref, gd_b_ref),
    ):
        wg, wu, wd = wg_ref[0], wu_ref[0], wd_ref[0]
        gate_pre = nn(expert_in, wg)
        up_pre = nn(expert_in, wu)
        sig = 1.0 / (1.0 + jnp.exp(-gate_pre))
        silu = gate_pre * sig
        hidden = (silu * up_pre).astype(bf16)
        part = nn(hidden, wd)
        expert_out = part if expert_out is None else expert_out + part
        hidden_grad = nt(out_grad, wd)
        gd_ref[0] = tn(hidden, out_grad).astype(bf16)
        gate_low = (hidden_grad * up_pre * sig * (1.0 + gate_pre * (1.0 - sig))).astype(bf16)
        up_low = (hidden_grad * silu).astype(bf16)
        gg_ref[0] = tn(expert_in, gate_low).astype(bf16)
        gu_ref[0] = tn(expert_in, up_low).astype(bf16)
        part = nt(gate_low, wg) + nt(up_low, wu)
        back = part if back is None else back + part
    slot_gate = jnp.sum(expert_out * slot_grad, axis=1, keepdims=True)
    gate_row = jnp.sum(jnp.where(hit, slot_gate, 0.0), axis=0, keepdims=True)
    moe = tn(onehot, (gate_slot * expert_out).astype(bf16))
    second_back = tn(onehot, back.astype(bf16))

    @pl.when(step == 0)
    def _():
        moe_ref[...] = moe
        back_ref[...] = second_back
        slot_grads_ref[...] = jnp.zeros_like(slot_grads_ref)

    @pl.when(step > 0)
    def _():
        moe_ref[...] += moe
        back_ref[...] += second_back

    slot_grads_ref[pl.ds(e, 1), :] = gate_row

    @pl.when(step == pl.num_programs(0) - 1)
    def _():
        gates = gates_ref[...]
        resid = resid_ref[...]
        out_ref[...] = (resid + moe_ref[...]).astype(bf16)
        gate_grad = slot_grads_ref[...]
        logit_grad = gates * (gate_grad - jnp.sum(gates * gate_grad, axis=0, keepdims=True))
        router_grad = None
        second_grad = back_ref[...]
        for piece in split_three(logit_grad):
            part = nn(piece, second)
            router_grad = part if router_grad is None else router_grad + part
            second_grad = second_grad + tn(piece, wr_ref[...])
        experts = gates.shape[0]
        small_ref[0:experts, :] = router_grad
        gain = gain_ref[...].astype(f32)
        scale = lax.rsqrt(jnp.mean(resid * resid, axis=-1, keepdims=True) + EPS)
        norm_grad = jnp.sum(second_grad * resid * scale, axis=0, keepdims=True)
        small_ref[experts : experts + 8, :] = jnp.where(
            lax.broadcasted_iota(jnp.int32, (8, resid.shape[1]), 0) == 0, norm_grad, 0.0
        )
        inner = jnp.mean(gain * second_grad * resid, axis=-1, keepdims=True)
        grad = scale * gain * second_grad - resid * (scale * scale * scale) * inner
        grad = grad + cot_ref[...].astype(f32)
        grad_ref[...] = grad
        low_ref[...] = grad.astype(bf16)


def experts_layer(order, second, cot, resid, gates, places, gain, wr_t, weights):
    rows, width = second.shape
    experts = gates.shape[0]
    window, _, hidden = weights[0].shape
    wide = pl.BlockSpec((1, width, hidden), lambda i, o: (i ^ o[0], 0, 0))
    tall = pl.BlockSpec((1, hidden, width), lambda i, o: (i ^ o[0], 0, 0))
    wide_rel = pl.BlockSpec((1, width, hidden), lambda i, o: (i, 0, 0))
    tall_rel = pl.BlockSpec((1, hidden, width), lambda i, o: (i, 0, 0))
    wide_out = jax.ShapeDtypeStruct((window, width, hidden), bf16)
    tall_out = jax.ShapeDtypeStruct((window, hidden, width), bf16)
    return pl.pallas_call(
        experts_kernel,
        grid_spec=pltpu.PrefetchScalarGridSpec(
        num_scalar_prefetch=1,
        grid=(window,),
        in_specs=[
            whole((rows, width)),
            whole((rows, width)),
            whole((rows, width)),
            whole((experts, rows)),
            whole((8, rows)),
            whole((1, width)),
            whole((experts, width)),
            wide,
            wide_rel,
            wide,
            wide_rel,
            tall,
            tall_rel,
        ],
        out_specs=[
            whole((rows, width)),
            whole((rows, width)),
            whole((rows, width)),
            whole((experts + 8, width)),
            wide,
            wide,
            wide,
            wide,
            tall,
            tall,
        ],
        scratch_shapes=[
            pltpu.VMEM((rows, width), f32),
            pltpu.VMEM((rows, width), f32),
            pltpu.VMEM((experts, rows), f32),
        ],
        ),
        out_shape=(
            jax.ShapeDtypeStruct((rows, width), bf16),
            jax.ShapeDtypeStruct((rows, width), bf16),
            jax.ShapeDtypeStruct((rows, width), f32),
            jax.ShapeDtypeStruct((experts + 8, width), f32),
            wide_out,
            wide_out,
            wide_out,
            wide_out,
            tall_out,
            tall_out,
        ),
        compiler_params=params(),
        cost_estimate=cost(39),
        name="experts",
    )(order, second, cot, resid, gates, places, gain, wr_t, *weights)


def attend_back_kernel(
    sel_ref, q_ref, k_ref, v_ref, lse_ref, cos_ref, up_ref, down_ref, segc_ref, segr_ref, low_ref, wo_ref,
    back_ref, bias_ref, dq_ref, dk_ref, dv_ref,
):
    rows = q_ref.shape[0]
    for start in range(0, rows, BLOCK):
        at_key = lax.broadcasted_iota(jnp.int32, (BLOCK, rows), 0) + start
        at_query = lax.broadcasted_iota(jnp.int32, (BLOCK, rows), 1)
        allowed = (at_key <= at_query) & (segc_ref[start : start + BLOCK, :] == segr_ref[...])
        bias_ref[start : start + BLOCK, :] = jnp.where(allowed, 0.0, NEG)
    upward = nt(low_ref[...], wo_ref[...]).astype(bf16)
    keys = doubled(k_ref[...].astype(f32))
    values = doubled(v_ref[...].astype(f32))
    low, high = halves_mask()
    dk_ref[...] = jnp.zeros_like(dk_ref)
    dv_ref[...] = jnp.zeros_like(dv_ref)
    lanes = lane_iota(BLOCK)
    for start in range(0, rows, BLOCK):
        width = start + BLOCK
        mine = slice(start, width)
        bias = bias_ref[:width, mine]
        bias = jnp.concatenate([bias, bias], axis=1)
        for kv in range(2):
            part = slice(kv * LANES, (kv + 1) * LANES)
            query = q_ref[mine, part]
            query = jnp.concatenate([query * low, query * high], axis=0)
            upper = upward[mine, part]
            upper = jnp.concatenate([upper * low, upper * high], axis=0)
            logs = jnp.concatenate(
                [lse_ref[0, 2 * kv : 2 * kv + 1, mine], lse_ref[0, 2 * kv + 1 : 2 * kv + 2, mine]], axis=1
            )
            key = keys[kv][:width]
            probs = jnp.exp(nt(key, query) + bias - logs)
            prob_grad = nt(values[kv][:width], upper)
            product = probs * prob_grad
            delta = jnp.sum(product, axis=0, keepdims=True)
            raw = (product - probs * delta).astype(bf16)
            dv_ref[kv, :width, :] += nn(probs.astype(bf16), upper)
            dk_ref[kv, :width, :] += nn(raw, query)
            back = tn(raw, key)
            dq_ref[mine, part] = jnp.where(lanes < HEAD_DIM, back[:BLOCK], back[BLOCK:])
    cosine, up, down = cos_ref[...], up_ref[...], down_ref[...]
    left = lane_iota(rows) < HEAD_DIM

    def both(ref):
        one, two = ref[0], ref[1]
        one = one + pltpu.roll(one, HEAD_DIM, 1)
        two = two + pltpu.roll(two, HEAD_DIM, 1)
        return jnp.where(left, one, two)

    back_ref[:, 2 * LANES : 3 * LANES] = rotate_back(both(dk_ref), cosine, up, down).astype(bf16)
    back_ref[:, 3 * LANES :] = both(dv_ref).astype(bf16)
    for kv in range(2):
        part = slice(kv * LANES, (kv + 1) * LANES)
        turned = rotate_back(dq_ref[:, part], cosine, up, down)
        back_ref[:, part] = (turned * HEAD_DIM**-0.5).astype(bf16)


def attend_back(sel, saved, tables, seg_col, seg_row, low_grad, wo):
    query, key, value, _, logs = saved
    rows, width = low_grad.shape

    def fixed(shape):
        return pl.BlockSpec(shape, lambda i, s: (0,) * len(shape))

    table = fixed((rows, LANES))
    wide = pl.BlockSpec((rows, GROUP), lambda i, s: (0, s[0]))
    thin = pl.BlockSpec((rows, LANES), lambda i, s: (0, s[0]))
    return pl.pallas_call(
        attend_back_kernel,
        grid_spec=pltpu.PrefetchScalarGridSpec(
            num_scalar_prefetch=1,
            grid=(1,),
            in_specs=[
                wide, thin, thin, pl.BlockSpec((1, 8, rows), lambda i, s: (s[0], 0, 0)),
                table, table, table, fixed((rows, 1)), fixed((1, rows)),
                fixed((rows, width)), pl.BlockSpec((GROUP, width), lambda i, s: (s[0], 0)),
            ],
            out_specs=fixed((rows, 2 * GROUP)),
            scratch_shapes=[
                pltpu.VMEM((rows, rows), f32),
                pltpu.VMEM((rows, GROUP), f32),
                pltpu.VMEM((2, rows, LANES), f32),
                pltpu.VMEM((2, rows, LANES), f32),
            ],
        ),
        out_shape=jax.ShapeDtypeStruct((rows, 2 * GROUP), bf16),
        compiler_params=params(),
        cost_estimate=cost(14),
        name="attend_back",
    )(sel, query, key, value, logs, *tables, seg_col, seg_row, low_grad, wo)


def project_kernel(final, fresh, sel_ref, back_ref, att_ref, low_ref, first_t_ref, wq_ref, wk_ref, wv_ref, *rest):
    if not fresh:
        before_ref, *rest = rest
    if final:
        x_ref, gain_ref, grad_ref, group_ref, token_ref, norm_ref = rest
    else:
        group_ref, sum_ref = rest
    back = back_ref[...]
    group_ref[:, : 2 * GROUP] = nn(first_t_ref[...], back).astype(bf16)
    group_ref[:, 2 * GROUP :] = tn(low_ref[...], att_ref[...]).astype(bf16)
    first_grad = nt(back[:, :GROUP], wq_ref[...])
    first_grad = first_grad + nt(back[:, GROUP : GROUP + LANES], wk_ref[...])
    first_grad = first_grad + nt(back[:, GROUP + LANES :], wv_ref[...])
    if not fresh:
        first_grad = before_ref[...] + first_grad
    if final:
        inputs = x_ref[...].astype(f32)
        gain = gain_ref[...].astype(f32)
        scale = lax.rsqrt(jnp.mean(inputs * inputs, axis=-1, keepdims=True) + EPS)
        norm_ref[...] = jnp.broadcast_to(
            jnp.sum(first_grad * inputs * scale, axis=0, keepdims=True), norm_ref.shape
        )
        inner = jnp.mean(gain * first_grad * inputs, axis=-1, keepdims=True)
        grad = scale * gain * first_grad - inputs * (scale * scale * scale) * inner
        token_ref[...] = (grad + grad_ref[...]).astype(bf16)
    else:
        sum_ref[...] = first_grad


def project(sel, back, att, low_grad, first_t, wq, wk, wv, before=None, final=None):
    rows, width = low_grad.shape

    def fixed(shape):
        return pl.BlockSpec(shape, lambda i, s: (0,) * len(shape))

    wide_w = pl.BlockSpec((width, GROUP), lambda i, s: (0, s[0]))
    thin_w = pl.BlockSpec((width, LANES), lambda i, s: (0, s[0]))
    square = fixed((rows, width))
    in_specs = [
        fixed((rows, 2 * GROUP)), pl.BlockSpec((rows, GROUP), lambda i, s: (0, s[0])),
        square, fixed((width, rows)), wide_w, thin_w, thin_w,
    ]
    out_specs = [fixed((width, 3 * GROUP))]
    out_shape = [jax.ShapeDtypeStruct((width, 3 * GROUP), bf16)]
    extra = ()
    if before is not None:
        in_specs.append(square)
        extra = (before,)
    if final is None:
        out_specs.append(square)
        out_shape.append(jax.ShapeDtypeStruct((rows, width), f32))
    else:
        extra = (*extra, *final)
        in_specs += [square, fixed((1, width)), square]
        out_specs += [square, fixed((8, width))]
        out_shape += [
            jax.ShapeDtypeStruct((rows, width), bf16),
            jax.ShapeDtypeStruct((8, width), f32),
        ]
    return pl.pallas_call(
        partial(project_kernel, final is not None, before is None),
        grid_spec=pltpu.PrefetchScalarGridSpec(
            num_scalar_prefetch=1, grid=(1,), in_specs=in_specs, out_specs=out_specs
        ),
        out_shape=tuple(out_shape),
        compiler_params=params(),
        cost_estimate=cost(7),
        name="project_final" if final is not None else "project",
    )(sel, back, att, low_grad, first_t, wq, wk, wv, *extra)


def plain_order(piece, place, count):
    shape = piece.shape
    bit = 1
    while bit < count:
        pairs = piece.reshape(-1, 2, bit * shape[0] // count, shape[1])
        flipped = jnp.concatenate([pairs[:, 1:], pairs[:, :1]], axis=1)
        piece = jnp.where((place // bit) % 2 == 1, flipped, pairs)
        bit *= 2
    return piece.reshape(shape)


def reorder(piece, place, count):
    rows, columns = piece.shape
    block = rows // count
    if block % 16:
        return plain_order(piece, place, count).astype(f32)

    def kernel(place_ref, in_ref, out_ref):
        for i in range(count):
            start = pl.multiple_of((i ^ place_ref[0]) * block, block)
            out_ref[i * block : (i + 1) * block, :] = in_ref[pl.ds(start, block), :].astype(f32)

    return pl.pallas_call(
        kernel,
        grid_spec=pltpu.PrefetchScalarGridSpec(
            num_scalar_prefetch=1,
            grid=(1,),
            in_specs=[pl.BlockSpec((rows, columns), lambda i, s: (0, 0))],
            out_specs=pl.BlockSpec((rows, columns), lambda i, s: (0, 0)),
        ),
        out_shape=jax.ShapeDtypeStruct((rows, columns), f32),
        compiler_params=params(),
        cost_estimate=cost(3),
        name="reorder",
    )(place[None], piece)


def unpack(mine, other, place, core, count):
    rows, columns = mine.shape
    block = rows // count
    shapes = (
        jax.ShapeDtypeStruct((rows, 2 * GROUP), f32),
        jax.ShapeDtypeStruct((rows, 2 * LANES), f32),
        jax.ShapeDtypeStruct((rows, 2 * LANES), f32),
        jax.ShapeDtypeStruct((2 * GROUP, rows), f32),
    )
    if block % 16:
        one, two = (plain_order(p, place, count) for p in (mine, other))
        zero, one = jnp.where(core == 0, one, two), jnp.where(core == 0, two, one)
        parts = ((0, GROUP), (GROUP, GROUP + LANES), (GROUP + LANES, 2 * GROUP), (2 * GROUP, 3 * GROUP))
        out = [jnp.concatenate([zero[:, a:b], one[:, a:b]], 1).astype(f32) for a, b in parts]
        return (*out[:3], out[3].T)

    def kernel(place_ref, mine_ref, other_ref, query_ref, key_ref, value_ref, output_ref):
        for group in range(2):
            for i in range(count):
                start = pl.multiple_of((i ^ place_ref[0]) * block, block)
                here = slice(i * block, (i + 1) * block)
                one = mine_ref[pl.ds(start, block), :].astype(f32)
                two = other_ref[pl.ds(start, block), :].astype(f32)
                rows_of = jnp.where(place_ref[1] == group, one, two)
                wide = slice(group * GROUP, (group + 1) * GROUP)
                thin = slice(group * LANES, (group + 1) * LANES)
                query_ref[here, wide] = rows_of[:, :GROUP]
                key_ref[here, thin] = rows_of[:, GROUP : GROUP + LANES]
                value_ref[here, thin] = rows_of[:, GROUP + LANES : 2 * GROUP]
                output_ref[wide, here] = rows_of[:, 2 * GROUP :].T

    return pl.pallas_call(
        kernel,
        grid_spec=pltpu.PrefetchScalarGridSpec(
            num_scalar_prefetch=1,
            grid=(1,),
            in_specs=[pl.BlockSpec((rows, columns), lambda i, s: (0, 0))] * 2,
            out_specs=[pl.BlockSpec(o.shape, lambda i, s: (0, 0)) for o in shapes],
        ),
        out_shape=shapes,
        compiler_params=params(),
        cost_estimate=cost(5),
        name="unpack",
    )(jnp.stack([place, core]), mine, other)


def swap_tensor(values):
    return lax.ppermute(values, "tensor", [(0, 1), (1, 0)])


def swap_dp(values, bit):
    count = lax.axis_size("dp")
    return lax.ppermute(values, "dp", [(i, i ^ bit) for i in range(count)])


def after(values, earlier):
    return lax.optimization_barrier((values, earlier))[0]


def bit_of(bit):
    return (lax.axis_index("dp") // bit) % 2


def cut(values, index, axis, count=2):
    size = values.shape[axis] // count
    return lax.dynamic_slice_in_dim(values, index * size, size, axis)


def total(terms, start=None, size=None):
    if start is not None:
        terms = [lax.dynamic_slice_in_dim(t, start, size, 0) for t in terms]
    if len(terms) == 1:
        return terms[0]
    out = terms[0].astype(f32)
    for term in terms[1:]:
        out = out + term.astype(f32)
    return out.astype(bf16)


def swap(values, bit):
    return swap_tensor(values) if bit == 0 else swap_dp(values, bit)


def scatter_sum(mine, theirs, order):
    for bit in order:
        if bit == 0:
            (got,) = yield [(total(theirs), 0)]
            mine, theirs = [*mine, got], None
            continue
        side = bit_of(bit)
        sides, requests = [], []
        for terms in (mine, theirs):
            if terms is None:
                continue
            half = terms[0].shape[0] // 2
            requests.append((total(terms, (1 - side) * half, half), bit))
            sides.append(total(terms, side * half, half))
        got = yield requests
        mine = [sides[0], got[0]]
        theirs = [sides[1], got[1]] if theirs is not None else None
    return total(mine)


def place_of(order):
    place = 0
    for bit in order:
        if bit:
            place = 2 * place + bit_of(bit)
    return place


def gather_back(piece, order):
    for bit in reversed(order):
        if bit:
            (got,) = yield [(piece, bit)]
            piece = jnp.concatenate([piece, got], 0)
    return piece


def sum_all(values):
    for bit in [0] + [1 << i for i in range(30) if (1 << i) < lax.axis_size("dp")]:
        (got,) = yield [(values, bit)]
        values = values + got
    return values


def full_sum(kept, sent, order):
    got = yield [(s, 1) for s in sent]
    piece = yield from scatter_sum([kept[0], got[0]], [kept[1], got[1]], order)
    piece = yield from gather_back(piece, order)
    (other,) = yield [(piece, 1)]
    return piece, other


class Chains:
    def __init__(self):
        self.live = {}
        self.done = {}

    def advance(self, names=None, fence=None):
        names = [n for n in (names or list(self.live)) if n in self.live]
        requests = {}
        waiting = {n: self.live[n][1] for n in names}
        if fence is not None:
            fence, waiting = lax.optimization_barrier((fence, waiting))
        for n in names:
            chain = self.live[n][0]
            try:
                requests[n] = chain.send(waiting[n])
            except StopIteration as stop:
                self.done[n] = stop.value
                del self.live[n]
        sends = {n: [v for v, _ in r] for n, r in requests.items()}
        if fence is not None:
            fence, sends = lax.optimization_barrier((fence, sends))
        for n, r in requests.items():
            self.live[n] = (self.live[n][0], [swap(v, bit) for v, (_, bit) in zip(sends[n], r)])
        return fence

    def add(self, name, chain):
        self.live[name] = (chain, None)

    def finish(self):
        self.advance([n for n in self.live if self.live[n][1] is None], fence=())
        while self.live:
            self.advance(fence=())


def per_device(
    tokens, cotangent, segments, routes, slot_index,
    w_query, w_key, w_value, w_output, norm_attn, norm_ffn, w_router, w_gate, w_up, w_down,
):
    length, width = tokens.shape
    side = lax.axis_index("tensor")
    dp_size = lax.axis_size("dp")
    core = lax.axis_index("dp") % 2
    rows = SEQ_LEN
    far = [8 << i for i in range(20) if (8 << i) < dp_size]

    def own(values):
        return lax.dynamic_slice_in_dim(values, side * rows, rows, 0)

    x = own(tokens)
    cot = own(cotangent)
    seg = own(segments)
    seg_row, seg_col = seg[None, :], seg[:, None]
    routes_t = own(routes).T
    slots_t = own(slot_index).T
    wr_t = w_router.T
    gain_one, gain_two = norm_attn[None, :], norm_ffn[None, :]
    half_dim = HEAD_DIM // 2
    frequency = THETA ** (-(2.0 * jnp.arange(half_dim, dtype=f32)) / HEAD_DIM)
    freq = jnp.broadcast_to(frequency[:, None], (half_dim, LANES))

    near_own = [cut(w, core, 1) for w in (w_query, w_key, w_value)]
    order_index = lax.axis_index("dp") % 4
    near = [swap_tensor(w) for w in near_own]
    near_out = swap_tensor(after(cut(w_output, core, 0), near[0]))
    last = near_out
    got = []
    for w in (w_gate, w_up, w_down):
        last = swap_tensor(after(lax.dynamic_slice_in_dim(w, order_index, 1, 0), last))
        got.append(last)

    first, first_t, *tables = prologue(x, gain_one, seg_row, freq)
    saved_a = attend(first, w_query, w_key, w_value, tables, seg_col, seg_row)
    near, first = lax.optimization_barrier((near, (first, saved_a)))
    first, saved_a = first
    far_qkv = [swap_dp(w, 1) for w in near]
    saved_b = attend(first, *near, tables, seg_col, seg_row)
    (near_out, got[0]), (first, saved_b) = lax.optimization_barrier(((near_out, got[0]), (first, saved_b)))
    far_out = swap_dp(near_out, 1)
    across = [swap_dp(got[0], 2)]
    beside = [swap_dp(got[0], 1)]
    saved_c = attend(first, *far_qkv, tables, seg_col, seg_row)
    (across[0], got[1]), saved_c = lax.optimization_barrier(((across[0], got[1]), saved_c))
    across.append(swap_dp(got[1], 2))
    beside.append(swap_dp(got[1], 1))
    corner = [swap_dp(across[0], 1)]
    resid, second, gates, places = router(
        x, (saved_a[3], saved_b[3], saved_c[3]), (w_output, near_out, far_out), gain_two, wr_t, routes_t, slots_t
    )
    (across[1], got[2]), second = lax.optimization_barrier(((across[1], got[2]), second))
    across.append(swap_dp(got[2], 2))
    beside.append(swap_dp(got[2], 1))
    corner.append(swap_dp(across[1], 1))
    corner.append(swap_dp(across[2], 1))
    r_gate, r_up, r_down = (jnp.concatenate(parts, axis=0) for parts in zip(got, beside, across, corner))
    (out, low_grad, resid_grad, small, gg_a, gg_b, gu_a, gu_b, gd_a, gd_b) = experts_layer(
        order_index[None], second, cot, resid, gates, places, gain_two, wr_t,
        (w_gate, r_gate, w_up, r_up, w_down, r_down),
    )

    chains = Chains()
    near_bits = ([2, 4], [4, 2])
    orders = [[*bits, 0, *far] for bits in near_bits]
    experts_orders = {"gate": orders[0], "up": orders[1], "down0": orders[0], "down1": orders[1]}

    def experts_chain(name, mine, theirs):
        flat = [g.reshape(-1, g.shape[-1]) for g in (mine, theirs)]
        kept = [cut(g, core, 0) for g in flat]
        sent = [cut(g, 1 - core, 0) for g in flat]
        chains.add(name, full_sum(kept, sent, experts_orders[name]))

    experts_chain("gate", gg_a, gg_b)
    experts_chain("up", gu_a, gu_b)
    experts_chain("down0", gd_a[:, : gd_a.shape[1] // 2], gd_b[:, : gd_a.shape[1] // 2])
    experts_chain("down1", gd_a[:, gd_a.shape[1] // 2 :], gd_b[:, gd_a.shape[1] // 2 :])
    chains.add("small", sum_all(small))
    grads_names = list(experts_orders)

    def one_swap(values, bit):
        (got,) = yield [(values, bit)]
        return got

    def piece_swaps(values, count):
        size = values.shape[0] // count
        received = []
        for i in range(count):
            (got,) = yield [(values[i * size : (i + 1) * size], 0)]
            received.append(got)
        return jnp.concatenate(received, 0)

    chains.add("out", piece_swaps(out, 4))
    zero = jnp.zeros((1,), jnp.int32)
    one_minus = 1 - core[None]
    shared = (tables, seg_col, seg_row)

    low_grad = chains.advance(fence=low_grad)
    back = attend_back(zero, saved_c, *shared, low_grad, far_out)
    back = chains.advance(grads_names + ["out", "small"], fence=back)
    group_d, partial_sum = project(zero, back, saved_c[3], low_grad, first_t, *far_qkv)
    chains.add("other", one_swap(group_d, 1))
    low_grad, partial_sum = chains.advance(["other", "out"], fence=(low_grad, partial_sum))
    back = attend_back(zero, saved_b, *shared, low_grad, near_out)
    back = chains.advance(["other", "out", "small"], fence=back)
    group_c, partial_sum = project(zero, back, saved_b[3], low_grad, first_t, *near, before=partial_sum)
    chains.add("theirs", piece_swaps(total([group_c, chains.done["other"]]), 2))
    low_grad, partial_sum = chains.advance(grads_names + ["theirs", "out"], fence=(low_grad, partial_sum))
    back = attend_back(one_minus, saved_a, *shared, low_grad, w_output)
    back = chains.advance(grads_names + ["small"], fence=back)
    group_b, partial_sum = project(
        one_minus, back, saved_a[3], low_grad, first_t, w_query, w_key, w_value, before=partial_sum
    )
    chains.add("mine", one_swap(group_b, 1))
    low_grad, partial_sum = chains.advance(["mine", "theirs"], fence=(low_grad, partial_sum))
    back = attend_back(core[None], saved_a, *shared, low_grad, w_output)
    back = chains.advance(grads_names + ["mine", "theirs", "small"], fence=back)
    group_a, token, norm_one = project(
        core[None], back, saved_a[3], low_grad, first_t, w_query, w_key, w_value,
        before=partial_sum, final=(x, gain_one, resid_grad),
    )
    chains.advance(["small"])
    terms = (group_a, chains.done["mine"], chains.done["theirs"])
    half = width // 2
    tails = [[*bits, *far] for bits in near_bits]

    def tail(index):
        piece = yield from scatter_sum([t[index * half : (index + 1) * half] for t in terms], None, tails[index])
        piece = yield from gather_back(piece, tails[index])
        (other,) = yield [(piece, 1)]
        return piece, other

    chains.add("token", piece_swaps(token, 4))
    chains.add("tail0", tail(0))
    chains.add("tail1", tail(1))
    chains.add("norm", sum_all(norm_one))
    chains.finish()
    done = chains.done

    halves = [
        unpack(*done[f"tail{i}"], place_of(tails[i]), core, dp_size // 2) for i in range(2)
    ]
    grad_query, grad_key, grad_value = (jnp.concatenate([a, b], 0) for a, b in zip(halves[0][:3], halves[1][:3]))
    grad_output = jnp.concatenate([halves[0][3], halves[1][3]], 1)

    def expert_grad(name):
        piece, other = done[name]
        place = place_of(experts_orders[name]) + core * (dp_size // 2)
        return reorder(jnp.concatenate([piece, other], 0), place, dp_size)

    grad_gate = expert_grad("gate").reshape(w_gate.shape)
    grad_up = expert_grad("up").reshape(w_up.shape)
    parts = [
        expert_grad(name).reshape(w_down.shape[0], w_down.shape[1] // 2, width) for name in ("down0", "down1")
    ]
    grad_down = jnp.concatenate(parts, 1)
    small = done["small"]
    experts = w_router.shape[1]

    def both(mine, other):
        return jnp.where(side == 0, jnp.concatenate([mine, other], 0), jnp.concatenate([other, mine], 0))

    return (
        both(out, done["out"]),
        both(token, done["token"]).astype(f32),
        grad_query,
        grad_key,
        grad_value,
        grad_output,
        done["norm"][0],
        small[experts],
        small[:experts].T,
        grad_gate,
        grad_up,
        grad_down,
    )


def solution(mesh):
    placed = (
        P("dp", None), P("dp", None), P("dp"), P("dp", None), P("dp", None),
        P(None, "tensor"), P(None, "tensor"), P(None, "tensor"), P("tensor", None),
        P(), P(), P(),
        P(None, None, "tensor"), P(None, None, "tensor"), P(None, "tensor", None),
    )
    return jax.shard_map(
        per_device,
        mesh=mesh,
        in_specs=placed,
        out_specs=(
            P("dp", None), P("dp", None),
            P(None, "tensor"), P(None, "tensor"), P(None, "tensor"), P("tensor", None),
            P(), P(), P(),
            P(None, None, "tensor"), P(None, None, "tensor"), P(None, "tensor", None),
        ),
        check_vma=False,
    )
```

```python
from functools import partial

import jax
import jax.numpy as jnp
from jax import lax
from jax.experimental import pallas as pl
from jax.experimental.pallas import tpu as pltpu
from jax.sharding import PartitionSpec as P

HEAD_DIM = 64
SEQ_LEN = 1024
CAP = 256
EPS = 1e-06
THETA = 10000.0
NEG = -1e30
BLOCK = 256
LANES = 128
GROUP = 4 * HEAD_DIM

f32 = jnp.float32
bf16 = jnp.bfloat16


def nn(left, right):
    return lax.dot_general(left, right, (((1,), (0,)), ((), ())), preferred_element_type=f32)


def nt(left, right):
    return lax.dot_general(left, right, (((1,), (1,)), ((), ())), preferred_element_type=f32)


def tn(left, right):
    return lax.dot_general(left, right, (((0,), (0,)), ((), ())), preferred_element_type=f32)


def params(count=1):
    return pltpu.CompilerParams(
        dimension_semantics=("arbitrary",) * count if count else None,
        vmem_limit_bytes=59 * 1024 * 1024,
    )


def cost(micros):
    return pl.CostEstimate(flops=int(micros * 1.1e9), bytes_accessed=1 << 20, transcendentals=0)


def whole(shape):
    return pl.BlockSpec(shape, lambda *_: (0,) * len(shape))


def once(shape):
    return pl.BlockSpec(shape, lambda *_: (0,) * len(shape), pipeline_mode=pl.Buffered(1))


def lane_iota(rows, lanes=LANES):
    return lax.broadcasted_iota(jnp.int32, (rows, lanes), 1)


def prologue_kernel(x_ref, gain_ref, seg_ref, freq_ref, first_ref, first_t_ref, cos_ref, up_ref, down_ref):
    rows = x_ref.shape[0]
    values = x_ref[...].astype(f32)
    scale = lax.rsqrt(jnp.mean(values * values, axis=-1, keepdims=True) + EPS)
    normed = values * scale * gain_ref[...].astype(f32)
    first_ref[...] = normed.astype(bf16)
    first_t_ref[...] = normed.astype(bf16).T
    seg = seg_ref[...]
    zeros = jnp.sum((seg == 0).astype(f32), axis=1, keepdims=True)
    ones = jnp.sum((seg == 1).astype(f32), axis=1, keepdims=True)
    places = lax.broadcasted_iota(jnp.int32, (1, rows), 1).astype(f32)
    places = places - jnp.where(seg >= 1, zeros, 0.0) - jnp.where(seg >= 2, ones, 0.0)
    angles = freq_ref[:, 0:1] * places
    cosine = jnp.cos(angles)
    sine = jnp.sin(angles)
    cosine = jnp.concatenate([cosine] * 4, axis=0).T
    sine = jnp.concatenate([sine] * 4, axis=0).T
    lower = (lane_iota(rows) % HEAD_DIM) < HEAD_DIM // 2
    cos_ref[...] = cosine
    up_ref[...] = jnp.where(lower, -sine, 0.0)
    down_ref[...] = jnp.where(lower, 0.0, sine)


def prologue(x, gain, seg_row, freq):
    rows, width = x.shape
    table = jax.ShapeDtypeStruct((rows, LANES), f32)
    return pl.pallas_call(
        prologue_kernel,
        out_shape=(
            jax.ShapeDtypeStruct((rows, width), bf16),
            jax.ShapeDtypeStruct((width, rows), bf16),
            table,
            table,
            table,
        ),
        compiler_params=params(0),
        cost_estimate=cost(5),
        name="prologue",
    )(x, gain, seg_row, freq)


def rotate(values, cosine, up, down):
    return (
        values * cosine
        + pltpu.roll(values, LANES - 32, 1) * up
        + pltpu.roll(values, 32, 1) * down
    )


def rotate_back(values, cosine, up, down):
    return (
        values * cosine
        - pltpu.roll(values, LANES - 32, 1) * up
        - pltpu.roll(values, 32, 1) * down
    )


def doubled(values):
    turned = pltpu.roll(values, HEAD_DIM, 1)
    left = lane_iota(values.shape[0]) < HEAD_DIM
    return (
        jnp.where(left, values, turned).astype(bf16),
        jnp.where(left, turned, values).astype(bf16),
    )


def halves_mask():
    left = (lane_iota(1) < HEAD_DIM).astype(f32)
    return left.astype(bf16), (1.0 - left).astype(bf16)


def attend_kernel(
    first_ref, wq_ref, wk_ref, wv_ref, cos_ref, up_ref, down_ref, segc_ref, segr_ref,
    q_ref, k_ref, v_ref, att_ref, lse_ref, bias_ref,
):
    rows = first_ref.shape[0]

    @pl.when(pl.program_id(0) == 0)
    def _():
        for start in range(0, rows, BLOCK):
            at_row = lax.broadcasted_iota(jnp.int32, (BLOCK, rows), 0) + start
            at_col = lax.broadcasted_iota(jnp.int32, (BLOCK, rows), 1)
            allowed = (at_col <= at_row) & (segc_ref[start : start + BLOCK, :] == segr_ref[...])
            bias_ref[start : start + BLOCK, :] = jnp.where(allowed, 0.0, NEG)

    first = first_ref[...]
    cosine, up, down = cos_ref[...], up_ref[...], down_ref[...]
    for tile in range(2):
        part = slice(tile * LANES, (tile + 1) * LANES)
        raw = nn(first, wq_ref[:, part])
        q_ref[:, part] = (rotate(raw, cosine, up, down) * HEAD_DIM**-0.5).astype(bf16)
    key = rotate(nn(first, wk_ref[...]), cosine, up, down)
    value = nn(first, wv_ref[...])
    k_ref[...] = key.astype(bf16)
    v_ref[...] = value.astype(bf16)
    keys, values = doubled(key), doubled(value)
    low, high = halves_mask()
    for start in range(0, rows, BLOCK):
        width = start + BLOCK
        mine = slice(start, width)
        bias = bias_ref[mine, :width]
        bias = jnp.concatenate([bias, bias], axis=0)
        logs = jnp.zeros((BLOCK, LANES), f32)
        lanes = lane_iota(BLOCK)
        for kv in range(2):
            part = slice(kv * LANES, (kv + 1) * LANES)
            query = q_ref[mine, part]
            query = jnp.concatenate([query * low, query * high], axis=0)
            scores = nt(query, keys[kv][:width]) + bias
            row_max = jnp.max(scores, axis=-1, keepdims=True)
            weights = jnp.exp(scores - row_max)
            total = jnp.sum(weights, axis=-1, keepdims=True)
            probs = (weights * (1.0 / total)).astype(bf16)
            out = nn(probs, values[kv][:width])
            att_ref[mine, part] = jnp.where(lanes < HEAD_DIM, out[:BLOCK], out[BLOCK:]).astype(bf16)
            log_total = row_max + jnp.log(total)
            logs = jnp.where(lanes == 2 * kv, log_total[:BLOCK], logs)
            logs = jnp.where(lanes == 2 * kv + 1, log_total[BLOCK:], logs)
        lse_ref[0, :, mine] = logs.T[:8]


def attend(first, wq, wk, wv, tables, seg_col, seg_row):
    rows, width = first.shape
    groups = wq.shape[1] // GROUP
    table = whole((rows, LANES))
    return pl.pallas_call(
        attend_kernel,
        grid=(groups,),
        in_specs=[
            whole((rows, width)),
            pl.BlockSpec((width, GROUP), lambda g: (0, g)),
            pl.BlockSpec((width, LANES), lambda g: (0, g)),
            pl.BlockSpec((width, LANES), lambda g: (0, g)),
            table,
            table,
            table,
            whole((rows, 1)),
            whole((1, rows)),
        ],
        out_specs=[
            pl.BlockSpec((rows, GROUP), lambda g: (0, g)),
            pl.BlockSpec((rows, LANES), lambda g: (0, g)),
            pl.BlockSpec((rows, LANES), lambda g: (0, g)),
            pl.BlockSpec((rows, GROUP), lambda g: (0, g)),
            pl.BlockSpec((1, 8, rows), lambda g: (g, 0, 0)),
        ],
        out_shape=(
            jax.ShapeDtypeStruct((rows, groups * GROUP), bf16),
            jax.ShapeDtypeStruct((rows, groups * LANES), bf16),
            jax.ShapeDtypeStruct((rows, groups * LANES), bf16),
            jax.ShapeDtypeStruct((rows, groups * GROUP), bf16),
            jax.ShapeDtypeStruct((groups, 8, rows), f32),
        ),
        scratch_shapes=[pltpu.VMEM((rows, rows), f32)],
        compiler_params=params(),
        cost_estimate=cost(10 * groups),
        name="attend",
    )(first, wq, wk, wv, *tables, seg_col, seg_row)


def router_kernel(
    x_ref, att_a_ref, att_b_ref, att_c_ref, wo_a_ref, wo_b_ref, wo_c_ref, gain_ref, wr_ref, routes_ref, slots_ref,
    resid_ref, second_ref, gates_ref, places_ref,
):
    mixed = nn(att_a_ref[...], wo_a_ref[...])
    mixed = mixed + nn(att_b_ref[...], wo_b_ref[...])
    mixed = mixed + nn(att_c_ref[...], wo_c_ref[...])
    resid = x_ref[...].astype(f32) + mixed
    resid_ref[...] = resid
    scale = lax.rsqrt(jnp.mean(resid * resid, axis=-1, keepdims=True) + EPS)
    second = (resid * scale * gain_ref[...].astype(f32)).astype(bf16)
    second_ref[...] = second
    logits = nt(wr_ref[...], second)
    experts, rows = logits.shape
    routes, slots = routes_ref[...], slots_ref[...]
    number = lax.broadcasted_iota(jnp.int32, (experts, rows), 0)
    chosen = jnp.zeros((experts, rows), f32)
    place = jnp.zeros((8, rows), jnp.int32)
    taken = jnp.zeros((8, rows), jnp.int32)
    for k in range(routes.shape[0]):
        hit = number == routes[k : k + 1, :]
        chosen = jnp.where(hit, 1.0, chosen)
        hit = number[:8] == routes[k : k + 1, :]
        place = jnp.where(hit, slots[k : k + 1, :], place)
        taken = jnp.where(hit, 1, taken)
    places_ref[...] = jnp.where(taken > 0, place, CAP)
    top = jnp.max(jnp.where(chosen > 0, logits, NEG), axis=0, keepdims=True)
    weights = jnp.where(chosen > 0, jnp.exp(logits - top), 0.0)
    gates_ref[...] = weights / jnp.sum(weights, axis=0, keepdims=True)


def router(x, attended, outputs, gain, wr_t, routes_t, slots_t):
    rows, width = x.shape
    return pl.pallas_call(
        router_kernel,
        out_shape=(
            jax.ShapeDtypeStruct((rows, width), f32),
            jax.ShapeDtypeStruct((rows, width), bf16),
            jax.ShapeDtypeStruct((wr_t.shape[0], rows), f32),
            jax.ShapeDtypeStruct((8, rows), jnp.int32),
        ),
        compiler_params=params(0),
        cost_estimate=cost(8),
        name="router",
    )(x, *attended, *outputs, gain, wr_t, routes_t, slots_t)


def split_three(values):
    first = values.astype(bf16)
    rest = values - first.astype(f32)
    second = rest.astype(bf16)
    return first, second, (rest - second.astype(f32)).astype(bf16)


def experts_kernel(
    order_ref, second_ref, cot_ref, resid_ref, gates_ref, places_ref, gain_ref, wr_ref,
    wg_a_ref, wg_b_ref, wu_a_ref, wu_b_ref, wd_a_ref, wd_b_ref,
    out_ref, low_ref, grad_ref, small_ref, kept_ref, sent_ref,
    moe_ref, slot_grads_ref,
):
    step = pl.program_id(0)
    e = step ^ order_ref[0]
    rows = second_ref.shape[0]
    second = second_ref[...]
    slots = lax.broadcasted_iota(jnp.int32, (CAP, rows), 0)
    hit = slots == places_ref[pl.ds(e, 1), :]
    gate_slot = jnp.sum(jnp.where(hit, gates_ref[pl.ds(e, 1), :], 0.0), axis=1, keepdims=True)
    onehot = jnp.where(hit, 1.0, 0.0).astype(bf16)
    expert_in = nn(onehot, second).astype(bf16)
    slot_grad = nn(onehot, cot_ref[...])
    out_grad = (gate_slot * slot_grad).astype(bf16)
    expert_out = None
    back = None
    factors = []
    for wg_ref, wu_ref, wd_ref in ((wg_a_ref, wu_a_ref, wd_a_ref), (wg_b_ref, wu_b_ref, wd_b_ref)):
        wg, wu, wd = wg_ref[0], wu_ref[0], wd_ref[0]
        gate_pre = nn(expert_in, wg)
        up_pre = nn(expert_in, wu)
        sig = 1.0 / (1.0 + jnp.exp(-gate_pre))
        silu = gate_pre * sig
        hidden = (silu * up_pre).astype(bf16)
        part = nn(hidden, wd)
        expert_out = part if expert_out is None else expert_out + part
        hidden_grad = nt(out_grad, wd)
        gate_low = (hidden_grad * up_pre * sig * (1.0 + gate_pre * (1.0 - sig))).astype(bf16)
        up_low = (hidden_grad * silu).astype(bf16)
        factors.append((gate_low, up_low, hidden))
        part = nt(gate_low, wg) + nt(up_low, wu)
        back = part if back is None else back + part

    def weight_grads(ref):
        size = hidden.shape[1]
        for half, (gate_low, up_low, mixed) in enumerate(factors):
            ref[0, half, :size, :] = tn(gate_low, expert_in).astype(bf16)
            ref[0, half, size : 2 * size, :] = tn(up_low, expert_in).astype(bf16)
            ref[0, half, 2 * size :, :] = tn(mixed, out_grad).astype(bf16)

    @pl.when(step % 2 == 0)
    def _():
        weight_grads(kept_ref)

    @pl.when(step % 2 == 1)
    def _():
        weight_grads(sent_ref)

    slot_gate = jnp.sum(expert_out * slot_grad, axis=1, keepdims=True)
    gate_row = jnp.sum(jnp.where(hit, slot_gate, 0.0), axis=0, keepdims=True)
    moe = tn(onehot, (gate_slot * expert_out).astype(bf16))
    second_back = tn(onehot, back.astype(bf16))

    @pl.when(step == 0)
    def _():
        moe_ref[...] = moe
        grad_ref[...] = second_back
        slot_grads_ref[...] = jnp.zeros_like(slot_grads_ref)

    @pl.when(step > 0)
    def _():
        moe_ref[...] += moe
        grad_ref[...] += second_back

    slot_grads_ref[pl.ds(e, 1), :] = gate_row

    @pl.when(step == pl.num_programs(0) - 1)
    def _():
        gates = gates_ref[...]
        resid = resid_ref[...]
        out_ref[...] = (resid + moe_ref[...]).astype(bf16)
        gate_grad = slot_grads_ref[...]
        logit_grad = gates * (gate_grad - jnp.sum(gates * gate_grad, axis=0, keepdims=True))
        router_grad = None
        second_grad = grad_ref[...]
        for piece in split_three(logit_grad):
            part = nn(piece, second)
            router_grad = part if router_grad is None else router_grad + part
            second_grad = second_grad + tn(piece, wr_ref[...])
        experts = gates.shape[0]
        small_ref[0:experts, :] = router_grad
        gain = gain_ref[...].astype(f32)
        scale = lax.rsqrt(jnp.mean(resid * resid, axis=-1, keepdims=True) + EPS)
        norm_grad = jnp.sum(second_grad * resid * scale, axis=0, keepdims=True)
        small_ref[experts : experts + 8, :] = jnp.where(
            lax.broadcasted_iota(jnp.int32, (8, resid.shape[1]), 0) == 0, norm_grad, 0.0
        )
        inner = jnp.mean(gain * second_grad * resid, axis=-1, keepdims=True)
        grad = scale * gain * second_grad - resid * (scale * scale * scale) * inner
        grad = grad + cot_ref[...].astype(f32)
        grad_ref[...] = grad
        low_ref[...] = grad.astype(bf16)


def experts_layer(order, second, cot, resid, gates, places, gain, wr_t, weights):
    rows, width = second.shape
    experts = gates.shape[0]
    window, _, hidden = weights[0].shape
    wide = pl.BlockSpec((1, width, hidden), lambda i, o: (i ^ o[0], 0, 0))
    tall = pl.BlockSpec((1, hidden, width), lambda i, o: (i ^ o[0], 0, 0))
    wide_rel = pl.BlockSpec((1, width, hidden), lambda i, o: (i, 0, 0))
    tall_rel = pl.BlockSpec((1, hidden, width), lambda i, o: (i, 0, 0))
    grads_out = jax.ShapeDtypeStruct((window // 2, 2, 3 * hidden, width), bf16)
    grads = pl.BlockSpec((1, 2, 3 * hidden, width), lambda i, o: ((i // 2) ^ (o[0] // 2), 0, 0, 0))
    return pl.pallas_call(
        experts_kernel,
        grid_spec=pltpu.PrefetchScalarGridSpec(
        num_scalar_prefetch=1,
        grid=(window,),
        in_specs=[
            once((rows, width)),
            once((rows, width)),
            once((rows, width)),
            whole((experts, rows)),
            whole((8, rows)),
            whole((1, width)),
            whole((experts, width)),
            wide,
            wide_rel,
            wide,
            wide_rel,
            tall,
            tall_rel,
        ],
        out_specs=[
            once((rows, width)),
            once((rows, width)),
            once((rows, width)),
            whole((experts + 8, width)),
            grads,
            grads,
        ],
        scratch_shapes=[
            pltpu.VMEM((rows, width), f32),
            pltpu.VMEM((experts, rows), f32),
        ],
        ),
        out_shape=(
            jax.ShapeDtypeStruct((rows, width), bf16),
            jax.ShapeDtypeStruct((rows, width), bf16),
            jax.ShapeDtypeStruct((rows, width), f32),
            jax.ShapeDtypeStruct((experts + 8, width), f32),
            grads_out,
            grads_out,
        ),
        compiler_params=params(),
        cost_estimate=cost(39),
        name="experts",
    )(order, second, cot, resid, gates, places, gain, wr_t, *weights)


def attend_back_kernel(
    sel_ref, q_ref, k_ref, v_ref, lse_ref, cos_ref, up_ref, down_ref, segc_ref, segr_ref, low_ref, wo_ref,
    back_ref, bias_ref, dq_ref, dk_ref, dv_ref,
):
    rows = q_ref.shape[0]
    for start in range(0, rows, BLOCK):
        at_key = lax.broadcasted_iota(jnp.int32, (BLOCK, rows), 0) + start
        at_query = lax.broadcasted_iota(jnp.int32, (BLOCK, rows), 1)
        allowed = (at_key <= at_query) & (segc_ref[start : start + BLOCK, :] == segr_ref[...])
        bias_ref[start : start + BLOCK, :] = jnp.where(allowed, 0.0, NEG)
    upward = nt(low_ref[...], wo_ref[...]).astype(bf16)
    keys = doubled(k_ref[...].astype(f32))
    values = doubled(v_ref[...].astype(f32))
    low, high = halves_mask()
    dk_ref[...] = jnp.zeros_like(dk_ref)
    dv_ref[...] = jnp.zeros_like(dv_ref)
    lanes = lane_iota(BLOCK)
    for start in range(0, rows, BLOCK):
        width = start + BLOCK
        mine = slice(start, width)
        bias = bias_ref[:width, mine]
        bias = jnp.concatenate([bias, bias], axis=1)
        for kv in range(2):
            part = slice(kv * LANES, (kv + 1) * LANES)
            query = q_ref[mine, part]
            query = jnp.concatenate([query * low, query * high], axis=0)
            upper = upward[mine, part]
            upper = jnp.concatenate([upper * low, upper * high], axis=0)
            logs = jnp.concatenate(
                [lse_ref[0, 2 * kv : 2 * kv + 1, mine], lse_ref[0, 2 * kv + 1 : 2 * kv + 2, mine]], axis=1
            )
            key = keys[kv][:width]
            probs = jnp.exp(nt(key, query) + bias - logs)
            prob_grad = nt(values[kv][:width], upper)
            product = probs * prob_grad
            delta = jnp.sum(product, axis=0, keepdims=True)
            raw = (product - probs * delta).astype(bf16)
            dv_ref[kv, :width, :] += nn(probs.astype(bf16), upper)
            dk_ref[kv, :width, :] += nn(raw, query)
            back = tn(raw, key)
            dq_ref[mine, part] = jnp.where(lanes < HEAD_DIM, back[:BLOCK], back[BLOCK:])
    cosine, up, down = cos_ref[...], up_ref[...], down_ref[...]
    left = lane_iota(rows) < HEAD_DIM

    def both(ref):
        one, two = ref[0], ref[1]
        one = one + pltpu.roll(one, HEAD_DIM, 1)
        two = two + pltpu.roll(two, HEAD_DIM, 1)
        return jnp.where(left, one, two)

    back_ref[:, 2 * LANES : 3 * LANES] = rotate_back(both(dk_ref), cosine, up, down).astype(bf16)
    back_ref[:, 3 * LANES :] = both(dv_ref).astype(bf16)
    for kv in range(2):
        part = slice(kv * LANES, (kv + 1) * LANES)
        turned = rotate_back(dq_ref[:, part], cosine, up, down)
        back_ref[:, part] = (turned * HEAD_DIM**-0.5).astype(bf16)


def attend_back(sel, saved, tables, seg_col, seg_row, low_grad, wo):
    query, key, value, _, logs = saved
    rows, width = low_grad.shape

    def fixed(shape):
        return pl.BlockSpec(shape, lambda i, s: (0,) * len(shape))

    table = fixed((rows, LANES))
    wide = pl.BlockSpec((rows, GROUP), lambda i, s: (0, s[0]))
    thin = pl.BlockSpec((rows, LANES), lambda i, s: (0, s[0]))
    return pl.pallas_call(
        attend_back_kernel,
        grid_spec=pltpu.PrefetchScalarGridSpec(
            num_scalar_prefetch=1,
            grid=(1,),
            in_specs=[
                wide, thin, thin, pl.BlockSpec((1, 8, rows), lambda i, s: (s[0], 0, 0)),
                table, table, table, fixed((rows, 1)), fixed((1, rows)),
                fixed((rows, width)), pl.BlockSpec((GROUP, width), lambda i, s: (s[0], 0)),
            ],
            out_specs=fixed((rows, 2 * GROUP)),
            scratch_shapes=[
                pltpu.VMEM((rows, rows), f32),
                pltpu.VMEM((rows, GROUP), f32),
                pltpu.VMEM((2, rows, LANES), f32),
                pltpu.VMEM((2, rows, LANES), f32),
            ],
        ),
        out_shape=jax.ShapeDtypeStruct((rows, 2 * GROUP), bf16),
        compiler_params=params(),
        cost_estimate=cost(14),
        name="attend_back",
    )(sel, query, key, value, logs, *tables, seg_col, seg_row, low_grad, wo)


def project_kernel(final, fresh, sel_ref, back_ref, att_ref, low_ref, first_t_ref, wq_ref, wk_ref, wv_ref, *rest):
    if not fresh:
        before_ref, *rest = rest
    if final:
        x_ref, gain_ref, grad_ref, group_ref, token_ref, norm_ref = rest
    else:
        group_ref, sum_ref = rest
    back = back_ref[...]
    group_ref[:, : 2 * GROUP] = nn(first_t_ref[...], back).astype(bf16)
    group_ref[:, 2 * GROUP :] = tn(low_ref[...], att_ref[...]).astype(bf16)
    first_grad = nt(back[:, :GROUP], wq_ref[...])
    first_grad = first_grad + nt(back[:, GROUP : GROUP + LANES], wk_ref[...])
    first_grad = first_grad + nt(back[:, GROUP + LANES :], wv_ref[...])
    if not fresh:
        first_grad = before_ref[...] + first_grad
    if final:
        inputs = x_ref[...].astype(f32)
        gain = gain_ref[...].astype(f32)
        scale = lax.rsqrt(jnp.mean(inputs * inputs, axis=-1, keepdims=True) + EPS)
        norm_ref[...] = jnp.broadcast_to(
            jnp.sum(first_grad * inputs * scale, axis=0, keepdims=True), norm_ref.shape
        )
        inner = jnp.mean(gain * first_grad * inputs, axis=-1, keepdims=True)
        grad = scale * gain * first_grad - inputs * (scale * scale * scale) * inner
        token_ref[...] = (grad + grad_ref[...]).astype(bf16)
    else:
        sum_ref[...] = first_grad


def project(sel, back, att, low_grad, first_t, wq, wk, wv, before=None, final=None):
    rows, width = low_grad.shape

    def fixed(shape):
        return pl.BlockSpec(shape, lambda i, s: (0,) * len(shape))

    wide_w = pl.BlockSpec((width, GROUP), lambda i, s: (0, s[0]))
    thin_w = pl.BlockSpec((width, LANES), lambda i, s: (0, s[0]))
    square = fixed((rows, width))
    in_specs = [
        fixed((rows, 2 * GROUP)), pl.BlockSpec((rows, GROUP), lambda i, s: (0, s[0])),
        square, fixed((width, rows)), wide_w, thin_w, thin_w,
    ]
    out_specs = [fixed((width, 3 * GROUP))]
    out_shape = [jax.ShapeDtypeStruct((width, 3 * GROUP), bf16)]
    extra = ()
    if before is not None:
        in_specs.append(square)
        extra = (before,)
    if final is None:
        out_specs.append(square)
        out_shape.append(jax.ShapeDtypeStruct((rows, width), f32))
    else:
        extra = (*extra, *final)
        in_specs += [square, fixed((1, width)), square]
        out_specs += [square, fixed((8, width))]
        out_shape += [
            jax.ShapeDtypeStruct((rows, width), bf16),
            jax.ShapeDtypeStruct((8, width), f32),
        ]
    return pl.pallas_call(
        partial(project_kernel, final is not None, before is None),
        grid_spec=pltpu.PrefetchScalarGridSpec(
            num_scalar_prefetch=1, grid=(1,), in_specs=in_specs, out_specs=out_specs
        ),
        out_shape=tuple(out_shape),
        compiler_params=params(),
        cost_estimate=cost(7),
        name="project_final" if final is not None else "project",
    )(sel, back, att, low_grad, first_t, wq, wk, wv, *extra)


def plain_order(piece, place, count):
    shape = piece.shape
    bit = 1
    while bit < count:
        pairs = piece.reshape(-1, 2, bit * shape[0] // count, shape[1])
        flipped = jnp.concatenate([pairs[:, 1:], pairs[:, :1]], axis=1)
        piece = jnp.where((place // bit) % 2 == 1, flipped, pairs)
        bit *= 2
    return piece.reshape(shape)


def add_split(colors, sides):
    rows = [terms[0][0].shape[1] for terms in colors]
    half = rows[0] // 2
    if half % 16:
        out = []
        for terms, side in zip(colors, sides):
            cutouts = [lax.slice_in_dim(t, i * n, (i + 1) * n, axis=0) for t, n, i in terms]
            both = []
            for at in (side, 1 - side):
                pieces = [lax.dynamic_slice_in_dim(t, at * half, half, 1).astype(f32) for t in cutouts]
                both.append(sum(pieces[1:], pieces[0]).astype(bf16))
            out.append(tuple(both))
        return out
    steps = 4 if half % 64 == 0 else (2 if half % 32 == 0 else 1)
    block = half // steps
    in_specs, operands, out_specs, shapes, counts = [], [], [], [], []
    for number, terms in enumerate(colors):
        counts.append(len(terms))
        for other in (0, 1):
            for array, lead, index in terms:

                def place(j, s, number=number, index=index, other=other):
                    return (index, (s[number] ^ other) * steps + j, 0)

                in_specs.append(pl.BlockSpec((lead, block, array.shape[2]), place))
                operands.append(array)
        array, lead, _ = terms[0]
        for _ in range(2):
            out_specs.append(pl.BlockSpec((lead, block, array.shape[2]), lambda j, s: (0, j, 0)))
            shapes.append(jax.ShapeDtypeStruct((lead, half, array.shape[2]), bf16))

    def kernel(side_ref, *refs):
        ins, outs = refs[: len(operands)], refs[len(operands) :]
        at = 0
        for number, count in enumerate(counts):
            for other in range(2):
                value = ins[at][...].astype(f32)
                for term in range(1, count):
                    value = value + ins[at + term][...].astype(f32)
                outs[2 * number + other][...] = value.astype(bf16)
                at += count

    out = pl.pallas_call(
        kernel,
        grid_spec=pltpu.PrefetchScalarGridSpec(
            num_scalar_prefetch=1, grid=(steps,), in_specs=in_specs, out_specs=out_specs
        ),
        out_shape=tuple(shapes),
        compiler_params=params(),
        cost_estimate=cost(4),
        name="add_split",
    )(jnp.stack(sides), *operands)
    return [(out[2 * i], out[2 * i + 1]) for i in range(len(colors))]


def add_halves(colors):
    count = len(colors)
    _, rows, columns = colors[0][0].shape

    def kernel(*refs):
        ins, (mine_ref, theirs_ref) = refs[:-2], refs[-2:]
        for i in range(count):
            value = (ins[2 * i][...].astype(f32) + ins[2 * i + 1][...].astype(f32)).astype(bf16)
            mine_ref[i] = value[0]
            theirs_ref[i] = value[1]

    shape = jax.ShapeDtypeStruct((count, rows, columns), bf16)
    return pl.pallas_call(
        kernel,
        out_shape=(shape, shape),
        compiler_params=params(0),
        cost_estimate=cost(3),
        name="add_halves",
    )(*[a for pair in colors for a in pair])


def straighten(pieces, places, count):
    if (pieces[0].shape[0] // count) % 16:
        return [plain_order(p, at, count) for p, at in zip(pieces, places)], [jnp.int32(0)] * len(places), 1
    return pieces, places, count


def unpack_experts(own, other, places, core, count):
    pairs = len(own)
    flat, places, count = straighten([*own, *other], [*places, *places], count)
    rows, width = flat[0].shape
    block, hidden = rows // count, rows // 3

    def kernel(place_ref, *refs):
        ins, (gate_ref, up_ref, down_ref, plain_ref) = refs[: 2 * pairs], refs[2 * pairs :]
        e = pl.program_id(0)
        for pair in range(pairs):
            for far in range(2):
                ref = ins[far * pairs + pair]

                @pl.when(e == 2 * pair + (place_ref[pairs] ^ far))
                def _(ref=ref, pair=pair):
                    for i in range(count):
                        start = pl.multiple_of((i ^ place_ref[pair]) * block, block)
                        plain_ref[i * block : (i + 1) * block, :] = ref[pl.ds(start, block), :].astype(f32)

        gate_ref[0] = plain_ref[:hidden, :].T
        up_ref[0] = plain_ref[hidden : 2 * hidden, :].T
        down_ref[0] = plain_ref[2 * hidden :, :]

    wide = jax.ShapeDtypeStruct((2 * pairs, width, hidden), f32)
    tall = jax.ShapeDtypeStruct((2 * pairs, hidden, width), f32)
    return pl.pallas_call(
        kernel,
        grid_spec=pltpu.PrefetchScalarGridSpec(
            num_scalar_prefetch=1,
            grid=(2 * pairs,),
            in_specs=[pl.BlockSpec((rows, width), lambda e, s: (0, 0))] * (2 * pairs),
            out_specs=[
                pl.BlockSpec((1, width, hidden), lambda e, s: (e, 0, 0)),
                pl.BlockSpec((1, width, hidden), lambda e, s: (e, 0, 0)),
                pl.BlockSpec((1, hidden, width), lambda e, s: (e, 0, 0)),
            ],
            scratch_shapes=[pltpu.VMEM((rows, width), f32)],
        ),
        out_shape=(wide, wide, tall),
        compiler_params=params(),
        cost_estimate=cost(10),
        name="unpack_experts",
    )(jnp.stack([*places[:pairs], core]), *flat)


def unpack(own, other, places, core, count):
    colors = len(own)
    flat, places, count = straighten([*own, *other], [*places, *places], count)
    rows, columns = flat[0].shape
    block = rows // count
    shapes = (
        jax.ShapeDtypeStruct((colors * rows, 2 * GROUP), f32),
        jax.ShapeDtypeStruct((colors * rows, 2 * LANES), f32),
        jax.ShapeDtypeStruct((colors * rows, 2 * LANES), f32),
        jax.ShapeDtypeStruct((2 * GROUP, colors * rows), f32),
    )

    def kernel(place_ref, *refs):
        ins, (query_ref, key_ref, value_ref, output_ref, plain_ref) = refs[: 2 * colors], refs[2 * colors :]
        for group in range(2):
            for color in range(colors):
                for i in range(count):
                    start = pl.multiple_of((i ^ place_ref[color]) * block, block)
                    one = ins[color][pl.ds(start, block), :].astype(f32)
                    two = ins[colors + color][pl.ds(start, block), :].astype(f32)
                    plain_ref[i * block : (i + 1) * block, :] = jnp.where(place_ref[colors] == group, one, two)
                here = slice(color * rows, (color + 1) * rows)
                wide = slice(group * GROUP, (group + 1) * GROUP)
                thin = slice(group * LANES, (group + 1) * LANES)
                query_ref[here, wide] = plain_ref[:, :GROUP]
                key_ref[here, thin] = plain_ref[:, GROUP : GROUP + LANES]
                value_ref[here, thin] = plain_ref[:, GROUP + LANES : 2 * GROUP]
                output_ref[wide, here] = plain_ref[:, 2 * GROUP :].T

    return pl.pallas_call(
        kernel,
        grid_spec=pltpu.PrefetchScalarGridSpec(
            num_scalar_prefetch=1,
            grid=(1,),
            in_specs=[pl.BlockSpec((rows, columns), lambda i, s: (0, 0))] * (2 * colors),
            out_specs=[pl.BlockSpec(o.shape, lambda i, s: (0, 0)) for o in shapes],
            scratch_shapes=[pltpu.VMEM((rows, columns), f32)],
        ),
        out_shape=shapes,
        compiler_params=params(),
        cost_estimate=cost(6),
        name="unpack",
    )(jnp.stack([*places[:colors], core]), *flat)


def swap_tensor(values):
    return lax.ppermute(values, "tensor", [(0, 1), (1, 0)])


def swap_dp(values, bit):
    count = lax.axis_size("dp")
    return lax.ppermute(values, "dp", [(i, i ^ bit) for i in range(count)])


def after(values, earlier):
    return lax.optimization_barrier((values, earlier))[0]


def bit_of(bit):
    return (lax.axis_index("dp") // bit) % 2


def cut(values, index, axis, count=2):
    size = values.shape[axis] // count
    return lax.dynamic_slice_in_dim(values, index * size, size, axis)


def total(terms):
    out = terms[0].astype(f32)
    for term in terms[1:]:
        out = out + term.astype(f32)
    return out.astype(bf16)


def swap(values, bit):
    return swap_tensor(values) if bit == 0 else swap_dp(values, bit)


def place_of(order):
    place = 0
    for bit in order:
        if bit:
            place = 2 * place + bit_of(bit)
    return place


def gather_back(pieces, orders):
    for bits in zip(*(reversed(order) for order in orders)):
        got = yield list(zip(pieces, bits))
        pieces = [jnp.concatenate([p, g], 0) for p, g in zip(pieces, got)]
    got = yield [(p, 1) for p in pieces]
    return pieces, got


def sum_all(values):
    for bit in [0] + [1 << i for i in range(30) if (1 << i) < lax.axis_size("dp")]:
        (got,) = yield [(values, bit)]
        values = values + got
    return values


def experts_sum(kept, sent, orders, far):
    flat = kept.reshape(-1, *kept.shape[2:])
    (got,) = yield [(sent.reshape(flat.shape), 1)]
    colors = [[(flat, 2, i), (got, 2, i)] for i in range(len(orders))]
    for bits in zip(*orders):
        split = add_split(colors, [bit_of(b) for b in bits])
        got = yield [(s, b) for (_, s), b in zip(split, bits)]
        colors = [[(k, 2, 0), (g, 2, 0)] for (k, _), g in zip(split, got)]
    mine, theirs = add_halves([[t for t, _, _ in terms] for terms in colors])
    (got,) = yield [(theirs, 0)]
    count = len(orders)
    for bit in far:
        ((mine, theirs),) = add_split([[(mine, count, 0), (got, count, 0)]], [bit_of(bit)])
        (got,) = yield [(theirs, bit)]
    piece = total([mine, got])
    for bit in reversed(far):
        (got,) = yield [(piece, bit)]
        piece = jnp.concatenate([piece, got], 1)
    return (yield from gather_back([piece[i] for i in range(count)], orders))


def attention_sum(terms, orders, far):
    count = len(orders)
    parts = [t.reshape(count, t.shape[0] // count, t.shape[1]) for t in terms]
    colors = [[(p, 1, i) for p in parts] for i in range(count)]
    for bits in [*zip(*orders), *[(b,) * count for b in far]]:
        split = add_split(colors, [bit_of(b) for b in bits])
        got = yield [(s, b) for (_, s), b in zip(split, bits)]
        colors = [[(k, 1, 0), (g, 1, 0)] for (k, _), g in zip(split, got)]
    pieces = [total([k[0], g[0]]) for (k, _, _), (g, _, _) in colors]
    return (yield from gather_back(pieces, [[*order, *far] for order in orders]))


class Chains:
    def __init__(self):
        self.live = {}
        self.done = {}

    def advance(self, names=None, fence=None):
        names = [n for n in (names or list(self.live)) if n in self.live]
        requests = {}
        waiting = {n: self.live[n][1] for n in names}
        if fence is not None:
            fence, waiting = lax.optimization_barrier((fence, waiting))
        for n in names:
            chain = self.live[n][0]
            try:
                requests[n] = chain.send(waiting[n])
            except StopIteration as stop:
                self.done[n] = stop.value
                del self.live[n]
        sends = {n: [v for v, _ in r] for n, r in requests.items()}
        if fence is not None:
            fence, sends = lax.optimization_barrier((fence, sends))
        for n, r in requests.items():
            self.live[n] = (self.live[n][0], [swap(v, bit) for v, (_, bit) in zip(sends[n], r)])
        return fence

    def add(self, name, chain):
        self.live[name] = (chain, None)

    def finish(self):
        self.advance([n for n in self.live if self.live[n][1] is None], fence=())
        while self.live:
            self.advance(fence=())


def per_device(
    tokens, cotangent, segments, routes, slot_index,
    w_query, w_key, w_value, w_output, norm_attn, norm_ffn, w_router, w_gate, w_up, w_down,
):
    length, width = tokens.shape
    side = lax.axis_index("tensor")
    dp_size = lax.axis_size("dp")
    core = lax.axis_index("dp") % 2
    rows = SEQ_LEN
    far = [8 << i for i in range(20) if (8 << i) < dp_size]

    def own(values):
        return lax.dynamic_slice_in_dim(values, side * rows, rows, 0)

    x = own(tokens)
    cot = own(cotangent)
    seg = own(segments)
    seg_row, seg_col = seg[None, :], seg[:, None]
    routes_t = own(routes).T
    slots_t = own(slot_index).T
    wr_t = w_router.T
    gain_one, gain_two = norm_attn[None, :], norm_ffn[None, :]
    half_dim = HEAD_DIM // 2
    frequency = THETA ** (-(2.0 * jnp.arange(half_dim, dtype=f32)) / HEAD_DIM)
    freq = jnp.broadcast_to(frequency[:, None], (half_dim, LANES))

    near_own = [cut(w, core, 1) for w in (w_query, w_key, w_value)]
    order_index = lax.axis_index("dp") % 4
    near = [swap_tensor(w) for w in near_own]
    near_out = swap_tensor(after(cut(w_output, core, 0), near[0]))
    last = near_out
    got = []
    for w in (w_gate, w_up, w_down):
        last = swap_tensor(after(lax.dynamic_slice_in_dim(w, order_index, 1, 0), last))
        got.append(last)

    first, first_t, *tables = prologue(x, gain_one, seg_row, freq)
    saved_a = attend(first, w_query, w_key, w_value, tables, seg_col, seg_row)
    near, first = lax.optimization_barrier((near, (first, saved_a)))
    first, saved_a = first
    far_qkv = [swap_dp(w, 1) for w in near]
    saved_b = attend(first, *near, tables, seg_col, seg_row)
    (near_out, got[0]), (first, saved_b) = lax.optimization_barrier(((near_out, got[0]), (first, saved_b)))
    far_out = swap_dp(near_out, 1)
    across = [swap_dp(got[0], 2)]
    beside = [swap_dp(got[0], 1)]
    saved_c = attend(first, *far_qkv, tables, seg_col, seg_row)
    (across[0], got[1]), saved_c = lax.optimization_barrier(((across[0], got[1]), saved_c))
    across.append(swap_dp(got[1], 2))
    beside.append(swap_dp(got[1], 1))
    corner = [swap_dp(across[0], 1)]
    resid, second, gates, places = router(
        x, (saved_a[3], saved_b[3], saved_c[3]), (w_output, near_out, far_out), gain_two, wr_t, routes_t, slots_t
    )
    (across[1], got[2]), second = lax.optimization_barrier(((across[1], got[2]), second))
    across.append(swap_dp(got[2], 2))
    beside.append(swap_dp(got[2], 1))
    corner.append(swap_dp(across[1], 1))
    corner.append(swap_dp(across[2], 1))
    r_gate, r_up, r_down = (jnp.concatenate(parts, axis=0) for parts in zip(got, beside, across, corner))
    out, low_grad, resid_grad, small, kept, sent = experts_layer(
        order_index[None], second, cot, resid, gates, places, gain_two, wr_t,
        (w_gate, r_gate, w_up, r_up, w_down, r_down),
    )
    small = lax.psum(small, ("dp", "tensor"))

    chains = Chains()
    orders = ([2, 4], [4, 2])

    def piece_swaps(values, count, bit=0):
        size = values.shape[0] // count
        received = []
        for i in range(count):
            (got,) = yield [(values[i * size : (i + 1) * size], bit)]
            received.append(got)
        return received[0] if count == 1 else jnp.concatenate(received, 0)

    chains.add("grads", experts_sum(kept, sent, orders, far))
    chains.add("out", piece_swaps(out, 2))
    zero = jnp.zeros((1,), jnp.int32)
    one_minus = 1 - core[None]
    shared = (tables, seg_col, seg_row)

    low_grad = chains.advance(fence=low_grad)
    back = attend_back(zero, saved_c, *shared, low_grad, far_out)
    back = chains.advance(["grads"], fence=back)
    group_d, partial_sum = project(zero, back, saved_c[3], low_grad, first_t, *far_qkv)
    chains.add("other", piece_swaps(group_d, 1, 1))
    low_grad, partial_sum = chains.advance(["other", "out"], fence=(low_grad, partial_sum))
    back = attend_back(zero, saved_b, *shared, low_grad, near_out)
    back = chains.advance(["other"], fence=back)
    group_c, partial_sum = project(zero, back, saved_b[3], low_grad, first_t, *near, before=partial_sum)
    chains.add("theirs", piece_swaps(total([group_c, chains.done["other"]]), 1))
    low_grad, partial_sum = chains.advance(["grads", "out", "theirs"], fence=(low_grad, partial_sum))
    back = attend_back(one_minus, saved_a, *shared, low_grad, w_output)
    back = chains.advance(["grads"], fence=back)
    group_b, partial_sum = project(
        one_minus, back, saved_a[3], low_grad, first_t, w_query, w_key, w_value, before=partial_sum
    )
    chains.add("mine", piece_swaps(group_b, 1, 1))
    low_grad, partial_sum = chains.advance(["mine"], fence=(low_grad, partial_sum))
    back = attend_back(core[None], saved_a, *shared, low_grad, w_output)
    back = chains.advance(["grads", "mine", "theirs"], fence=back)
    group_a, token, norm_one = project(
        core[None], back, saved_a[3], low_grad, first_t, w_query, w_key, w_value,
        before=partial_sum, final=(x, gain_one, resid_grad),
    )
    chains.add("token", piece_swaps(token, 4))
    chains.add("tail", attention_sum((group_a, chains.done["mine"], chains.done["theirs"]), orders, far))
    chains.add("norm", sum_all(norm_one))
    chains.finish()
    done = chains.done

    place_far = place_of(far)
    size_far = 2 ** len(far)
    own_grads, other_grads = done["grads"]
    places = [place_of(order) * size_far + place_far for order in orders]
    grad_gate, grad_up, grad_down = unpack_experts(own_grads, other_grads, places, core, dp_size // 2)
    own_tail, other_tail = done["tail"]
    grad_query, grad_key, grad_value, grad_output = unpack(own_tail, other_tail, places, core, dp_size // 2)
    experts = w_router.shape[1]

    def both(mine, other):
        return jnp.where(side == 0, jnp.concatenate([mine, other], 0), jnp.concatenate([other, mine], 0))

    return (
        both(out, done["out"]),
        both(token, done["token"]).astype(f32),
        grad_query,
        grad_key,
        grad_value,
        grad_output,
        done["norm"][0],
        small[experts],
        small[:experts].T,
        grad_gate,
        grad_up,
        grad_down,
    )


def solution(mesh):
    placed = (
        P("dp", None), P("dp", None), P("dp"), P("dp", None), P("dp", None),
        P(None, "tensor"), P(None, "tensor"), P(None, "tensor"), P("tensor", None),
        P(), P(), P(),
        P(None, None, "tensor"), P(None, None, "tensor"), P(None, "tensor", None),
    )
    return jax.shard_map(
        per_device,
        mesh=mesh,
        in_specs=placed,
        out_specs=(
            P("dp", None), P("dp", None),
            P(None, "tensor"), P(None, "tensor"), P(None, "tensor"), P("tensor", None),
            P(), P(), P(),
            P(None, None, "tensor"), P(None, None, "tensor"), P(None, "tensor", None),
        ),
        check_vma=False,
    )
```

```python
from functools import partial

import jax
import jax.numpy as jnp
from jax import lax
from jax.experimental import pallas as pl
from jax.experimental.pallas import tpu as pltpu
from jax.sharding import PartitionSpec as P

HEAD_DIM = 64
SEQ_LEN = 1024
CAP = 256
EPS = 1e-06
THETA = 10000.0
NEG = -1e30
BLOCK = 256
LANES = 128
GROUP = 4 * HEAD_DIM

f32 = jnp.float32
bf16 = jnp.bfloat16


def nn(left, right):
    return lax.dot_general(left, right, (((1,), (0,)), ((), ())), preferred_element_type=f32)


def nt(left, right):
    return lax.dot_general(left, right, (((1,), (1,)), ((), ())), preferred_element_type=f32)


def tn(left, right):
    return lax.dot_general(left, right, (((0,), (0,)), ((), ())), preferred_element_type=f32)


def params(count=1):
    return pltpu.CompilerParams(
        dimension_semantics=("arbitrary",) * count if count else None,
        vmem_limit_bytes=60 * 1024 * 1024,
    )


def cost(micros):
    return pl.CostEstimate(flops=int(micros * 0.5e9), bytes_accessed=1 << 20, transcendentals=0)


def whole(shape):
    return pl.BlockSpec(shape, lambda *_: (0,) * len(shape))


def once(shape):
    return pl.BlockSpec(shape, lambda *_: (0,) * len(shape), pipeline_mode=pl.Buffered(1))


def lane_iota(rows, lanes=LANES):
    return lax.broadcasted_iota(jnp.int32, (rows, lanes), 1)


def prologue_kernel(side_ref, x_ref, gain_ref, seg_ref, freq_ref, first_ref, first_t_ref, cos_ref, up_ref, down_ref):
    rows = x_ref.shape[0]
    values = x_ref[...].astype(f32)
    scale = lax.rsqrt(jnp.mean(values * values, axis=-1, keepdims=True) + EPS)
    normed = values * scale * gain_ref[...].astype(f32)
    first_ref[...] = normed.astype(bf16)
    first_t_ref[...] = normed.astype(bf16).T
    seg = seg_ref[...]
    zeros = jnp.sum((seg == 0).astype(f32), axis=1, keepdims=True)
    ones = jnp.sum((seg == 1).astype(f32), axis=1, keepdims=True)
    places = lax.broadcasted_iota(jnp.int32, (1, rows), 1).astype(f32)
    places = places - jnp.where(seg >= 1, zeros, 0.0) - jnp.where(seg >= 2, ones, 0.0)
    angles = freq_ref[:, 0:1] * places
    cosine = jnp.cos(angles)
    sine = jnp.sin(angles)
    cosine = jnp.concatenate([cosine] * 4, axis=0).T
    sine = jnp.concatenate([sine] * 4, axis=0).T
    lower = (lane_iota(rows) % HEAD_DIM) < HEAD_DIM // 2
    cos_ref[...] = cosine
    up_ref[...] = jnp.where(lower, -sine, 0.0)
    down_ref[...] = jnp.where(lower, 0.0, sine)


def own_rows(shape):
    return pl.BlockSpec(shape, lambda i, s: (s[0], 0), pipeline_mode=pl.Buffered(1))


def prologue(side, tokens, gain, seg_row, freq):
    rows, width = seg_row.shape[1], tokens.shape[1]
    table = jax.ShapeDtypeStruct((rows, LANES), f32)
    shapes = (
        jax.ShapeDtypeStruct((rows, width), bf16),
        jax.ShapeDtypeStruct((width, rows), bf16),
        table,
        table,
        table,
    )
    return pl.pallas_call(
        prologue_kernel,
        grid_spec=pltpu.PrefetchScalarGridSpec(
            num_scalar_prefetch=1,
            grid=(1,),
            in_specs=[own_rows((rows, width)), once(gain.shape), once(seg_row.shape), once(freq.shape)],
            out_specs=[whole(o.shape) for o in shapes],
        ),
        out_shape=shapes,
        compiler_params=params(),
        cost_estimate=cost(5),
        name="prologue",
    )(side, tokens, gain, seg_row, freq)


def rotate(values, cosine, up, down):
    return (
        values * cosine
        + pltpu.roll(values, LANES - 32, 1) * up
        + pltpu.roll(values, 32, 1) * down
    )


def rotate_back(values, cosine, up, down):
    return (
        values * cosine
        - pltpu.roll(values, LANES - 32, 1) * up
        - pltpu.roll(values, 32, 1) * down
    )


def doubled(values):
    turned = pltpu.roll(values, HEAD_DIM, 1)
    left = lane_iota(values.shape[0]) < HEAD_DIM
    return (
        jnp.where(left, values, turned).astype(bf16),
        jnp.where(left, turned, values).astype(bf16),
    )


def halves_mask():
    left = (lane_iota(1) < HEAD_DIM).astype(f32)
    return left.astype(bf16), (1.0 - left).astype(bf16)


def attend_kernel(
    first_ref, wq_ref, wk_ref, wv_ref, cos_ref, up_ref, down_ref, segc_ref, segr_ref,
    q_ref, k_ref, v_ref, att_ref, lse_ref, bias_ref,
):
    rows = first_ref.shape[0]

    @pl.when(pl.program_id(0) == 0)
    def _():
        for start in range(0, rows, BLOCK):
            at_row = lax.broadcasted_iota(jnp.int32, (BLOCK, rows), 0) + start
            at_col = lax.broadcasted_iota(jnp.int32, (BLOCK, rows), 1)
            allowed = (at_col <= at_row) & (segc_ref[start : start + BLOCK, :] == segr_ref[...])
            bias_ref[start : start + BLOCK, :] = jnp.where(allowed, 0.0, NEG)

    first = first_ref[...]
    cosine, up, down = cos_ref[...], up_ref[...], down_ref[...]
    for tile in range(2):
        part = slice(tile * LANES, (tile + 1) * LANES)
        raw = nn(first, wq_ref[:, part])
        q_ref[:, part] = (rotate(raw, cosine, up, down) * HEAD_DIM**-0.5).astype(bf16)
    key = rotate(nn(first, wk_ref[...]), cosine, up, down)
    value = nn(first, wv_ref[...])
    k_ref[...] = key.astype(bf16)
    v_ref[...] = value.astype(bf16)
    keys, values = doubled(key), doubled(value)
    low, high = halves_mask()
    for start in range(0, rows, BLOCK):
        width = start + BLOCK
        mine = slice(start, width)
        bias = bias_ref[mine, :width]
        bias = jnp.concatenate([bias, bias], axis=0)
        logs = jnp.zeros((BLOCK, LANES), f32)
        lanes = lane_iota(BLOCK)
        for kv in range(2):
            part = slice(kv * LANES, (kv + 1) * LANES)
            query = q_ref[mine, part]
            query = jnp.concatenate([query * low, query * high], axis=0)
            scores = nt(query, keys[kv][:width]) + bias
            row_max = jnp.max(scores, axis=-1, keepdims=True)
            weights = jnp.exp(scores - row_max)
            total = jnp.sum(weights, axis=-1, keepdims=True)
            probs = (weights * (1.0 / total)).astype(bf16)
            out = nn(probs, values[kv][:width])
            att_ref[mine, part] = jnp.where(lanes < HEAD_DIM, out[:BLOCK], out[BLOCK:]).astype(bf16)
            log_total = row_max + jnp.log(total)
            logs = jnp.where(lanes == 2 * kv, log_total[:BLOCK], logs)
            logs = jnp.where(lanes == 2 * kv + 1, log_total[BLOCK:], logs)
        lse_ref[0, :, mine] = logs.T[:8]


def attend(first, wq, wk, wv, tables, seg_col, seg_row):
    rows, width = first.shape
    groups = wq.shape[1] // GROUP
    table = whole((rows, LANES))
    return pl.pallas_call(
        attend_kernel,
        grid=(groups,),
        in_specs=[
            whole((rows, width)),
            pl.BlockSpec((width, GROUP), lambda g: (0, g)),
            pl.BlockSpec((width, LANES), lambda g: (0, g)),
            pl.BlockSpec((width, LANES), lambda g: (0, g)),
            table,
            table,
            table,
            whole((rows, 1)),
            whole((1, rows)),
        ],
        out_specs=[
            pl.BlockSpec((rows, GROUP), lambda g: (0, g)),
            pl.BlockSpec((rows, LANES), lambda g: (0, g)),
            pl.BlockSpec((rows, LANES), lambda g: (0, g)),
            pl.BlockSpec((rows, GROUP), lambda g: (0, g)),
            pl.BlockSpec((1, 8, rows), lambda g: (g, 0, 0)),
        ],
        out_shape=(
            jax.ShapeDtypeStruct((rows, groups * GROUP), bf16),
            jax.ShapeDtypeStruct((rows, groups * LANES), bf16),
            jax.ShapeDtypeStruct((rows, groups * LANES), bf16),
            jax.ShapeDtypeStruct((rows, groups * GROUP), bf16),
            jax.ShapeDtypeStruct((groups, 8, rows), f32),
        ),
        scratch_shapes=[pltpu.VMEM((rows, rows), f32)],
        compiler_params=params(),
        cost_estimate=cost(10 * groups),
        name="attend",
    )(first, wq, wk, wv, *tables, seg_col, seg_row)


def router_kernel(
    side_ref, x_ref, att_a_ref, att_b_ref, att_c_ref, wo_a_ref, wo_b_ref, wo_c_ref, gain_ref, wr_ref, routes_ref, slots_ref,
    resid_ref, second_ref, gates_ref, places_ref,
):
    mixed = nn(att_a_ref[...], wo_a_ref[...])
    mixed = mixed + nn(att_b_ref[...], wo_b_ref[...])
    mixed = mixed + nn(att_c_ref[...], wo_c_ref[...])
    resid = x_ref[...].astype(f32) + mixed
    resid_ref[...] = resid
    scale = lax.rsqrt(jnp.mean(resid * resid, axis=-1, keepdims=True) + EPS)
    second = (resid * scale * gain_ref[...].astype(f32)).astype(bf16)
    second_ref[...] = second
    logits = nt(wr_ref[...], second)
    experts, rows = logits.shape
    routes, slots = routes_ref[...], slots_ref[...]
    number = lax.broadcasted_iota(jnp.int32, (experts, rows), 0)
    chosen = jnp.zeros((experts, rows), f32)
    place = jnp.zeros((8, rows), jnp.int32)
    taken = jnp.zeros((8, rows), jnp.int32)
    for k in range(routes.shape[0]):
        hit = number == routes[k : k + 1, :]
        chosen = jnp.where(hit, 1.0, chosen)
        hit = number[:8] == routes[k : k + 1, :]
        place = jnp.where(hit, slots[k : k + 1, :], place)
        taken = jnp.where(hit, 1, taken)
    places_ref[...] = jnp.where(taken > 0, place, CAP)
    top = jnp.max(jnp.where(chosen > 0, logits, NEG), axis=0, keepdims=True)
    weights = jnp.where(chosen > 0, jnp.exp(logits - top), 0.0)
    gates_ref[...] = weights / jnp.sum(weights, axis=0, keepdims=True)


def router(side, tokens, attended, outputs, gain, wr_t, routes_t, slots_t):
    rows, width = routes_t.shape[1], tokens.shape[1]
    rest = (*attended, *outputs, gain, wr_t, routes_t, slots_t)
    shapes = (
        jax.ShapeDtypeStruct((rows, width), f32),
        jax.ShapeDtypeStruct((rows, width), bf16),
        jax.ShapeDtypeStruct((wr_t.shape[0], rows), f32),
        jax.ShapeDtypeStruct((8, rows), jnp.int32),
    )
    return pl.pallas_call(
        router_kernel,
        grid_spec=pltpu.PrefetchScalarGridSpec(
            num_scalar_prefetch=1,
            grid=(1,),
            in_specs=[own_rows((rows, width)), *[once(a.shape) for a in rest]],
            out_specs=[whole(o.shape) for o in shapes],
        ),
        out_shape=shapes,
        compiler_params=params(),
        cost_estimate=cost(8),
        name="router",
    )(side, tokens, *rest)


def split_three(values):
    first = values.astype(bf16)
    rest = values - first.astype(f32)
    second = rest.astype(bf16)
    return first, second, (rest - second.astype(f32)).astype(bf16)


def experts_kernel(
    order_ref, second_ref, cot_ref, resid_ref, gates_ref, places_ref, gain_ref, wr_ref,
    wg_a_ref, wg_b_ref, wu_a_ref, wu_b_ref, wd_a_ref, wd_b_ref,
    out_ref, low_t_ref, low_ref, grad_ref, small_ref, kept_ref, sent_ref,
    moe_ref, slot_grads_ref,
):
    step = pl.program_id(0)
    e = step ^ order_ref[0]
    rows = second_ref.shape[0]
    second = second_ref[...]
    slots = lax.broadcasted_iota(jnp.int32, (CAP, rows), 0)
    hit = slots == places_ref[pl.ds(e, 1), :]
    gate_slot = jnp.sum(jnp.where(hit, gates_ref[pl.ds(e, 1), :], 0.0), axis=1, keepdims=True)
    onehot = jnp.where(hit, 1.0, 0.0).astype(bf16)
    expert_in = nn(onehot, second).astype(bf16)
    slot_grad = nn(onehot, cot_ref[...])
    out_grad = (gate_slot * slot_grad).astype(bf16)
    expert_out = None
    back = None
    factors = []
    for wg_ref, wu_ref, wd_ref in ((wg_a_ref, wu_a_ref, wd_a_ref), (wg_b_ref, wu_b_ref, wd_b_ref)):
        wg, wu, wd = wg_ref[0], wu_ref[0], wd_ref[0]
        gate_pre = nn(expert_in, wg)
        up_pre = nn(expert_in, wu)
        sig = 1.0 / (1.0 + jnp.exp(-gate_pre))
        silu = gate_pre * sig
        hidden = (silu * up_pre).astype(bf16)
        part = nn(hidden, wd)
        expert_out = part if expert_out is None else expert_out + part
        hidden_grad = nt(out_grad, wd)
        gate_low = (hidden_grad * up_pre * sig * (1.0 + gate_pre * (1.0 - sig))).astype(bf16)
        up_low = (hidden_grad * silu).astype(bf16)
        factors.append((gate_low, up_low, hidden))
        part = nt(gate_low, wg) + nt(up_low, wu)
        back = part if back is None else back + part

    def weight_grads(ref):
        size = hidden.shape[1]
        for half, (gate_low, up_low, mixed) in enumerate(factors):
            ref[0, half, :size, :] = tn(gate_low, expert_in).astype(bf16)
            ref[0, half, size : 2 * size, :] = tn(up_low, expert_in).astype(bf16)
            ref[0, half, 2 * size :, :] = tn(mixed, out_grad).astype(bf16)

    @pl.when(step % 2 == 0)
    def _():
        weight_grads(kept_ref)

    @pl.when(step % 2 == 1)
    def _():
        weight_grads(sent_ref)

    slot_gate = jnp.sum(expert_out * slot_grad, axis=1, keepdims=True)
    gate_row = jnp.sum(jnp.where(hit, slot_gate, 0.0), axis=0, keepdims=True)
    moe = tn(onehot, (gate_slot * expert_out).astype(bf16))
    second_back = tn(onehot, back.astype(bf16))

    @pl.when(step == 0)
    def _():
        moe_ref[...] = moe
        grad_ref[...] = second_back
        slot_grads_ref[...] = jnp.zeros_like(slot_grads_ref)

    @pl.when(step > 0)
    def _():
        moe_ref[...] += moe
        grad_ref[...] += second_back

    slot_grads_ref[pl.ds(e, 1), :] = gate_row

    @pl.when(step == pl.num_programs(0) - 1)
    def _():
        gates = gates_ref[...]
        resid = resid_ref[...]
        out_ref[...] = (resid + moe_ref[...]).astype(bf16)
        gate_grad = slot_grads_ref[...]
        logit_grad = gates * (gate_grad - jnp.sum(gates * gate_grad, axis=0, keepdims=True))
        router_grad = None
        second_grad = grad_ref[...]
        for piece in split_three(logit_grad):
            part = nn(piece, second)
            router_grad = part if router_grad is None else router_grad + part
            second_grad = second_grad + tn(piece, wr_ref[...])
        experts = gates.shape[0]
        small_ref[0:experts, :] = router_grad
        gain = gain_ref[...].astype(f32)
        scale = lax.rsqrt(jnp.mean(resid * resid, axis=-1, keepdims=True) + EPS)
        norm_grad = jnp.sum(second_grad * resid * scale, axis=0, keepdims=True)
        small_ref[experts : experts + 8, :] = jnp.where(
            lax.broadcasted_iota(jnp.int32, (8, resid.shape[1]), 0) == 0, norm_grad, 0.0
        )
        inner = jnp.mean(gain * second_grad * resid, axis=-1, keepdims=True)
        grad = scale * gain * second_grad - resid * (scale * scale * scale) * inner
        grad = grad + cot_ref[...].astype(f32)
        grad_ref[...] = grad
        low_ref[...] = grad.astype(bf16)
        low_t_ref[...] = grad.astype(bf16).T


def experts_layer(order, second, cot, resid, gates, places, gain, wr_t, weights):
    rows, width = second.shape
    own_cot = pl.BlockSpec((rows, width), lambda i, o: (o[1], 0), pipeline_mode=pl.Buffered(1))
    experts = gates.shape[0]
    window, _, hidden = weights[0].shape
    wide = pl.BlockSpec((1, width, hidden), lambda i, o: (i ^ o[0], 0, 0))
    tall = pl.BlockSpec((1, hidden, width), lambda i, o: (i ^ o[0], 0, 0))
    wide_rel = pl.BlockSpec((1, width, hidden), lambda i, o: (i, 0, 0))
    tall_rel = pl.BlockSpec((1, hidden, width), lambda i, o: (i, 0, 0))
    grads_out = jax.ShapeDtypeStruct((window // 2, 2, 3 * hidden, width), bf16)
    grads = pl.BlockSpec((1, 2, 3 * hidden, width), lambda i, o: ((i // 2) ^ (o[0] // 2), 0, 0, 0))
    return pl.pallas_call(
        experts_kernel,
        grid_spec=pltpu.PrefetchScalarGridSpec(
        num_scalar_prefetch=1,
        grid=(window,),
        in_specs=[
            once((rows, width)),
            own_cot,
            once((rows, width)),
            whole((experts, rows)),
            whole((8, rows)),
            whole((1, width)),
            whole((experts, width)),
            wide,
            wide_rel,
            wide,
            wide_rel,
            tall,
            tall_rel,
        ],
        out_specs=[
            once((rows, width)),
            once((width, rows)),
            once((rows, width)),
            once((rows, width)),
            whole((experts + 8, width)),
            grads,
            grads,
        ],
        scratch_shapes=[
            pltpu.VMEM((rows, width), f32),
            pltpu.VMEM((experts, rows), f32),
        ],
        ),
        out_shape=(
            jax.ShapeDtypeStruct((rows, width), bf16),
            jax.ShapeDtypeStruct((width, rows), bf16),
            jax.ShapeDtypeStruct((rows, width), bf16),
            jax.ShapeDtypeStruct((rows, width), f32),
            jax.ShapeDtypeStruct((experts + 8, width), f32),
            grads_out,
            grads_out,
        ),
        compiler_params=params(),
        cost_estimate=cost(39),
        name="experts",
    )(order, second, cot, resid, gates, places, gain, wr_t, *weights)


def attend_back_kernel(
    sel_ref, q_ref, k_ref, v_ref, lse_ref, cos_ref, up_ref, down_ref, segc_ref, segr_ref, low_ref, wo_ref,
    back_ref, bias_ref, dq_ref, dk_ref, dv_ref,
):
    rows = q_ref.shape[0]
    for start in range(0, rows, BLOCK):
        at_key = lax.broadcasted_iota(jnp.int32, (BLOCK, rows), 0) + start
        at_query = lax.broadcasted_iota(jnp.int32, (BLOCK, rows), 1)
        allowed = (at_key <= at_query) & (segc_ref[start : start + BLOCK, :] == segr_ref[...])
        bias_ref[start : start + BLOCK, :] = jnp.where(allowed, 0.0, NEG)
    upward = nt(low_ref[...], wo_ref[...]).astype(bf16)
    keys = doubled(k_ref[...].astype(f32))
    values = doubled(v_ref[...].astype(f32))
    low, high = halves_mask()
    dk_ref[...] = jnp.zeros_like(dk_ref)
    dv_ref[...] = jnp.zeros_like(dv_ref)
    lanes = lane_iota(BLOCK)
    for start in range(0, rows, BLOCK):
        width = start + BLOCK
        mine = slice(start, width)
        bias = bias_ref[:width, mine]
        bias = jnp.concatenate([bias, bias], axis=1)
        for kv in range(2):
            part = slice(kv * LANES, (kv + 1) * LANES)
            query = q_ref[mine, part]
            query = jnp.concatenate([query * low, query * high], axis=0)
            upper = upward[mine, part]
            upper = jnp.concatenate([upper * low, upper * high], axis=0)
            logs = jnp.concatenate(
                [lse_ref[0, 2 * kv : 2 * kv + 1, mine], lse_ref[0, 2 * kv + 1 : 2 * kv + 2, mine]], axis=1
            )
            key = keys[kv][:width]
            probs = jnp.exp(nt(key, query) + bias - logs)
            prob_grad = nt(values[kv][:width], upper)
            product = probs * prob_grad
            delta = jnp.sum(product, axis=0, keepdims=True)
            raw = (product - probs * delta).astype(bf16)
            dv_ref[kv, :width, :] += nn(probs.astype(bf16), upper)
            dk_ref[kv, :width, :] += nn(raw, query)
            back = tn(raw, key)
            dq_ref[mine, part] = jnp.where(lanes < HEAD_DIM, back[:BLOCK], back[BLOCK:])
    cosine, up, down = cos_ref[...], up_ref[...], down_ref[...]
    left = lane_iota(rows) < HEAD_DIM

    def both(ref):
        one, two = ref[0], ref[1]
        one = one + pltpu.roll(one, HEAD_DIM, 1)
        two = two + pltpu.roll(two, HEAD_DIM, 1)
        return jnp.where(left, one, two)

    back_ref[:, 2 * LANES : 3 * LANES] = rotate_back(both(dk_ref), cosine, up, down).astype(bf16)
    back_ref[:, 3 * LANES :] = both(dv_ref).astype(bf16)
    for kv in range(2):
        part = slice(kv * LANES, (kv + 1) * LANES)
        turned = rotate_back(dq_ref[:, part], cosine, up, down)
        back_ref[:, part] = (turned * HEAD_DIM**-0.5).astype(bf16)


def attend_back(sel, saved, tables, seg_col, seg_row, low_grad, wo):
    query, key, value, _, logs = saved
    rows, width = low_grad.shape

    def fixed(shape):
        return pl.BlockSpec(shape, lambda i, s: (0,) * len(shape))

    table = fixed((rows, LANES))
    wide = pl.BlockSpec((rows, GROUP), lambda i, s: (0, s[0]))
    thin = pl.BlockSpec((rows, LANES), lambda i, s: (0, s[0]))
    return pl.pallas_call(
        attend_back_kernel,
        grid_spec=pltpu.PrefetchScalarGridSpec(
            num_scalar_prefetch=1,
            grid=(1,),
            in_specs=[
                wide, thin, thin, pl.BlockSpec((1, 8, rows), lambda i, s: (s[0], 0, 0)),
                table, table, table, fixed((rows, 1)), fixed((1, rows)),
                fixed((rows, width)), pl.BlockSpec((GROUP, width), lambda i, s: (s[0], 0)),
            ],
            out_specs=fixed((rows, 2 * GROUP)),
            scratch_shapes=[
                pltpu.VMEM((rows, rows), f32),
                pltpu.VMEM((rows, GROUP), f32),
                pltpu.VMEM((2, rows, LANES), f32),
                pltpu.VMEM((2, rows, LANES), f32),
            ],
        ),
        out_shape=jax.ShapeDtypeStruct((rows, 2 * GROUP), bf16),
        compiler_params=params(),
        cost_estimate=cost(14),
        name="attend_back",
    )(sel, query, key, value, logs, *tables, seg_col, seg_row, low_grad, wo)


def project_kernel(final, fresh, sel_ref, back_ref, att_ref, low_t_ref, first_t_ref, wq_ref, wk_ref, wv_ref, *rest):
    if not fresh:
        before_ref, *rest = rest
    if final:
        x_ref, gain_ref, grad_ref, group_ref, token_ref, norm_ref = rest
    else:
        group_ref, sum_ref = rest
    back = back_ref[...]
    group_ref[:, : 2 * GROUP] = nn(first_t_ref[...], back).astype(bf16)
    group_ref[:, 2 * GROUP :] = nn(low_t_ref[...], att_ref[...]).astype(bf16)
    first_grad = nt(back[:, :GROUP], wq_ref[...])
    first_grad = first_grad + nt(back[:, GROUP : GROUP + LANES], wk_ref[...])
    first_grad = first_grad + nt(back[:, GROUP + LANES :], wv_ref[...])
    if not fresh:
        first_grad = before_ref[...] + first_grad
    if final:
        inputs = x_ref[...].astype(f32)
        gain = gain_ref[...].astype(f32)
        scale = lax.rsqrt(jnp.mean(inputs * inputs, axis=-1, keepdims=True) + EPS)
        norm_ref[...] = jnp.broadcast_to(
            jnp.sum(first_grad * inputs * scale, axis=0, keepdims=True), norm_ref.shape
        )
        inner = jnp.mean(gain * first_grad * inputs, axis=-1, keepdims=True)
        grad = scale * gain * first_grad - inputs * (scale * scale * scale) * inner
        token_ref[...] = (grad + grad_ref[...]).astype(bf16)
    else:
        sum_ref[...] = first_grad


def project(sel, back, att, low_t, first_t, wq, wk, wv, before=None, final=None):
    width, rows = low_t.shape

    def fixed(shape):
        return pl.BlockSpec(shape, lambda i, s: (0,) * len(shape))

    wide_w = pl.BlockSpec((width, GROUP), lambda i, s: (0, s[0]))
    thin_w = pl.BlockSpec((width, LANES), lambda i, s: (0, s[0]))
    square = fixed((rows, width))
    in_specs = [
        fixed((rows, 2 * GROUP)), pl.BlockSpec((rows, GROUP), lambda i, s: (0, s[0])),
        fixed((width, rows)), fixed((width, rows)), wide_w, thin_w, thin_w,
    ]
    out_specs = [fixed((width, 3 * GROUP))]
    out_shape = [jax.ShapeDtypeStruct((width, 3 * GROUP), bf16)]
    extra = ()
    if before is not None:
        in_specs.append(square)
        extra = (before,)
    if final is None:
        out_specs.append(square)
        out_shape.append(jax.ShapeDtypeStruct((rows, width), f32))
    else:
        extra = (*extra, *final)
        in_specs += [pl.BlockSpec((rows, width), lambda i, s: (s[1], 0)), fixed((1, width)), square]
        out_specs += [square, fixed((8, width))]
        out_shape += [
            jax.ShapeDtypeStruct((rows, width), bf16),
            jax.ShapeDtypeStruct((8, width), f32),
        ]
    return pl.pallas_call(
        partial(project_kernel, final is not None, before is None),
        grid_spec=pltpu.PrefetchScalarGridSpec(
            num_scalar_prefetch=1, grid=(1,), in_specs=in_specs, out_specs=out_specs
        ),
        out_shape=tuple(out_shape),
        compiler_params=params(),
        cost_estimate=cost(7),
        name="project_final" if final is not None else "project",
    )(sel, back, att, low_t, first_t, wq, wk, wv, *extra)


def plain_order(piece, place, count):
    shape = piece.shape
    bit = 1
    while bit < count:
        pairs = piece.reshape(-1, 2, bit * shape[0] // count, shape[1])
        flipped = jnp.concatenate([pairs[:, 1:], pairs[:, :1]], axis=1)
        piece = jnp.where((place // bit) % 2 == 1, flipped, pairs)
        bit *= 2
    return piece.reshape(shape)


def add_split(colors, sides):
    rows = [terms[0][0].shape[1] for terms in colors]
    half = rows[0] // 2
    if half % 16:
        out = []
        for terms, side in zip(colors, sides):
            cutouts = [lax.slice_in_dim(t, i * n, (i + 1) * n, axis=0) for t, n, i in terms]
            both = []
            for at in (side, 1 - side):
                pieces = [lax.dynamic_slice_in_dim(t, at * half, half, 1).astype(f32) for t in cutouts]
                both.append(sum(pieces[1:], pieces[0]).astype(bf16))
            out.append(tuple(both))
        return out
    steps = 4 if half % 64 == 0 else (2 if half % 32 == 0 else 1)
    block = half // steps
    in_specs, operands, out_specs, shapes, counts = [], [], [], [], []
    for number, terms in enumerate(colors):
        counts.append(len(terms))
        for other in (0, 1):
            for array, lead, index in terms:

                def place(j, s, number=number, index=index, other=other):
                    return (index, (s[number] ^ other) * steps + j, 0)

                in_specs.append(pl.BlockSpec((lead, block, array.shape[2]), place))
                operands.append(array)
        array, lead, _ = terms[0]
        for _ in range(2):
            out_specs.append(pl.BlockSpec((lead, block, array.shape[2]), lambda j, s: (0, j, 0)))
            shapes.append(jax.ShapeDtypeStruct((lead, half, array.shape[2]), bf16))

    def kernel(side_ref, *refs):
        ins, outs = refs[: len(operands)], refs[len(operands) :]
        at = 0
        for number, count in enumerate(counts):
            for other in range(2):
                value = ins[at][...].astype(f32)
                for term in range(1, count):
                    value = value + ins[at + term][...].astype(f32)
                outs[2 * number + other][...] = value.astype(bf16)
                at += count

    out = pl.pallas_call(
        kernel,
        grid_spec=pltpu.PrefetchScalarGridSpec(
            num_scalar_prefetch=1, grid=(steps,), in_specs=in_specs, out_specs=out_specs
        ),
        out_shape=tuple(shapes),
        compiler_params=params(),
        cost_estimate=cost(4),
        name="add_split",
    )(jnp.stack(sides), *operands)
    return [(out[2 * i], out[2 * i + 1]) for i in range(len(colors))]


def add_halves(colors):
    count = len(colors)
    _, rows, columns = colors[0][0].shape

    def kernel(*refs):
        ins, (mine_ref, theirs_ref) = refs[:-2], refs[-2:]
        for i in range(count):
            value = (ins[2 * i][...].astype(f32) + ins[2 * i + 1][...].astype(f32)).astype(bf16)
            mine_ref[i] = value[0]
            theirs_ref[i] = value[1]

    shape = jax.ShapeDtypeStruct((count, rows, columns), bf16)
    return pl.pallas_call(
        kernel,
        out_shape=(shape, shape),
        compiler_params=params(0),
        cost_estimate=cost(3),
        name="add_halves",
    )(*[a for pair in colors for a in pair])


def straighten(pieces, places, count):
    if (pieces[0].shape[0] // count) % 16:
        return [plain_order(p, at, count) for p, at in zip(pieces, places)], [jnp.int32(0)] * len(places), 1
    return pieces, places, count


def unpack_experts(own, other, places, core, count):
    pairs = len(own)
    flat, places, count = straighten([*own, *other], [*places, *places], count)
    rows, width = flat[0].shape
    block, hidden = rows // count, rows // 3

    def kernel(place_ref, *refs):
        ins, (gate_ref, up_ref, down_ref, plain_ref) = refs[: 2 * pairs], refs[2 * pairs :]
        e = pl.program_id(0)
        for pair in range(pairs):
            for far in range(2):
                ref = ins[far * pairs + pair]

                @pl.when(e == 2 * pair + (place_ref[pairs] ^ far))
                def _(ref=ref, pair=pair):
                    for i in range(count):
                        start = pl.multiple_of((i ^ place_ref[pair]) * block, block)
                        plain_ref[i * block : (i + 1) * block, :] = ref[pl.ds(start, block), :].astype(f32)

        gate_ref[0] = plain_ref[:hidden, :].T
        up_ref[0] = plain_ref[hidden : 2 * hidden, :].T
        down_ref[0] = plain_ref[2 * hidden :, :]

    wide = jax.ShapeDtypeStruct((2 * pairs, width, hidden), f32)
    tall = jax.ShapeDtypeStruct((2 * pairs, hidden, width), f32)
    return pl.pallas_call(
        kernel,
        grid_spec=pltpu.PrefetchScalarGridSpec(
            num_scalar_prefetch=1,
            grid=(2 * pairs,),
            in_specs=[pl.BlockSpec((rows, width), lambda e, s: (0, 0))] * (2 * pairs),
            out_specs=[
                pl.BlockSpec((1, width, hidden), lambda e, s: (e, 0, 0)),
                pl.BlockSpec((1, width, hidden), lambda e, s: (e, 0, 0)),
                pl.BlockSpec((1, hidden, width), lambda e, s: (e, 0, 0)),
            ],
            scratch_shapes=[pltpu.VMEM((rows, width), f32)],
        ),
        out_shape=(wide, wide, tall),
        compiler_params=params(),
        cost_estimate=cost(10),
        name="unpack_experts",
    )(jnp.stack([*places[:pairs], core]), *flat)


def unpack(own, other, places, core, count):
    colors = len(own)
    flat, places, count = straighten([*own, *other], [*places, *places], count)
    rows, columns = flat[0].shape
    block = rows // count
    shapes = (
        jax.ShapeDtypeStruct((colors * rows, 2 * GROUP), f32),
        jax.ShapeDtypeStruct((colors * rows, 2 * LANES), f32),
        jax.ShapeDtypeStruct((colors * rows, 2 * LANES), f32),
        jax.ShapeDtypeStruct((2 * GROUP, colors * rows), f32),
    )

    def kernel(place_ref, *refs):
        ins, (query_ref, key_ref, value_ref, output_ref, plain_ref) = refs[: 2 * colors], refs[2 * colors :]
        for group in range(2):
            for color in range(colors):
                for i in range(count):
                    start = pl.multiple_of((i ^ place_ref[color]) * block, block)
                    one = ins[color][pl.ds(start, block), :].astype(f32)
                    two = ins[colors + color][pl.ds(start, block), :].astype(f32)
                    plain_ref[i * block : (i + 1) * block, :] = jnp.where(place_ref[colors] == group, one, two)
                here = slice(color * rows, (color + 1) * rows)
                wide = slice(group * GROUP, (group + 1) * GROUP)
                thin = slice(group * LANES, (group + 1) * LANES)
                query_ref[here, wide] = plain_ref[:, :GROUP]
                key_ref[here, thin] = plain_ref[:, GROUP : GROUP + LANES]
                value_ref[here, thin] = plain_ref[:, GROUP + LANES : 2 * GROUP]
                output_ref[wide, here] = plain_ref[:, 2 * GROUP :].T

    return pl.pallas_call(
        kernel,
        grid_spec=pltpu.PrefetchScalarGridSpec(
            num_scalar_prefetch=1,
            grid=(1,),
            in_specs=[pl.BlockSpec((rows, columns), lambda i, s: (0, 0))] * (2 * colors),
            out_specs=[pl.BlockSpec(o.shape, lambda i, s: (0, 0)) for o in shapes],
            scratch_shapes=[pltpu.VMEM((rows, columns), f32)],
        ),
        out_shape=shapes,
        compiler_params=params(),
        cost_estimate=cost(6),
        name="unpack",
    )(jnp.stack([*places[:colors], core]), *flat)


def swap_tensor(values):
    return lax.ppermute(values, "tensor", [(0, 1), (1, 0)])


def swap_dp(values, bit):
    count = lax.axis_size("dp")
    return lax.ppermute(values, "dp", [(i, i ^ bit) for i in range(count)])


def after(values, earlier):
    return lax.optimization_barrier((values, earlier))[0]


def bit_of(bit):
    return (lax.axis_index("dp") // bit) % 2


def cut(values, index, axis, count=2):
    size = values.shape[axis] // count
    return lax.dynamic_slice_in_dim(values, index * size, size, axis)


def total(terms):
    out = terms[0].astype(f32)
    for term in terms[1:]:
        out = out + term.astype(f32)
    return out.astype(bf16)


def swap(values, bit):
    return swap_tensor(values) if bit == 0 else swap_dp(values, bit)


def place_of(order):
    place = 0
    for bit in order:
        if bit:
            place = 2 * place + bit_of(bit)
    return place


def gather_back(pieces, orders):
    for bits in zip(*(reversed(order) for order in orders)):
        got = yield list(zip(pieces, bits))
        pieces = [jnp.concatenate([p, g], 0) for p, g in zip(pieces, got)]
    got = yield [(p, 1) for p in pieces]
    return pieces, got


def sum_all(values):
    for bit in [0] + [1 << i for i in range(30) if (1 << i) < lax.axis_size("dp")]:
        (got,) = yield [(values, bit)]
        values = values + got
    return values


def experts_sum(kept, sent, orders, far):
    flat = kept.reshape(-1, *kept.shape[2:])
    (got,) = yield [(sent.reshape(flat.shape), 1)]
    colors = [[(flat, 2, i), (got, 2, i)] for i in range(len(orders))]
    for bits in zip(*orders):
        split = add_split(colors, [bit_of(b) for b in bits])
        got = yield [(s, b) for (_, s), b in zip(split, bits)]
        colors = [[(k, 2, 0), (g, 2, 0)] for (k, _), g in zip(split, got)]
    mine, theirs = add_halves([[t for t, _, _ in terms] for terms in colors])
    (got,) = yield [(theirs, 0)]
    count = len(orders)
    for bit in far:
        ((mine, theirs),) = add_split([[(mine, count, 0), (got, count, 0)]], [bit_of(bit)])
        (got,) = yield [(theirs, bit)]
    piece = total([mine, got])
    for bit in reversed(far):
        (got,) = yield [(piece, bit)]
        piece = jnp.concatenate([piece, got], 1)
    return (yield from gather_back([piece[i] for i in range(count)], orders))


def attention_sum(terms, orders, far):
    count = len(orders)
    parts = [t.reshape(count, t.shape[0] // count, t.shape[1]) for t in terms]
    colors = [[(p, 1, i) for p in parts] for i in range(count)]
    for bits in [*zip(*orders), *[(b,) * count for b in far]]:
        split = add_split(colors, [bit_of(b) for b in bits])
        got = yield [(s, b) for (_, s), b in zip(split, bits)]
        colors = [[(k, 1, 0), (g, 1, 0)] for (k, _), g in zip(split, got)]
    pieces = [total([k[0], g[0]]) for (k, _, _), (g, _, _) in colors]
    return (yield from gather_back(pieces, [[*order, *far] for order in orders]))


class Chains:
    def __init__(self):
        self.live = {}
        self.done = {}

    def advance(self, names=None, fence=None):
        names = [n for n in (names or list(self.live)) if n in self.live]
        requests = {}
        waiting = {n: self.live[n][1] for n in names}
        if fence is not None:
            fence, waiting = lax.optimization_barrier((fence, waiting))
        for n in names:
            chain = self.live[n][0]
            try:
                requests[n] = chain.send(waiting[n])
            except StopIteration as stop:
                self.done[n] = stop.value
                del self.live[n]
        sends = {n: [v for v, _ in r] for n, r in requests.items()}
        if fence is not None:
            fence, sends = lax.optimization_barrier((fence, sends))
        for n, r in requests.items():
            self.live[n] = (self.live[n][0], [swap(v, bit) for v, (_, bit) in zip(sends[n], r)])
        return fence

    def add(self, name, chain):
        self.live[name] = (chain, None)

    def finish(self):
        self.advance([n for n in self.live if self.live[n][1] is None], fence=())
        while self.live:
            self.advance(fence=())


def per_device(
    tokens, cotangent, segments, routes, slot_index,
    w_query, w_key, w_value, w_output, norm_attn, norm_ffn, w_router, w_gate, w_up, w_down,
):
    length, width = tokens.shape
    side = lax.axis_index("tensor")
    dp_size = lax.axis_size("dp")
    core = lax.axis_index("dp") % 2
    rows = SEQ_LEN
    far = [8 << i for i in range(20) if (8 << i) < dp_size]

    def own(values):
        return lax.dynamic_slice_in_dim(values, side * rows, rows, 0)

    seg = own(segments)
    seg_row, seg_col = seg[None, :], seg[:, None]
    routes_t = own(routes).T
    slots_t = own(slot_index).T
    wr_t = w_router.T
    gain_one, gain_two = norm_attn[None, :], norm_ffn[None, :]
    half_dim = HEAD_DIM // 2
    frequency = THETA ** (-(2.0 * jnp.arange(half_dim, dtype=f32)) / HEAD_DIM)
    freq = jnp.broadcast_to(frequency[:, None], (half_dim, LANES))

    near_own = [cut(w, core, 1) for w in (w_query, w_key, w_value)]
    order_index = lax.axis_index("dp") % 4
    experts_own = [lax.dynamic_slice_in_dim(w, order_index, 1, 0) for w in (w_gate, w_up, w_down)]
    near = [swap_tensor(w) for w in near_own]
    got = [swap_tensor(after(experts_own[0], near[1]))]

    first, first_t, *tables = prologue(side[None], tokens, gain_one, seg_row, freq)
    saved_a = attend(first, w_query, w_key, w_value, tables, seg_col, seg_row)
    (near, got[0]), (first, saved_a) = lax.optimization_barrier(((near, got[0]), (first, saved_a)))
    far_qkv = [swap_dp(w, 1) for w in near]
    near_out = swap_tensor(after(cut(w_output, core, 0), near[0]))
    got.append(swap_tensor(after(experts_own[1], near[0])))
    across = [swap_dp(got[0], 2)]
    beside = [swap_dp(got[0], 1)]
    saved_b = attend(first, *near, tables, seg_col, seg_row)
    (near_out, got[1], across[0]), (first, saved_b) = lax.optimization_barrier(
        ((near_out, got[1], across[0]), (first, saved_b))
    )
    far_out = swap_dp(near_out, 1)
    got.append(swap_tensor(after(experts_own[2], near_out)))
    across.append(swap_dp(got[1], 2))
    beside.append(swap_dp(got[1], 1))
    corner = [swap_dp(across[0], 1)]
    saved_c = attend(first, *far_qkv, tables, seg_col, seg_row)
    (across[1], got[2]), saved_c = lax.optimization_barrier(((across[1], got[2]), saved_c))
    across.append(swap_dp(got[2], 2))
    beside.append(swap_dp(got[2], 1))
    corner.append(swap_dp(across[1], 1))
    resid, second, gates, places = router(
        side[None], tokens, (saved_a[3], saved_b[3], saved_c[3]), (w_output, near_out, far_out), gain_two, wr_t, routes_t, slots_t
    )
    across[2], second = lax.optimization_barrier((across[2], second))
    corner.append(swap_dp(across[2], 1))
    r_gate, r_up, r_down = (jnp.concatenate(parts, axis=0) for parts in zip(got, beside, across, corner))
    out, low_t, low_grad, resid_grad, small, kept, sent = experts_layer(
        jnp.stack([order_index, side]), second, cotangent, resid, gates, places, gain_two, wr_t,
        (w_gate, r_gate, w_up, r_up, w_down, r_down),
    )

    chains = Chains()
    orders = ([2, 4], [4, 2])

    def piece_swaps(values, count, bit=0):
        size = values.shape[0] // count
        received = []
        for i in range(count):
            (got,) = yield [(values[i * size : (i + 1) * size], bit)]
            received.append(got)
        return received[0] if count == 1 else jnp.concatenate(received, 0)

    chains.add("grads", experts_sum(kept, sent, orders, far))
    chains.add("out", piece_swaps(out, 2))
    zero = jnp.zeros((1,), jnp.int32)
    one_minus = 1 - core[None]
    shared = (tables, seg_col, seg_row)

    low_grad = chains.advance(fence=low_grad)
    back = attend_back(zero, saved_c, *shared, low_grad, far_out)
    back = chains.advance(["grads"], fence=back)
    group_d, partial_sum = project(zero, back, saved_c[3], low_t, first_t, *far_qkv)
    chains.add("other", piece_swaps(group_d, 1, 1))
    low_grad, partial_sum = chains.advance(["other", "out"], fence=(low_grad, partial_sum))
    back = attend_back(zero, saved_b, *shared, low_grad, near_out)
    back = chains.advance(["other"], fence=back)
    group_c, partial_sum = project(zero, back, saved_b[3], low_t, first_t, *near, before=partial_sum)
    chains.add("theirs", piece_swaps(total([group_c, chains.done["other"]]), 1))
    low_grad, partial_sum = chains.advance(["grads", "out", "theirs"], fence=(low_grad, partial_sum))
    back = attend_back(one_minus, saved_a, *shared, low_grad, w_output)
    back = chains.advance(["grads"], fence=back)
    group_b, partial_sum = project(
        one_minus, back, saved_a[3], low_t, first_t, w_query, w_key, w_value, before=partial_sum
    )
    chains.add("mine", piece_swaps(group_b, 1, 1))
    low_grad, partial_sum = chains.advance(["mine"], fence=(low_grad, partial_sum))
    back = attend_back(core[None], saved_a, *shared, low_grad, w_output)
    back = chains.advance(["grads", "mine", "theirs"], fence=back)
    group_a, token, norm_one = project(
        jnp.stack([core, side]), back, saved_a[3], low_t, first_t, w_query, w_key, w_value,
        before=partial_sum, final=(tokens, gain_one, resid_grad),
    )
    chains.add("token", piece_swaps(token, 4))
    chains.add("tail", attention_sum((group_a, chains.done["mine"], chains.done["theirs"]), orders, far))
    chains.add("small", sum_all(jnp.concatenate([small, norm_one], 0)))
    chains.finish()
    done = chains.done

    place_far = place_of(far)
    size_far = 2 ** len(far)
    own_grads, other_grads = done["grads"]
    places = [place_of(order) * size_far + place_far for order in orders]
    grad_gate, grad_up, grad_down = unpack_experts(own_grads, other_grads, places, core, dp_size // 2)
    own_tail, other_tail = done["tail"]
    grad_query, grad_key, grad_value, grad_output = unpack(own_tail, other_tail, places, core, dp_size // 2)
    small = done["small"]
    experts = w_router.shape[1]

    def both(mine, other):
        return jnp.where(side == 0, jnp.concatenate([mine, other], 0), jnp.concatenate([other, mine], 0))

    return (
        both(out, done["out"]),
        both(token, done["token"]).astype(f32),
        grad_query,
        grad_key,
        grad_value,
        grad_output,
        small[experts + 8],
        small[experts],
        small[:experts].T,
        grad_gate,
        grad_up,
        grad_down,
    )


def solution(mesh):
    placed = (
        P("dp", None), P("dp", None), P("dp"), P("dp", None), P("dp", None),
        P(None, "tensor"), P(None, "tensor"), P(None, "tensor"), P("tensor", None),
        P(), P(), P(),
        P(None, None, "tensor"), P(None, None, "tensor"), P(None, "tensor", None),
    )
    return jax.shard_map(
        per_device,
        mesh=mesh,
        in_specs=placed,
        out_specs=(
            P("dp", None), P("dp", None),
            P(None, "tensor"), P(None, "tensor"), P(None, "tensor"), P("tensor", None),
            P(), P(), P(),
            P(None, None, "tensor"), P(None, None, "tensor"), P(None, "tensor", None),
        ),
        check_vma=False,
    )
```

```python
from functools import partial

import jax
import jax.numpy as jnp
from jax import lax
from jax.experimental import pallas as pl
from jax.experimental.pallas import tpu as pltpu
from jax.sharding import PartitionSpec as P

HEAD_DIM = 64
SEQ_LEN = 1024
CAP = 256
EPS = 1e-06
THETA = 10000.0
NEG = -1e30
BLOCK = 256
LANES = 128
GROUP = 4 * HEAD_DIM

f32 = jnp.float32
bf16 = jnp.bfloat16


def nn(left, right):
    return lax.dot_general(left, right, (((1,), (0,)), ((), ())), preferred_element_type=f32)


def nt(left, right):
    return lax.dot_general(left, right, (((1,), (1,)), ((), ())), preferred_element_type=f32)


def tn(left, right):
    return lax.dot_general(left, right, (((0,), (0,)), ((), ())), preferred_element_type=f32)


def params(count=1):
    return pltpu.CompilerParams(
        dimension_semantics=("arbitrary",) * count if count else None,
        vmem_limit_bytes=60 * 1024 * 1024,
    )


def cost(micros):
    return pl.CostEstimate(flops=int(micros * 1.1e9), bytes_accessed=1 << 20, transcendentals=0)


def whole(shape):
    return pl.BlockSpec(shape, lambda *_: (0,) * len(shape))


def once(shape):
    return pl.BlockSpec(shape, lambda *_: (0,) * len(shape), pipeline_mode=pl.Buffered(1))


def lane_iota(rows, lanes=LANES):
    return lax.broadcasted_iota(jnp.int32, (rows, lanes), 1)


def prologue_kernel(side_ref, x_ref, gain_ref, seg_ref, freq_ref, first_ref, first_t_ref, cos_ref, up_ref, down_ref):
    rows = x_ref.shape[0]
    values = x_ref[...].astype(f32)
    scale = lax.rsqrt(jnp.mean(values * values, axis=-1, keepdims=True) + EPS)
    normed = values * scale * gain_ref[...].astype(f32)
    first_ref[...] = normed.astype(bf16)
    first_t_ref[...] = normed.astype(bf16).T
    seg = seg_ref[...]
    zeros = jnp.sum((seg == 0).astype(f32), axis=1, keepdims=True)
    ones = jnp.sum((seg == 1).astype(f32), axis=1, keepdims=True)
    places = lax.broadcasted_iota(jnp.int32, (1, rows), 1).astype(f32)
    places = places - jnp.where(seg >= 1, zeros, 0.0) - jnp.where(seg >= 2, ones, 0.0)
    angles = freq_ref[:, 0:1] * places
    cosine = jnp.cos(angles)
    sine = jnp.sin(angles)
    cosine = jnp.concatenate([cosine] * 4, axis=0).T
    sine = jnp.concatenate([sine] * 4, axis=0).T
    lower = (lane_iota(rows) % HEAD_DIM) < HEAD_DIM // 2
    cos_ref[...] = cosine
    up_ref[...] = jnp.where(lower, -sine, 0.0)
    down_ref[...] = jnp.where(lower, 0.0, sine)


def own_rows(shape):
    return pl.BlockSpec(shape, lambda i, s: (s[0], 0), pipeline_mode=pl.Buffered(1))


def prologue(side, tokens, gain, seg_row, freq):
    rows, width = seg_row.shape[1], tokens.shape[1]
    table = jax.ShapeDtypeStruct((rows, LANES), f32)
    shapes = (
        jax.ShapeDtypeStruct((rows, width), bf16),
        jax.ShapeDtypeStruct((width, rows), bf16),
        table,
        table,
        table,
    )
    return pl.pallas_call(
        prologue_kernel,
        grid_spec=pltpu.PrefetchScalarGridSpec(
            num_scalar_prefetch=1,
            grid=(1,),
            in_specs=[own_rows((rows, width)), once(gain.shape), once(seg_row.shape), once(freq.shape)],
            out_specs=[whole(o.shape) for o in shapes],
        ),
        out_shape=shapes,
        compiler_params=params(),
        cost_estimate=cost(5),
        name="prologue",
    )(side, tokens, gain, seg_row, freq)


def rotate(values, cosine, up, down):
    return (
        values * cosine
        + pltpu.roll(values, LANES - 32, 1) * up
        + pltpu.roll(values, 32, 1) * down
    )


def rotate_back(values, cosine, up, down):
    return (
        values * cosine
        - pltpu.roll(values, LANES - 32, 1) * up
        - pltpu.roll(values, 32, 1) * down
    )


def doubled(values):
    turned = pltpu.roll(values, HEAD_DIM, 1)
    left = lane_iota(values.shape[0]) < HEAD_DIM
    return (
        jnp.where(left, values, turned).astype(bf16),
        jnp.where(left, turned, values).astype(bf16),
    )


def halves_mask():
    left = (lane_iota(1) < HEAD_DIM).astype(f32)
    return left.astype(bf16), (1.0 - left).astype(bf16)


def attend_kernel(
    first_ref, wq_ref, wk_ref, wv_ref, cos_ref, up_ref, down_ref, segc_ref, segr_ref,
    q_ref, k_ref, v_ref, att_ref, lse_ref, bias_ref,
):
    rows = first_ref.shape[0]

    @pl.when(pl.program_id(0) == 0)
    def _():
        for start in range(0, rows, BLOCK):
            at_row = lax.broadcasted_iota(jnp.int32, (BLOCK, rows), 0) + start
            at_col = lax.broadcasted_iota(jnp.int32, (BLOCK, rows), 1)
            allowed = (at_col <= at_row) & (segc_ref[start : start + BLOCK, :] == segr_ref[...])
            bias_ref[start : start + BLOCK, :] = jnp.where(allowed, 0.0, NEG)

    first = first_ref[...]
    cosine, up, down = cos_ref[...], up_ref[...], down_ref[...]
    for tile in range(2):
        part = slice(tile * LANES, (tile + 1) * LANES)
        raw = nn(first, wq_ref[:, part])
        q_ref[:, part] = (rotate(raw, cosine, up, down) * HEAD_DIM**-0.5).astype(bf16)
    key = rotate(nn(first, wk_ref[...]), cosine, up, down)
    value = nn(first, wv_ref[...])
    k_ref[...] = key.astype(bf16)
    v_ref[...] = value.astype(bf16)
    keys, values = doubled(key), doubled(value)
    low, high = halves_mask()
    for start in range(0, rows, BLOCK):
        width = start + BLOCK
        mine = slice(start, width)
        bias = bias_ref[mine, :width]
        bias = jnp.concatenate([bias, bias], axis=0)
        logs = jnp.zeros((BLOCK, LANES), f32)
        lanes = lane_iota(BLOCK)
        for kv in range(2):
            part = slice(kv * LANES, (kv + 1) * LANES)
            query = q_ref[mine, part]
            query = jnp.concatenate([query * low, query * high], axis=0)
            scores = nt(query, keys[kv][:width]) + bias
            row_max = jnp.max(scores, axis=-1, keepdims=True)
            weights = jnp.exp(scores - row_max)
            total = jnp.sum(weights, axis=-1, keepdims=True)
            probs = (weights * (1.0 / total)).astype(bf16)
            out = nn(probs, values[kv][:width])
            att_ref[mine, part] = jnp.where(lanes < HEAD_DIM, out[:BLOCK], out[BLOCK:]).astype(bf16)
            log_total = row_max + jnp.log(total)
            logs = jnp.where(lanes == 2 * kv, log_total[:BLOCK], logs)
            logs = jnp.where(lanes == 2 * kv + 1, log_total[BLOCK:], logs)
        lse_ref[0, :, mine] = logs.T[:8]


def attend(first, wq, wk, wv, tables, seg_col, seg_row):
    rows, width = first.shape
    groups = wq.shape[1] // GROUP
    table = whole((rows, LANES))
    return pl.pallas_call(
        attend_kernel,
        grid=(groups,),
        in_specs=[
            whole((rows, width)),
            pl.BlockSpec((width, GROUP), lambda g: (0, g)),
            pl.BlockSpec((width, LANES), lambda g: (0, g)),
            pl.BlockSpec((width, LANES), lambda g: (0, g)),
            table,
            table,
            table,
            whole((rows, 1)),
            whole((1, rows)),
        ],
        out_specs=[
            pl.BlockSpec((rows, GROUP), lambda g: (0, g)),
            pl.BlockSpec((rows, LANES), lambda g: (0, g)),
            pl.BlockSpec((rows, LANES), lambda g: (0, g)),
            pl.BlockSpec((rows, GROUP), lambda g: (0, g)),
            pl.BlockSpec((1, 8, rows), lambda g: (g, 0, 0)),
        ],
        out_shape=(
            jax.ShapeDtypeStruct((rows, groups * GROUP), bf16),
            jax.ShapeDtypeStruct((rows, groups * LANES), bf16),
            jax.ShapeDtypeStruct((rows, groups * LANES), bf16),
            jax.ShapeDtypeStruct((rows, groups * GROUP), bf16),
            jax.ShapeDtypeStruct((groups, 8, rows), f32),
        ),
        scratch_shapes=[pltpu.VMEM((rows, rows), f32)],
        compiler_params=params(),
        cost_estimate=cost(10 * groups),
        name="attend",
    )(first, wq, wk, wv, *tables, seg_col, seg_row)


def router_kernel(
    side_ref, x_ref, att_a_ref, att_b_ref, att_c_ref, wo_a_ref, wo_b_ref, wo_c_ref, gain_ref, wr_ref, routes_ref, slots_ref,
    resid_ref, second_ref, gates_ref, places_ref,
):
    mixed = nn(att_a_ref[...], wo_a_ref[...])
    mixed = mixed + nn(att_b_ref[...], wo_b_ref[...])
    mixed = mixed + nn(att_c_ref[...], wo_c_ref[...])
    resid = x_ref[...].astype(f32) + mixed
    resid_ref[...] = resid
    scale = lax.rsqrt(jnp.mean(resid * resid, axis=-1, keepdims=True) + EPS)
    second = (resid * scale * gain_ref[...].astype(f32)).astype(bf16)
    second_ref[...] = second
    logits = nt(wr_ref[...], second)
    experts, rows = logits.shape
    routes, slots = routes_ref[...], slots_ref[...]
    number = lax.broadcasted_iota(jnp.int32, (experts, rows), 0)
    chosen = jnp.zeros((experts, rows), f32)
    place = jnp.zeros((8, rows), jnp.int32)
    taken = jnp.zeros((8, rows), jnp.int32)
    for k in range(routes.shape[0]):
        hit = number == routes[k : k + 1, :]
        chosen = jnp.where(hit, 1.0, chosen)
        hit = number[:8] == routes[k : k + 1, :]
        place = jnp.where(hit, slots[k : k + 1, :], place)
        taken = jnp.where(hit, 1, taken)
    places_ref[...] = jnp.where(taken > 0, place, CAP)
    top = jnp.max(jnp.where(chosen > 0, logits, NEG), axis=0, keepdims=True)
    weights = jnp.where(chosen > 0, jnp.exp(logits - top), 0.0)
    gates_ref[...] = weights / jnp.sum(weights, axis=0, keepdims=True)


def router(side, tokens, attended, outputs, gain, wr_t, routes_t, slots_t):
    rows, width = routes_t.shape[1], tokens.shape[1]
    rest = (*attended, *outputs, gain, wr_t, routes_t, slots_t)
    shapes = (
        jax.ShapeDtypeStruct((rows, width), f32),
        jax.ShapeDtypeStruct((rows, width), bf16),
        jax.ShapeDtypeStruct((wr_t.shape[0], rows), f32),
        jax.ShapeDtypeStruct((8, rows), jnp.int32),
    )
    return pl.pallas_call(
        router_kernel,
        grid_spec=pltpu.PrefetchScalarGridSpec(
            num_scalar_prefetch=1,
            grid=(1,),
            in_specs=[own_rows((rows, width)), *[once(a.shape) for a in rest]],
            out_specs=[whole(o.shape) for o in shapes],
        ),
        out_shape=shapes,
        compiler_params=params(),
        cost_estimate=cost(8),
        name="router",
    )(side, tokens, *rest)


def split_three(values):
    first = values.astype(bf16)
    rest = values - first.astype(f32)
    second = rest.astype(bf16)
    return first, second, (rest - second.astype(f32)).astype(bf16)


def experts_kernel(
    order_ref, second_ref, cot_ref, resid_ref, gates_ref, places_ref, gain_ref, wr_ref,
    wg_a_ref, wg_b_ref, wu_a_ref, wu_b_ref, wd_a_ref, wd_b_ref,
    out_ref, low_t_ref, low_ref, grad_ref, small_ref, kept_ref, sent_ref,
    moe_ref, slot_grads_ref,
):
    step = pl.program_id(0)
    e = step ^ order_ref[0]
    rows = second_ref.shape[0]
    second = second_ref[...]
    slots = lax.broadcasted_iota(jnp.int32, (CAP, rows), 0)
    hit = slots == places_ref[pl.ds(e, 1), :]
    gate_slot = jnp.sum(jnp.where(hit, gates_ref[pl.ds(e, 1), :], 0.0), axis=1, keepdims=True)
    onehot = jnp.where(hit, 1.0, 0.0).astype(bf16)
    expert_in = nn(onehot, second).astype(bf16)
    slot_grad = nn(onehot, cot_ref[...])
    out_grad = (gate_slot * slot_grad).astype(bf16)
    expert_out = None
    back = None
    factors = []
    for wg_ref, wu_ref, wd_ref in ((wg_a_ref, wu_a_ref, wd_a_ref), (wg_b_ref, wu_b_ref, wd_b_ref)):
        wg, wu, wd = wg_ref[0], wu_ref[0], wd_ref[0]
        gate_pre = nn(expert_in, wg)
        up_pre = nn(expert_in, wu)
        sig = 1.0 / (1.0 + jnp.exp(-gate_pre))
        silu = gate_pre * sig
        hidden = (silu * up_pre).astype(bf16)
        part = nn(hidden, wd)
        expert_out = part if expert_out is None else expert_out + part
        hidden_grad = nt(out_grad, wd)
        gate_low = (hidden_grad * up_pre * sig * (1.0 + gate_pre * (1.0 - sig))).astype(bf16)
        up_low = (hidden_grad * silu).astype(bf16)
        factors.append((gate_low, up_low, hidden))
        part = nt(gate_low, wg) + nt(up_low, wu)
        back = part if back is None else back + part

    def weight_grads(ref):
        size = hidden.shape[1]
        for half, (gate_low, up_low, mixed) in enumerate(factors):
            ref[0, half, :size, :] = tn(gate_low, expert_in).astype(bf16)
            ref[0, half, size : 2 * size, :] = tn(up_low, expert_in).astype(bf16)
            ref[0, half, 2 * size :, :] = tn(mixed, out_grad).astype(bf16)

    @pl.when(step % 2 == 0)
    def _():
        weight_grads(kept_ref)

    @pl.when(step % 2 == 1)
    def _():
        weight_grads(sent_ref)

    slot_gate = jnp.sum(expert_out * slot_grad, axis=1, keepdims=True)
    gate_row = jnp.sum(jnp.where(hit, slot_gate, 0.0), axis=0, keepdims=True)
    moe = tn(onehot, (gate_slot * expert_out).astype(bf16))
    second_back = tn(onehot, back.astype(bf16))

    @pl.when(step == 0)
    def _():
        moe_ref[...] = moe
        grad_ref[...] = second_back
        slot_grads_ref[...] = jnp.zeros_like(slot_grads_ref)

    @pl.when(step > 0)
    def _():
        moe_ref[...] += moe
        grad_ref[...] += second_back

    slot_grads_ref[pl.ds(e, 1), :] = gate_row

    @pl.when(step == pl.num_programs(0) - 1)
    def _():
        gates = gates_ref[...]
        resid = resid_ref[...]
        out_ref[...] = (resid + moe_ref[...]).astype(bf16)
        gate_grad = slot_grads_ref[...]
        logit_grad = gates * (gate_grad - jnp.sum(gates * gate_grad, axis=0, keepdims=True))
        router_grad = None
        second_grad = grad_ref[...]
        for piece in split_three(logit_grad):
            part = nn(piece, second)
            router_grad = part if router_grad is None else router_grad + part
            second_grad = second_grad + tn(piece, wr_ref[...])
        experts = gates.shape[0]
        small_ref[0:experts, :] = router_grad
        gain = gain_ref[...].astype(f32)
        scale = lax.rsqrt(jnp.mean(resid * resid, axis=-1, keepdims=True) + EPS)
        norm_grad = jnp.sum(second_grad * resid * scale, axis=0, keepdims=True)
        small_ref[experts : experts + 8, :] = jnp.where(
            lax.broadcasted_iota(jnp.int32, (8, resid.shape[1]), 0) == 0, norm_grad, 0.0
        )
        inner = jnp.mean(gain * second_grad * resid, axis=-1, keepdims=True)
        grad = scale * gain * second_grad - resid * (scale * scale * scale) * inner
        grad = grad + cot_ref[...].astype(f32)
        grad_ref[...] = grad
        low_ref[...] = grad.astype(bf16)
        low_t_ref[...] = grad.astype(bf16).T


def experts_layer(order, second, cot, resid, gates, places, gain, wr_t, weights):
    rows, width = second.shape
    own_cot = pl.BlockSpec((rows, width), lambda i, o: (o[1], 0), pipeline_mode=pl.Buffered(1))
    experts = gates.shape[0]
    window, _, hidden = weights[0].shape
    wide = pl.BlockSpec((1, width, hidden), lambda i, o: (i ^ o[0], 0, 0))
    tall = pl.BlockSpec((1, hidden, width), lambda i, o: (i ^ o[0], 0, 0))
    wide_rel = pl.BlockSpec((1, width, hidden), lambda i, o: (i, 0, 0))
    tall_rel = pl.BlockSpec((1, hidden, width), lambda i, o: (i, 0, 0))
    grads_out = jax.ShapeDtypeStruct((window // 2, 2, 3 * hidden, width), bf16)
    grads = pl.BlockSpec((1, 2, 3 * hidden, width), lambda i, o: ((i // 2) ^ (o[0] // 2), 0, 0, 0))
    return pl.pallas_call(
        experts_kernel,
        grid_spec=pltpu.PrefetchScalarGridSpec(
        num_scalar_prefetch=1,
        grid=(window,),
        in_specs=[
            once((rows, width)),
            own_cot,
            once((rows, width)),
            whole((experts, rows)),
            whole((8, rows)),
            whole((1, width)),
            whole((experts, width)),
            wide,
            wide_rel,
            wide,
            wide_rel,
            tall,
            tall_rel,
        ],
        out_specs=[
            once((rows, width)),
            once((width, rows)),
            once((rows, width)),
            once((rows, width)),
            whole((experts + 8, width)),
            grads,
            grads,
        ],
        scratch_shapes=[
            pltpu.VMEM((rows, width), f32),
            pltpu.VMEM((experts, rows), f32),
        ],
        ),
        out_shape=(
            jax.ShapeDtypeStruct((rows, width), bf16),
            jax.ShapeDtypeStruct((width, rows), bf16),
            jax.ShapeDtypeStruct((rows, width), bf16),
            jax.ShapeDtypeStruct((rows, width), f32),
            jax.ShapeDtypeStruct((experts + 8, width), f32),
            grads_out,
            grads_out,
        ),
        compiler_params=params(),
        cost_estimate=cost(39),
        name="experts",
    )(order, second, cot, resid, gates, places, gain, wr_t, *weights)


def attend_back_kernel(
    sel_ref, q_ref, k_ref, v_ref, lse_ref, cos_ref, up_ref, down_ref, segc_ref, segr_ref, low_ref, wo_ref,
    back_ref, bias_ref, dq_ref, dk_ref, dv_ref,
):
    rows = q_ref.shape[0]
    for start in range(0, rows, BLOCK):
        at_key = lax.broadcasted_iota(jnp.int32, (BLOCK, rows), 0) + start
        at_query = lax.broadcasted_iota(jnp.int32, (BLOCK, rows), 1)
        allowed = (at_key <= at_query) & (segc_ref[start : start + BLOCK, :] == segr_ref[...])
        bias_ref[start : start + BLOCK, :] = jnp.where(allowed, 0.0, NEG)
    upward = nt(low_ref[...], wo_ref[...]).astype(bf16)
    keys = doubled(k_ref[...].astype(f32))
    values = doubled(v_ref[...].astype(f32))
    low, high = halves_mask()
    dk_ref[...] = jnp.zeros_like(dk_ref)
    dv_ref[...] = jnp.zeros_like(dv_ref)
    lanes = lane_iota(BLOCK)
    for start in range(0, rows, BLOCK):
        width = start + BLOCK
        mine = slice(start, width)
        bias = bias_ref[:width, mine]
        bias = jnp.concatenate([bias, bias], axis=1)
        for kv in range(2):
            part = slice(kv * LANES, (kv + 1) * LANES)
            query = q_ref[mine, part]
            query = jnp.concatenate([query * low, query * high], axis=0)
            upper = upward[mine, part]
            upper = jnp.concatenate([upper * low, upper * high], axis=0)
            logs = jnp.concatenate(
                [lse_ref[0, 2 * kv : 2 * kv + 1, mine], lse_ref[0, 2 * kv + 1 : 2 * kv + 2, mine]], axis=1
            )
            key = keys[kv][:width]
            probs = jnp.exp(nt(key, query) + bias - logs)
            prob_grad = nt(values[kv][:width], upper)
            product = probs * prob_grad
            delta = jnp.sum(product, axis=0, keepdims=True)
            raw = (product - probs * delta).astype(bf16)
            dv_ref[kv, :width, :] += nn(probs.astype(bf16), upper)
            dk_ref[kv, :width, :] += nn(raw, query)
            back = tn(raw, key)
            dq_ref[mine, part] = jnp.where(lanes < HEAD_DIM, back[:BLOCK], back[BLOCK:])
    cosine, up, down = cos_ref[...], up_ref[...], down_ref[...]
    left = lane_iota(rows) < HEAD_DIM

    def both(ref):
        one, two = ref[0], ref[1]
        one = one + pltpu.roll(one, HEAD_DIM, 1)
        two = two + pltpu.roll(two, HEAD_DIM, 1)
        return jnp.where(left, one, two)

    back_ref[:, 2 * LANES : 3 * LANES] = rotate_back(both(dk_ref), cosine, up, down).astype(bf16)
    back_ref[:, 3 * LANES :] = both(dv_ref).astype(bf16)
    for kv in range(2):
        part = slice(kv * LANES, (kv + 1) * LANES)
        turned = rotate_back(dq_ref[:, part], cosine, up, down)
        back_ref[:, part] = (turned * HEAD_DIM**-0.5).astype(bf16)


def attend_back(sel, saved, tables, seg_col, seg_row, low_grad, wo):
    query, key, value, _, logs = saved
    rows, width = low_grad.shape

    def fixed(shape):
        return pl.BlockSpec(shape, lambda i, s: (0,) * len(shape))

    table = fixed((rows, LANES))
    wide = pl.BlockSpec((rows, GROUP), lambda i, s: (0, s[0]))
    thin = pl.BlockSpec((rows, LANES), lambda i, s: (0, s[0]))
    return pl.pallas_call(
        attend_back_kernel,
        grid_spec=pltpu.PrefetchScalarGridSpec(
            num_scalar_prefetch=1,
            grid=(1,),
            in_specs=[
                wide, thin, thin, pl.BlockSpec((1, 8, rows), lambda i, s: (s[0], 0, 0)),
                table, table, table, fixed((rows, 1)), fixed((1, rows)),
                fixed((rows, width)), pl.BlockSpec((GROUP, width), lambda i, s: (s[0], 0)),
            ],
            out_specs=fixed((rows, 2 * GROUP)),
            scratch_shapes=[
                pltpu.VMEM((rows, rows), f32),
                pltpu.VMEM((rows, GROUP), f32),
                pltpu.VMEM((2, rows, LANES), f32),
                pltpu.VMEM((2, rows, LANES), f32),
            ],
        ),
        out_shape=jax.ShapeDtypeStruct((rows, 2 * GROUP), bf16),
        compiler_params=params(),
        cost_estimate=cost(14),
        name="attend_back",
    )(sel, query, key, value, logs, *tables, seg_col, seg_row, low_grad, wo)


def project_kernel(
    final, fresh, sel_ref, back_ref, att_ref, low_t_ref, first_t_ref, wq_ref, wk_ref, wv_ref, *rest
):
    if not fresh:
        before_ref, *rest = rest
    if final:
        x_ref, gain_ref, grad_ref, group_ref, token_ref, norm_ref = rest
    else:
        group_ref, sum_ref = rest
    step = pl.program_id(0)
    block = first_t_ref.shape[0]
    group_ref[:, : 2 * GROUP] = nn(first_t_ref[...], back_ref[...]).astype(bf16)
    group_ref[:, 2 * GROUP :] = nn(low_t_ref[...], att_ref[...]).astype(bf16)
    back = back_ref[pl.ds(pl.multiple_of(step * block, block), block), :]
    first_grad = nt(back[:, :GROUP], wq_ref[...])
    first_grad = first_grad + nt(back[:, GROUP : GROUP + LANES], wk_ref[...])
    first_grad = first_grad + nt(back[:, GROUP + LANES :], wv_ref[...])
    if not fresh:
        first_grad = before_ref[...] + first_grad
    if final:
        inputs = x_ref[...].astype(f32)
        gain = gain_ref[...].astype(f32)
        scale = lax.rsqrt(jnp.mean(inputs * inputs, axis=-1, keepdims=True) + EPS)
        norm = jnp.broadcast_to(jnp.sum(first_grad * inputs * scale, axis=0, keepdims=True), norm_ref.shape)

        @pl.when(step == 0)
        def _():
            norm_ref[...] = norm

        @pl.when(step > 0)
        def _():
            norm_ref[...] += norm

        inner = jnp.mean(gain * first_grad * inputs, axis=-1, keepdims=True)
        grad = scale * gain * first_grad - inputs * (scale * scale * scale) * inner
        token_ref[...] = (grad + grad_ref[...]).astype(bf16)
    else:
        sum_ref[...] = first_grad


def project(sel, back, att, low_t, first_t, wq, wk, wv, before=None, final=None):
    width, rows = low_t.shape
    steps = 4
    block = rows // steps
    assert rows == width

    def fixed(shape):
        return pl.BlockSpec(shape, lambda i, s: (0,) * len(shape))

    wide_w = pl.BlockSpec((width, GROUP), lambda i, s: (0, s[0]))
    thin_w = pl.BlockSpec((width, LANES), lambda i, s: (0, s[0]))
    strip = pl.BlockSpec((block, width), lambda i, s: (i, 0))
    in_specs = [
        fixed((rows, 2 * GROUP)), pl.BlockSpec((rows, GROUP), lambda i, s: (0, s[0])),
        strip, strip, wide_w, thin_w, thin_w,
    ]
    out_specs = [pl.BlockSpec((block, 3 * GROUP), lambda i, s: (i, 0))]
    out_shape = [jax.ShapeDtypeStruct((width, 3 * GROUP), bf16)]
    extra = ()
    if before is not None:
        in_specs.append(strip)
        extra = (before,)
    if final is None:
        out_specs.append(strip)
        out_shape.append(jax.ShapeDtypeStruct((rows, width), f32))
    else:
        extra = (*extra, *final)
        in_specs += [pl.BlockSpec((block, width), lambda i, s: (s[1] * steps + i, 0)), fixed((1, width)), strip]
        out_specs += [strip, fixed((8, width))]
        out_shape += [
            jax.ShapeDtypeStruct((rows, width), bf16),
            jax.ShapeDtypeStruct((8, width), f32),
        ]
    return pl.pallas_call(
        partial(project_kernel, final is not None, before is None),
        grid_spec=pltpu.PrefetchScalarGridSpec(
            num_scalar_prefetch=1, grid=(steps,), in_specs=in_specs, out_specs=out_specs
        ),
        out_shape=tuple(out_shape),
        compiler_params=params(),
        cost_estimate=cost(7),
        name="project_final" if final is not None else "project",
    )(sel, back, att, low_t, first_t, wq, wk, wv, *extra)


def plain_order(piece, place, count):
    shape = piece.shape
    bit = 1
    while bit < count:
        pairs = piece.reshape(-1, 2, bit * shape[0] // count, shape[1])
        flipped = jnp.concatenate([pairs[:, 1:], pairs[:, :1]], axis=1)
        piece = jnp.where((place // bit) % 2 == 1, flipped, pairs)
        bit *= 2
    return piece.reshape(shape)


def add_split(colors, sides):
    rows = [terms[0][0].shape[1] for terms in colors]
    half = rows[0] // 2
    if half % 16:
        out = []
        for terms, side in zip(colors, sides):
            cutouts = [lax.slice_in_dim(t, i * n, (i + 1) * n, axis=0) for t, n, i in terms]
            both = []
            for at in (side, 1 - side):
                pieces = [lax.dynamic_slice_in_dim(t, at * half, half, 1).astype(f32) for t in cutouts]
                both.append(sum(pieces[1:], pieces[0]).astype(bf16))
            out.append(tuple(both))
        return out
    steps = 4 if half % 64 == 0 else (2 if half % 32 == 0 else 1)
    block = half // steps
    in_specs, operands, out_specs, shapes, counts = [], [], [], [], []
    for number, terms in enumerate(colors):
        counts.append(len(terms))
        for other in (0, 1):
            for array, lead, index in terms:

                def place(j, s, number=number, index=index, other=other):
                    return (index, (s[number] ^ other) * steps + j, 0)

                in_specs.append(pl.BlockSpec((lead, block, array.shape[2]), place))
                operands.append(array)
        array, lead, _ = terms[0]
        for _ in range(2):
            out_specs.append(pl.BlockSpec((lead, block, array.shape[2]), lambda j, s: (0, j, 0)))
            shapes.append(jax.ShapeDtypeStruct((lead, half, array.shape[2]), bf16))

    def kernel(side_ref, *refs):
        ins, outs = refs[: len(operands)], refs[len(operands) :]
        at = 0
        for number, count in enumerate(counts):
            for other in range(2):
                value = ins[at][...].astype(f32)
                for term in range(1, count):
                    value = value + ins[at + term][...].astype(f32)
                outs[2 * number + other][...] = value.astype(bf16)
                at += count

    out = pl.pallas_call(
        kernel,
        grid_spec=pltpu.PrefetchScalarGridSpec(
            num_scalar_prefetch=1, grid=(steps,), in_specs=in_specs, out_specs=out_specs
        ),
        out_shape=tuple(shapes),
        compiler_params=params(),
        cost_estimate=cost(4),
        name="add_split",
    )(jnp.stack(sides), *operands)
    return [(out[2 * i], out[2 * i + 1]) for i in range(len(colors))]


def add_halves(colors):
    count = len(colors)
    _, rows, columns = colors[0][0].shape

    def kernel(*refs):
        ins, (mine_ref, theirs_ref) = refs[:-2], refs[-2:]
        for i in range(count):
            value = (ins[2 * i][...].astype(f32) + ins[2 * i + 1][...].astype(f32)).astype(bf16)
            mine_ref[i] = value[0]
            theirs_ref[i] = value[1]

    shape = jax.ShapeDtypeStruct((count, rows, columns), bf16)
    return pl.pallas_call(
        kernel,
        out_shape=(shape, shape),
        compiler_params=params(0),
        cost_estimate=cost(3),
        name="add_halves",
    )(*[a for pair in colors for a in pair])


def straighten(pieces, places, count):
    if (pieces[0].shape[0] // count) % 16:
        return [plain_order(p, at, count) for p, at in zip(pieces, places)], [jnp.int32(0)] * len(places), 1
    return pieces, places, count


def unpack_experts(own, other, places, core, count):
    pairs = len(own)
    flat, places, count = straighten([*own, *other], [*places, *places], count)
    rows, width = flat[0].shape
    block, hidden = rows // count, rows // 3

    def kernel(place_ref, *refs):
        ins, (gate_ref, up_ref, down_ref, plain_ref) = refs[: 2 * pairs], refs[2 * pairs :]
        e = pl.program_id(0)
        for pair in range(pairs):
            for far in range(2):
                ref = ins[far * pairs + pair]

                @pl.when(e == 2 * pair + (place_ref[pairs] ^ far))
                def _(ref=ref, pair=pair):
                    for i in range(count):
                        start = pl.multiple_of((i ^ place_ref[pair]) * block, block)
                        plain_ref[i * block : (i + 1) * block, :] = ref[pl.ds(start, block), :].astype(f32)

        gate_ref[0] = plain_ref[:hidden, :].T
        up_ref[0] = plain_ref[hidden : 2 * hidden, :].T
        down_ref[0] = plain_ref[2 * hidden :, :]

    wide = jax.ShapeDtypeStruct((2 * pairs, width, hidden), f32)
    tall = jax.ShapeDtypeStruct((2 * pairs, hidden, width), f32)
    return pl.pallas_call(
        kernel,
        grid_spec=pltpu.PrefetchScalarGridSpec(
            num_scalar_prefetch=1,
            grid=(2 * pairs,),
            in_specs=[pl.BlockSpec((rows, width), lambda e, s: (0, 0))] * (2 * pairs),
            out_specs=[
                pl.BlockSpec((1, width, hidden), lambda e, s: (e, 0, 0)),
                pl.BlockSpec((1, width, hidden), lambda e, s: (e, 0, 0)),
                pl.BlockSpec((1, hidden, width), lambda e, s: (e, 0, 0)),
            ],
            scratch_shapes=[pltpu.VMEM((rows, width), f32)],
        ),
        out_shape=(wide, wide, tall),
        compiler_params=params(),
        cost_estimate=cost(10),
        name="unpack_experts",
    )(jnp.stack([*places[:pairs], core]), *flat)


def unpack(own, other, places, core, count):
    colors = len(own)
    flat, places, count = straighten([*own, *other], [*places, *places], count)
    rows, columns = flat[0].shape
    block = rows // count
    shapes = (
        jax.ShapeDtypeStruct((colors * rows, 2 * GROUP), f32),
        jax.ShapeDtypeStruct((colors * rows, 2 * LANES), f32),
        jax.ShapeDtypeStruct((colors * rows, 2 * LANES), f32),
        jax.ShapeDtypeStruct((2 * GROUP, colors * rows), f32),
    )

    def kernel(place_ref, *refs):
        ins, (query_ref, key_ref, value_ref, output_ref, plain_ref) = refs[: 2 * colors], refs[2 * colors :]
        for group in range(2):
            for color in range(colors):
                for i in range(count):
                    start = pl.multiple_of((i ^ place_ref[color]) * block, block)
                    one = ins[color][pl.ds(start, block), :].astype(f32)
                    two = ins[colors + color][pl.ds(start, block), :].astype(f32)
                    plain_ref[i * block : (i + 1) * block, :] = jnp.where(place_ref[colors] == group, one, two)
                here = slice(color * rows, (color + 1) * rows)
                wide = slice(group * GROUP, (group + 1) * GROUP)
                thin = slice(group * LANES, (group + 1) * LANES)
                query_ref[here, wide] = plain_ref[:, :GROUP]
                key_ref[here, thin] = plain_ref[:, GROUP : GROUP + LANES]
                value_ref[here, thin] = plain_ref[:, GROUP + LANES : 2 * GROUP]
                output_ref[wide, here] = plain_ref[:, 2 * GROUP :].T

    return pl.pallas_call(
        kernel,
        grid_spec=pltpu.PrefetchScalarGridSpec(
            num_scalar_prefetch=1,
            grid=(1,),
            in_specs=[pl.BlockSpec((rows, columns), lambda i, s: (0, 0))] * (2 * colors),
            out_specs=[pl.BlockSpec(o.shape, lambda i, s: (0, 0)) for o in shapes],
            scratch_shapes=[pltpu.VMEM((rows, columns), f32)],
        ),
        out_shape=shapes,
        compiler_params=params(),
        cost_estimate=cost(6),
        name="unpack",
    )(jnp.stack([*places[:colors], core]), *flat)


def swap_tensor(values):
    return lax.ppermute(values, "tensor", [(0, 1), (1, 0)])


def swap_dp(values, bit):
    count = lax.axis_size("dp")
    return lax.ppermute(values, "dp", [(i, i ^ bit) for i in range(count)])


def after(values, earlier):
    return lax.optimization_barrier((values, earlier))[0]


def bit_of(bit):
    return (lax.axis_index("dp") // bit) % 2


def cut(values, index, axis, count=2):
    size = values.shape[axis] // count
    return lax.dynamic_slice_in_dim(values, index * size, size, axis)


def total(terms):
    out = terms[0].astype(f32)
    for term in terms[1:]:
        out = out + term.astype(f32)
    return out.astype(bf16)


def swap(values, bit):
    return swap_tensor(values) if bit == 0 else swap_dp(values, bit)


def place_of(order):
    place = 0
    for bit in order:
        if bit:
            place = 2 * place + bit_of(bit)
    return place


def gather_back(pieces, orders):
    for bits in zip(*(reversed(order) for order in orders)):
        got = yield list(zip(pieces, bits))
        pieces = [jnp.concatenate([p, g], 0) for p, g in zip(pieces, got)]
    got = yield [(p, 1) for p in pieces]
    return pieces, got


def sum_all(values):
    for bit in [0] + [1 << i for i in range(30) if (1 << i) < lax.axis_size("dp")]:
        (got,) = yield [(values, bit)]
        values = values + got
    return values


def experts_sum(kept, sent, orders, far):
    flat = kept.reshape(-1, *kept.shape[2:])
    (got,) = yield [(sent.reshape(flat.shape), 1)]
    colors = [[(flat, 2, i), (got, 2, i)] for i in range(len(orders))]
    for bits in zip(*orders):
        split = add_split(colors, [bit_of(b) for b in bits])
        got = yield [(s, b) for (_, s), b in zip(split, bits)]
        colors = [[(k, 2, 0), (g, 2, 0)] for (k, _), g in zip(split, got)]
    mine, theirs = add_halves([[t for t, _, _ in terms] for terms in colors])
    (got,) = yield [(theirs, 0)]
    count = len(orders)
    for bit in far:
        ((mine, theirs),) = add_split([[(mine, count, 0), (got, count, 0)]], [bit_of(bit)])
        (got,) = yield [(theirs, bit)]
    piece = total([mine, got])
    for bit in reversed(far):
        (got,) = yield [(piece, bit)]
        piece = jnp.concatenate([piece, got], 1)
    return (yield from gather_back([piece[i] for i in range(count)], orders))


def attention_sum(terms, orders, far):
    count = len(orders)
    parts = [t.reshape(count, t.shape[0] // count, t.shape[1]) for t in terms]
    colors = [[(p, 1, i) for p in parts] for i in range(count)]
    for bits in zip(*orders):
        split = add_split(colors, [bit_of(b) for b in bits])
        got = yield [(s, b) for (_, s), b in zip(split, bits)]
        colors = [[(k, 1, 0), (g, 1, 0)] for (k, _), g in zip(split, got)]
    for bit in far:
        split = add_split(colors, [bit_of(bit)] * count)
        (got,) = yield [(jnp.concatenate([s for _, s in split], 0), bit)]
        colors = [[(k, 1, 0), (got, 1, i)] for i, (k, _) in enumerate(split)]
    piece = jnp.concatenate(
        [total([lax.slice_in_dim(t, i, i + n, axis=0) for t, n, i in terms]) for terms in colors], 0
    )
    for bit in reversed(far):
        (got,) = yield [(piece, bit)]
        piece = jnp.concatenate([piece, got], 1)
    return (yield from gather_back([piece[i] for i in range(count)], orders))


class Chains:
    def __init__(self):
        self.live = {}
        self.done = {}

    def advance(self, names=None, fence=None):
        names = [n for n in (names or list(self.live)) if n in self.live]
        requests = {}
        waiting = {n: self.live[n][1] for n in names}
        if fence is not None:
            fence, waiting = lax.optimization_barrier((fence, waiting))
        for n in names:
            chain = self.live[n][0]
            try:
                requests[n] = chain.send(waiting[n])
            except StopIteration as stop:
                self.done[n] = stop.value
                del self.live[n]
        sends = {n: [v for v, _ in r] for n, r in requests.items()}
        if fence is not None:
            fence, sends = lax.optimization_barrier((fence, sends))
        for n, r in requests.items():
            self.live[n] = (self.live[n][0], [swap(v, bit) for v, (_, bit) in zip(sends[n], r)])
        return fence

    def add(self, name, chain):
        self.live[name] = (chain, None)


def per_device(
    tokens, cotangent, segments, routes, slot_index,
    w_query, w_key, w_value, w_output, norm_attn, norm_ffn, w_router, w_gate, w_up, w_down,
):
    length, width = tokens.shape
    side = lax.axis_index("tensor")
    dp_size = lax.axis_size("dp")
    core = lax.axis_index("dp") % 2
    rows = SEQ_LEN
    far = [8 << i for i in range(20) if (8 << i) < dp_size]

    def own(values):
        return lax.dynamic_slice_in_dim(values, side * rows, rows, 0)

    seg = own(segments)
    seg_row, seg_col = seg[None, :], seg[:, None]
    routes_t = own(routes).T
    slots_t = own(slot_index).T
    wr_t = w_router.T
    gain_one, gain_two = norm_attn[None, :], norm_ffn[None, :]
    half_dim = HEAD_DIM // 2
    frequency = THETA ** (-(2.0 * jnp.arange(half_dim, dtype=f32)) / HEAD_DIM)
    freq = jnp.broadcast_to(frequency[:, None], (half_dim, LANES))

    near_own = [cut(w, core, 1) for w in (w_query, w_key, w_value)]
    order_index = lax.axis_index("dp") % 4
    experts_own = [lax.dynamic_slice_in_dim(w, order_index, 1, 0) for w in (w_gate, w_up, w_down)]
    near = [swap_tensor(w) for w in near_own]
    got = [swap_tensor(after(experts_own[0], near[1]))]

    first, first_t, *tables = prologue(side[None], tokens, gain_one, seg_row, freq)
    saved_a = attend(first, w_query, w_key, w_value, tables, seg_col, seg_row)
    (near, got[0]), (first, saved_a) = lax.optimization_barrier(((near, got[0]), (first, saved_a)))
    far_qkv = [swap_dp(w, 1) for w in near]
    near_out = swap_tensor(after(cut(w_output, core, 0), near[0]))
    got.append(swap_tensor(after(experts_own[1], near[0])))
    across = [swap_dp(got[0], 2)]
    beside = [swap_dp(got[0], 1)]
    saved_b = attend(first, *near, tables, seg_col, seg_row)
    (near_out, got[1], across[0]), (first, saved_b) = lax.optimization_barrier(
        ((near_out, got[1], across[0]), (first, saved_b))
    )
    far_out = swap_dp(near_out, 1)
    got.append(swap_tensor(after(experts_own[2], near_out)))
    across.append(swap_dp(got[1], 2))
    beside.append(swap_dp(got[1], 1))
    corner = [swap_dp(across[0], 1)]
    saved_c = attend(first, *far_qkv, tables, seg_col, seg_row)
    (across[1], got[2]), saved_c = lax.optimization_barrier(((across[1], got[2]), saved_c))
    across.append(swap_dp(got[2], 2))
    beside.append(swap_dp(got[2], 1))
    corner.append(swap_dp(across[1], 1))
    resid, second, gates, places = router(
        side[None], tokens, (saved_a[3], saved_b[3], saved_c[3]), (w_output, near_out, far_out), gain_two, wr_t, routes_t, slots_t
    )
    across[2], second = lax.optimization_barrier((across[2], second))
    corner.append(swap_dp(across[2], 1))
    r_gate, r_up, r_down = (jnp.concatenate(parts, axis=0) for parts in zip(got, beside, across, corner))
    out, low_t, low_grad, resid_grad, small, kept, sent = experts_layer(
        jnp.stack([order_index, side]), second, cotangent, resid, gates, places, gain_two, wr_t,
        (w_gate, r_gate, w_up, r_up, w_down, r_down),
    )

    chains = Chains()
    orders = ([2, 4], [4, 2])

    def piece_swaps(values, count, bit=0):
        size = values.shape[0] // count
        received = []
        for i in range(count):
            (got,) = yield [(values[i * size : (i + 1) * size], bit)]
            received.append(got)
        return received[0] if count == 1 else jnp.concatenate(received, 0)

    chains.add("grads", experts_sum(kept, sent, orders, far))
    chains.add("out", piece_swaps(out, 2))
    zero = jnp.zeros((1,), jnp.int32)
    one_minus = 1 - core[None]
    shared = (tables, seg_col, seg_row)

    low_grad = chains.advance(fence=low_grad)
    back = attend_back(zero, saved_c, *shared, low_grad, far_out)
    back = chains.advance(["grads"], fence=back)
    group_d, partial_sum = project(zero, back, saved_c[3], low_t, first_t, *far_qkv)
    chains.add("other", piece_swaps(group_d, 1, 1))
    low_grad, partial_sum = chains.advance(["other", "out"], fence=(low_grad, partial_sum))
    back = attend_back(zero, saved_b, *shared, low_grad, near_out)
    back = chains.advance(["other"], fence=back)
    group_c, partial_sum = project(zero, back, saved_b[3], low_t, first_t, *near, before=partial_sum)
    chains.add("theirs", piece_swaps(total([group_c, chains.done["other"]]), 1))
    low_grad, partial_sum = chains.advance(["grads", "out", "theirs"], fence=(low_grad, partial_sum))
    back = attend_back(one_minus, saved_a, *shared, low_grad, w_output)
    back = chains.advance(["grads"], fence=back)
    group_b, partial_sum = project(
        one_minus, back, saved_a[3], low_t, first_t, w_query, w_key, w_value, before=partial_sum
    )
    chains.add("mine", piece_swaps(group_b, 1, 1))
    low_grad, partial_sum = chains.advance(["mine"], fence=(low_grad, partial_sum))
    back = attend_back(core[None], saved_a, *shared, low_grad, w_output)
    back = chains.advance(["grads", "mine", "theirs"], fence=back)
    group_a, token, norm_one = project(
        jnp.stack([core, side]), back, saved_a[3], low_t, first_t, w_query, w_key, w_value,
        before=partial_sum, final=(tokens, gain_one, resid_grad),
    )
    chains.add("token", piece_swaps(token, 4))
    chains.add("tail", attention_sum((group_a, chains.done["mine"], chains.done["theirs"]), orders, far))
    chains.add("small", sum_all(jnp.concatenate([small, norm_one], 0)))

    def both(mine, other):
        return jnp.where(side == 0, jnp.concatenate([mine, other], 0), jnp.concatenate([other, mine], 0))

    place_far = place_of(far)
    size_far = 2 ** len(far)
    places = [place_of(order) * size_far + place_far for order in orders]
    done = chains.done
    finishers = {
        "out": lambda got: both(out, got),
        "token": lambda got: both(token, got).astype(f32),
        "grads": lambda got: unpack_experts(*got, places, core, dp_size // 2),
    }
    results = {}
    chains.advance(["token", "tail", "small"], fence=())
    while chains.live:
        ready = {n: f(done[n]) for n, f in finishers.items() if n in done and n not in results}
        results.update(chains.advance(fence=ready))
    for name, finisher in finishers.items():
        if name not in results:
            results[name] = finisher(done[name])
    grad_gate, grad_up, grad_down = results["grads"]
    own_tail, other_tail = done["tail"]
    grad_query, grad_key, grad_value, grad_output = unpack(own_tail, other_tail, places, core, dp_size // 2)
    small = done["small"]
    experts = w_router.shape[1]

    return (
        results["out"],
        results["token"],
        grad_query,
        grad_key,
        grad_value,
        grad_output,
        small[experts + 8],
        small[experts],
        small[:experts].T,
        grad_gate,
        grad_up,
        grad_down,
    )


def solution(mesh):
    placed = (
        P("dp", None), P("dp", None), P("dp"), P("dp", None), P("dp", None),
        P(None, "tensor"), P(None, "tensor"), P(None, "tensor"), P("tensor", None),
        P(), P(), P(),
        P(None, None, "tensor"), P(None, None, "tensor"), P(None, "tensor", None),
    )
    return jax.shard_map(
        per_device,
        mesh=mesh,
        in_specs=placed,
        out_specs=(
            P("dp", None), P("dp", None),
            P(None, "tensor"), P(None, "tensor"), P(None, "tensor"), P("tensor", None),
            P(), P(), P(),
            P(None, None, "tensor"), P(None, None, "tensor"), P(None, "tensor", None),
        ),
        check_vma=False,
    )
```

```python
from functools import partial

import jax
import jax.numpy as jnp
from jax import lax
from jax.experimental import pallas as pl
from jax.experimental.pallas import tpu as pltpu
from jax.sharding import PartitionSpec as P

HEAD_DIM = 64
SEQ_LEN = 1024
CAP = 256
EPS = 1e-06
THETA = 10000.0
NEG = -1e30
BLOCK = 256
LANES = 128
GROUP = 4 * HEAD_DIM

f32 = jnp.float32
bf16 = jnp.bfloat16


def nn(left, right):
    return lax.dot_general(left, right, (((1,), (0,)), ((), ())), preferred_element_type=f32)


def nt(left, right):
    return lax.dot_general(left, right, (((1,), (1,)), ((), ())), preferred_element_type=f32)


def tn(left, right):
    return lax.dot_general(left, right, (((0,), (0,)), ((), ())), preferred_element_type=f32)


def params(count=1):
    return pltpu.CompilerParams(
        dimension_semantics=("arbitrary",) * count if count else None,
        vmem_limit_bytes=60 * 1024 * 1024,
    )


def cost(micros):
    return pl.CostEstimate(flops=int(micros * 1.1e9), bytes_accessed=1 << 20, transcendentals=0)


def whole(shape):
    return pl.BlockSpec(shape, lambda *_: (0,) * len(shape))


def once(shape):
    return pl.BlockSpec(shape, lambda *_: (0,) * len(shape), pipeline_mode=pl.Buffered(1))


def lane_iota(rows, lanes=LANES):
    return lax.broadcasted_iota(jnp.int32, (rows, lanes), 1)


def prologue_kernel(side_ref, x_ref, gain_ref, seg_ref, freq_ref, first_ref, first_t_ref, cos_ref, up_ref, down_ref):
    rows = x_ref.shape[0]
    values = x_ref[...].astype(f32)
    scale = lax.rsqrt(jnp.mean(values * values, axis=-1, keepdims=True) + EPS)
    normed = values * scale * gain_ref[...].astype(f32)
    first_ref[...] = normed.astype(bf16)
    first_t_ref[...] = normed.astype(bf16).T
    seg = seg_ref[...]
    zeros = jnp.sum((seg == 0).astype(f32), axis=1, keepdims=True)
    ones = jnp.sum((seg == 1).astype(f32), axis=1, keepdims=True)
    places = lax.broadcasted_iota(jnp.int32, (1, rows), 1).astype(f32)
    places = places - jnp.where(seg >= 1, zeros, 0.0) - jnp.where(seg >= 2, ones, 0.0)
    angles = freq_ref[:, 0:1] * places
    cosine = jnp.cos(angles)
    sine = jnp.sin(angles)
    cosine = jnp.concatenate([cosine] * 4, axis=0).T
    sine = jnp.concatenate([sine] * 4, axis=0).T
    lower = (lane_iota(rows) % HEAD_DIM) < HEAD_DIM // 2
    cos_ref[...] = cosine
    up_ref[...] = jnp.where(lower, -sine, 0.0)
    down_ref[...] = jnp.where(lower, 0.0, sine)


def own_rows(shape):
    return pl.BlockSpec(shape, lambda i, s: (s[0], 0), pipeline_mode=pl.Buffered(1))


def prologue(side, tokens, gain, seg_row, freq):
    rows, width = seg_row.shape[1], tokens.shape[1]
    table = jax.ShapeDtypeStruct((rows, LANES), f32)
    shapes = (
        jax.ShapeDtypeStruct((rows, width), bf16),
        jax.ShapeDtypeStruct((width, rows), bf16),
        table,
        table,
        table,
    )
    return pl.pallas_call(
        prologue_kernel,
        grid_spec=pltpu.PrefetchScalarGridSpec(
            num_scalar_prefetch=1,
            grid=(1,),
            in_specs=[own_rows((rows, width)), once(gain.shape), once(seg_row.shape), once(freq.shape)],
            out_specs=[whole(o.shape) for o in shapes],
        ),
        out_shape=shapes,
        compiler_params=params(),
        cost_estimate=cost(5),
        name="prologue",
    )(side, tokens, gain, seg_row, freq)


def rotate(values, cosine, up, down):
    return (
        values * cosine
        + pltpu.roll(values, LANES - 32, 1) * up
        + pltpu.roll(values, 32, 1) * down
    )


def rotate_back(values, cosine, up, down):
    return (
        values * cosine
        - pltpu.roll(values, LANES - 32, 1) * up
        - pltpu.roll(values, 32, 1) * down
    )


def doubled(values):
    turned = pltpu.roll(values, HEAD_DIM, 1)
    left = lane_iota(values.shape[0]) < HEAD_DIM
    return (
        jnp.where(left, values, turned).astype(bf16),
        jnp.where(left, turned, values).astype(bf16),
    )


def halves_mask():
    left = (lane_iota(1) < HEAD_DIM).astype(f32)
    return left.astype(bf16), (1.0 - left).astype(bf16)


def attend_kernel(
    first_ref, wq_ref, wk_ref, wv_ref, cos_ref, up_ref, down_ref, segc_ref, segr_ref,
    q_ref, k_ref, v_ref, att_ref, lse_ref, bias_ref,
):
    rows = first_ref.shape[0]

    @pl.when(pl.program_id(0) == 0)
    def _():
        for start in range(0, rows, BLOCK):
            at_row = lax.broadcasted_iota(jnp.int32, (BLOCK, rows), 0) + start
            at_col = lax.broadcasted_iota(jnp.int32, (BLOCK, rows), 1)
            allowed = (at_col <= at_row) & (segc_ref[start : start + BLOCK, :] == segr_ref[...])
            bias_ref[start : start + BLOCK, :] = jnp.where(allowed, 0.0, NEG)

    first = first_ref[...]
    cosine, up, down = cos_ref[...], up_ref[...], down_ref[...]
    for tile in range(2):
        part = slice(tile * LANES, (tile + 1) * LANES)
        raw = nn(first, wq_ref[:, part])
        q_ref[:, part] = (rotate(raw, cosine, up, down) * HEAD_DIM**-0.5).astype(bf16)
    key = rotate(nn(first, wk_ref[...]), cosine, up, down)
    value = nn(first, wv_ref[...])
    k_ref[...] = key.astype(bf16)
    v_ref[...] = value.astype(bf16)
    keys, values = doubled(key), doubled(value)
    low, high = halves_mask()
    for start in range(0, rows, BLOCK):
        width = start + BLOCK
        mine = slice(start, width)
        bias = bias_ref[mine, :width]
        bias = jnp.concatenate([bias, bias], axis=0)
        logs = jnp.zeros((BLOCK, LANES), f32)
        lanes = lane_iota(BLOCK)
        for kv in range(2):
            part = slice(kv * LANES, (kv + 1) * LANES)
            query = q_ref[mine, part]
            query = jnp.concatenate([query * low, query * high], axis=0)
            scores = nt(query, keys[kv][:width]) + bias
            row_max = jnp.max(scores, axis=-1, keepdims=True)
            weights = jnp.exp(scores - row_max)
            total = jnp.sum(weights, axis=-1, keepdims=True)
            probs = (weights * (1.0 / total)).astype(bf16)
            out = nn(probs, values[kv][:width])
            att_ref[mine, part] = jnp.where(lanes < HEAD_DIM, out[:BLOCK], out[BLOCK:]).astype(bf16)
            log_total = row_max + jnp.log(total)
            logs = jnp.where(lanes == 2 * kv, log_total[:BLOCK], logs)
            logs = jnp.where(lanes == 2 * kv + 1, log_total[BLOCK:], logs)
        lse_ref[0, :, mine] = logs.T[:8]


def attend(first, weights, tables, seg_col, seg_row):
    rows, width = first.shape
    packed = len(weights) == 1
    wq, wk, wv = weights * 3 if packed else weights
    groups = 1 if packed else wq.shape[1] // GROUP
    table = whole((rows, LANES))
    return pl.pallas_call(
        attend_kernel,
        grid=(groups,),
        in_specs=[
            whole((rows, width)),
            pl.BlockSpec((width, GROUP), lambda g: (0, g)),
            pl.BlockSpec((width, LANES), lambda g: (0, 2 if packed else g)),
            pl.BlockSpec((width, LANES), lambda g: (0, 3 if packed else g)),
            table,
            table,
            table,
            whole((rows, 1)),
            whole((1, rows)),
        ],
        out_specs=[
            pl.BlockSpec((rows, GROUP), lambda g: (0, g)),
            pl.BlockSpec((rows, LANES), lambda g: (0, g)),
            pl.BlockSpec((rows, LANES), lambda g: (0, g)),
            pl.BlockSpec((rows, GROUP), lambda g: (0, g)),
            pl.BlockSpec((1, 8, rows), lambda g: (g, 0, 0)),
        ],
        out_shape=(
            jax.ShapeDtypeStruct((rows, groups * GROUP), bf16),
            jax.ShapeDtypeStruct((rows, groups * LANES), bf16),
            jax.ShapeDtypeStruct((rows, groups * LANES), bf16),
            jax.ShapeDtypeStruct((rows, groups * GROUP), bf16),
            jax.ShapeDtypeStruct((groups, 8, rows), f32),
        ),
        scratch_shapes=[pltpu.VMEM((rows, rows), f32)],
        compiler_params=params(),
        cost_estimate=cost(10 * groups),
        name="attend",
    )(first, wq, wk, wv, *tables, seg_col, seg_row)


def router_kernel(
    side_ref, x_ref, att_a_ref, att_b_ref, att_c_ref, wo_a_ref, wo_b_ref, wo_c_ref, gain_ref, wr_ref, routes_ref, slots_ref,
    resid_ref, second_ref, gates_ref, places_ref,
):
    mixed = nn(att_a_ref[...], wo_a_ref[...])
    mixed = mixed + nn(att_b_ref[...], wo_b_ref[...])
    mixed = mixed + nn(att_c_ref[...], wo_c_ref[...])
    resid = x_ref[...].astype(f32) + mixed
    resid_ref[...] = resid
    scale = lax.rsqrt(jnp.mean(resid * resid, axis=-1, keepdims=True) + EPS)
    second = (resid * scale * gain_ref[...].astype(f32)).astype(bf16)
    second_ref[...] = second
    logits = nt(wr_ref[...], second)
    experts, rows = logits.shape
    routes, slots = routes_ref[...], slots_ref[...]
    number = lax.broadcasted_iota(jnp.int32, (experts, rows), 0)
    chosen = jnp.zeros((experts, rows), f32)
    place = jnp.zeros((8, rows), jnp.int32)
    taken = jnp.zeros((8, rows), jnp.int32)
    for k in range(routes.shape[0]):
        hit = number == routes[k : k + 1, :]
        chosen = jnp.where(hit, 1.0, chosen)
        hit = number[:8] == routes[k : k + 1, :]
        place = jnp.where(hit, slots[k : k + 1, :], place)
        taken = jnp.where(hit, 1, taken)
    places_ref[...] = jnp.where(taken > 0, place, CAP)
    top = jnp.max(jnp.where(chosen > 0, logits, NEG), axis=0, keepdims=True)
    weights = jnp.where(chosen > 0, jnp.exp(logits - top), 0.0)
    gates_ref[...] = weights / jnp.sum(weights, axis=0, keepdims=True)


def router(side, tokens, attended, outputs, gain, wr_t, routes_t, slots_t):
    rows, width = routes_t.shape[1], tokens.shape[1]
    rest = (*attended, *outputs, gain, wr_t, routes_t, slots_t)
    shapes = (
        jax.ShapeDtypeStruct((rows, width), f32),
        jax.ShapeDtypeStruct((rows, width), bf16),
        jax.ShapeDtypeStruct((wr_t.shape[0], rows), f32),
        jax.ShapeDtypeStruct((8, rows), jnp.int32),
    )
    return pl.pallas_call(
        router_kernel,
        grid_spec=pltpu.PrefetchScalarGridSpec(
            num_scalar_prefetch=1,
            grid=(1,),
            in_specs=[own_rows((rows, width)), *[once(a.shape) for a in rest]],
            out_specs=[whole(o.shape) for o in shapes],
        ),
        out_shape=shapes,
        compiler_params=params(),
        cost_estimate=cost(8),
        name="router",
    )(side, tokens, *rest)


def split_three(values):
    first = values.astype(bf16)
    rest = values - first.astype(f32)
    second = rest.astype(bf16)
    return first, second, (rest - second.astype(f32)).astype(bf16)


def experts_kernel(
    order_ref, second_ref, cot_ref, resid_ref, gates_ref, places_ref, gain_ref, wr_ref,
    wg_a_ref, wg_b_ref, wu_a_ref, wu_b_ref, wd_a_ref, wd_b_ref,
    out_ref, low_t_ref, low_ref, grad_ref, small_ref, kept_ref, sent_ref,
    moe_ref, slot_grads_ref,
):
    step = pl.program_id(0)
    e = step ^ order_ref[0]
    rows = second_ref.shape[0]
    second = second_ref[...]
    slots = lax.broadcasted_iota(jnp.int32, (CAP, rows), 0)
    hit = slots == places_ref[pl.ds(e, 1), :]
    gate_slot = jnp.sum(jnp.where(hit, gates_ref[pl.ds(e, 1), :], 0.0), axis=1, keepdims=True)
    onehot = jnp.where(hit, 1.0, 0.0).astype(bf16)
    expert_in = nn(onehot, second).astype(bf16)
    slot_grad = nn(onehot, cot_ref[...])
    out_grad = (gate_slot * slot_grad).astype(bf16)
    expert_out = None
    back = None
    factors = []
    for wg_ref, wu_ref, wd_ref in ((wg_a_ref, wu_a_ref, wd_a_ref), (wg_b_ref, wu_b_ref, wd_b_ref)):
        wg, wu, wd = wg_ref[0], wu_ref[0], wd_ref[0]
        gate_pre = nn(expert_in, wg)
        up_pre = nn(expert_in, wu)
        sig = 1.0 / (1.0 + jnp.exp(-gate_pre))
        silu = gate_pre * sig
        hidden = (silu * up_pre).astype(bf16)
        part = nn(hidden, wd)
        expert_out = part if expert_out is None else expert_out + part
        hidden_grad = nt(out_grad, wd)
        gate_low = (hidden_grad * up_pre * sig * (1.0 + gate_pre * (1.0 - sig))).astype(bf16)
        up_low = (hidden_grad * silu).astype(bf16)
        factors.append((gate_low, up_low, hidden))
        part = nt(gate_low, wg) + nt(up_low, wu)
        back = part if back is None else back + part

    def weight_grads(ref):
        size = hidden.shape[1]
        for half, (gate_low, up_low, mixed) in enumerate(factors):
            ref[0, half, :size, :] = tn(gate_low, expert_in).astype(bf16)
            ref[0, half, size : 2 * size, :] = tn(up_low, expert_in).astype(bf16)
            ref[0, half, 2 * size :, :] = tn(mixed, out_grad).astype(bf16)

    @pl.when(step % 2 == 0)
    def _():
        weight_grads(kept_ref)

    @pl.when(step % 2 == 1)
    def _():
        weight_grads(sent_ref)

    slot_gate = jnp.sum(expert_out * slot_grad, axis=1, keepdims=True)
    gate_row = jnp.sum(jnp.where(hit, slot_gate, 0.0), axis=0, keepdims=True)
    moe = tn(onehot, (gate_slot * expert_out).astype(bf16))
    second_back = tn(onehot, back.astype(bf16))

    @pl.when(step == 0)
    def _():
        moe_ref[...] = moe
        grad_ref[...] = second_back
        slot_grads_ref[...] = jnp.zeros_like(slot_grads_ref)

    @pl.when(step > 0)
    def _():
        moe_ref[...] += moe
        grad_ref[...] += second_back

    slot_grads_ref[pl.ds(e, 1), :] = gate_row

    @pl.when(step == pl.num_programs(0) - 1)
    def _():
        gates = gates_ref[...]
        resid = resid_ref[...]
        out_ref[...] = (resid + moe_ref[...]).astype(bf16)
        gate_grad = slot_grads_ref[...]
        logit_grad = gates * (gate_grad - jnp.sum(gates * gate_grad, axis=0, keepdims=True))
        router_grad = None
        second_grad = grad_ref[...]
        for piece in split_three(logit_grad):
            part = nn(piece, second)
            router_grad = part if router_grad is None else router_grad + part
            second_grad = second_grad + tn(piece, wr_ref[...])
        experts = gates.shape[0]
        small_ref[0:experts, :] = router_grad
        gain = gain_ref[...].astype(f32)
        scale = lax.rsqrt(jnp.mean(resid * resid, axis=-1, keepdims=True) + EPS)
        norm_grad = jnp.sum(second_grad * resid * scale, axis=0, keepdims=True)
        small_ref[experts : experts + 8, :] = jnp.where(
            lax.broadcasted_iota(jnp.int32, (8, resid.shape[1]), 0) == 0, norm_grad, 0.0
        )
        inner = jnp.mean(gain * second_grad * resid, axis=-1, keepdims=True)
        grad = scale * gain * second_grad - resid * (scale * scale * scale) * inner
        grad = grad + cot_ref[...].astype(f32)
        grad_ref[...] = grad
        low_ref[...] = grad.astype(bf16)
        low_t_ref[...] = grad.astype(bf16).T


def experts_layer(order, second, cot, resid, gates, places, gain, wr_t, weights):
    rows, width = second.shape
    own_cot = pl.BlockSpec((rows, width), lambda i, o: (o[1], 0), pipeline_mode=pl.Buffered(1))
    experts = gates.shape[0]
    window, _, hidden = weights[0].shape
    wide = pl.BlockSpec((1, width, hidden), lambda i, o: (i ^ o[0], 0, 0))
    tall = pl.BlockSpec((1, hidden, width), lambda i, o: (i ^ o[0], 0, 0))
    wide_rel = pl.BlockSpec((1, width, hidden), lambda i, o: (i, 0, 0))
    tall_rel = pl.BlockSpec((1, hidden, width), lambda i, o: (i, 0, 0))
    grads_out = jax.ShapeDtypeStruct((window // 2, 2, 3 * hidden, width), bf16)
    grads = pl.BlockSpec((1, 2, 3 * hidden, width), lambda i, o: ((i // 2) ^ (o[0] // 2), 0, 0, 0))
    return pl.pallas_call(
        experts_kernel,
        grid_spec=pltpu.PrefetchScalarGridSpec(
        num_scalar_prefetch=1,
        grid=(window,),
        in_specs=[
            once((rows, width)),
            own_cot,
            once((rows, width)),
            whole((experts, rows)),
            whole((8, rows)),
            whole((1, width)),
            whole((experts, width)),
            wide,
            wide_rel,
            wide,
            wide_rel,
            tall,
            tall_rel,
        ],
        out_specs=[
            once((rows, width)),
            once((width, rows)),
            once((rows, width)),
            once((rows, width)),
            whole((experts + 8, width)),
            grads,
            grads,
        ],
        scratch_shapes=[
            pltpu.VMEM((rows, width), f32),
            pltpu.VMEM((experts, rows), f32),
        ],
        ),
        out_shape=(
            jax.ShapeDtypeStruct((rows, width), bf16),
            jax.ShapeDtypeStruct((width, rows), bf16),
            jax.ShapeDtypeStruct((rows, width), bf16),
            jax.ShapeDtypeStruct((rows, width), f32),
            jax.ShapeDtypeStruct((experts + 8, width), f32),
            grads_out,
            grads_out,
        ),
        compiler_params=params(),
        cost_estimate=cost(39),
        name="experts",
    )(order, second, cot, resid, gates, places, gain, wr_t, *weights)


def attend_back_kernel(
    sel_ref, q_ref, k_ref, v_ref, lse_ref, cos_ref, up_ref, down_ref, segc_ref, segr_ref, low_ref, wo_ref,
    back_ref, bias_ref, dq_ref, dk_ref, dv_ref,
):
    rows = q_ref.shape[0]
    for start in range(0, rows, BLOCK):
        at_key = lax.broadcasted_iota(jnp.int32, (BLOCK, rows), 0) + start
        at_query = lax.broadcasted_iota(jnp.int32, (BLOCK, rows), 1)
        allowed = (at_key <= at_query) & (segc_ref[start : start + BLOCK, :] == segr_ref[...])
        bias_ref[start : start + BLOCK, :] = jnp.where(allowed, 0.0, NEG)
    upward = nt(low_ref[...], wo_ref[...]).astype(bf16)
    keys = doubled(k_ref[...].astype(f32))
    values = doubled(v_ref[...].astype(f32))
    low, high = halves_mask()
    dk_ref[...] = jnp.zeros_like(dk_ref)
    dv_ref[...] = jnp.zeros_like(dv_ref)
    lanes = lane_iota(BLOCK)
    for start in range(0, rows, BLOCK):
        width = start + BLOCK
        mine = slice(start, width)
        bias = bias_ref[:width, mine]
        bias = jnp.concatenate([bias, bias], axis=1)
        for kv in range(2):
            part = slice(kv * LANES, (kv + 1) * LANES)
            query = q_ref[mine, part]
            query = jnp.concatenate([query * low, query * high], axis=0)
            upper = upward[mine, part]
            upper = jnp.concatenate([upper * low, upper * high], axis=0)
            logs = jnp.concatenate(
                [lse_ref[0, 2 * kv : 2 * kv + 1, mine], lse_ref[0, 2 * kv + 1 : 2 * kv + 2, mine]], axis=1
            )
            key = keys[kv][:width]
            probs = jnp.exp(nt(key, query) + bias - logs)
            prob_grad = nt(values[kv][:width], upper)
            product = probs * prob_grad
            delta = jnp.sum(product, axis=0, keepdims=True)
            raw = (product - probs * delta).astype(bf16)
            dv_ref[kv, :width, :] += nn(probs.astype(bf16), upper)
            dk_ref[kv, :width, :] += nn(raw, query)
            back = tn(raw, key)
            dq_ref[mine, part] = jnp.where(lanes < HEAD_DIM, back[:BLOCK], back[BLOCK:])
    cosine, up, down = cos_ref[...], up_ref[...], down_ref[...]
    left = lane_iota(rows) < HEAD_DIM

    def both(ref):
        one, two = ref[0], ref[1]
        one = one + pltpu.roll(one, HEAD_DIM, 1)
        two = two + pltpu.roll(two, HEAD_DIM, 1)
        return jnp.where(left, one, two)

    back_ref[:, 2 * LANES : 3 * LANES] = rotate_back(both(dk_ref), cosine, up, down).astype(bf16)
    back_ref[:, 3 * LANES :] = both(dv_ref).astype(bf16)
    for kv in range(2):
        part = slice(kv * LANES, (kv + 1) * LANES)
        turned = rotate_back(dq_ref[:, part], cosine, up, down)
        back_ref[:, part] = (turned * HEAD_DIM**-0.5).astype(bf16)


def attend_back(sel, saved, tables, seg_col, seg_row, low_grad, wo):
    query, key, value, _, logs = saved
    rows, width = low_grad.shape

    def fixed(shape):
        return pl.BlockSpec(shape, lambda i, s: (0,) * len(shape))

    table = fixed((rows, LANES))
    wide = pl.BlockSpec((rows, GROUP), lambda i, s: (0, s[0]))
    thin = pl.BlockSpec((rows, LANES), lambda i, s: (0, s[0]))
    return pl.pallas_call(
        attend_back_kernel,
        grid_spec=pltpu.PrefetchScalarGridSpec(
            num_scalar_prefetch=1,
            grid=(1,),
            in_specs=[
                wide, thin, thin, pl.BlockSpec((1, 8, rows), lambda i, s: (s[0], 0, 0)),
                table, table, table, fixed((rows, 1)), fixed((1, rows)),
                fixed((rows, width)), pl.BlockSpec((GROUP, width), lambda i, s: (s[0], 0)),
            ],
            out_specs=fixed((rows, 2 * GROUP)),
            scratch_shapes=[
                pltpu.VMEM((rows, rows), f32),
                pltpu.VMEM((rows, GROUP), f32),
                pltpu.VMEM((2, rows, LANES), f32),
                pltpu.VMEM((2, rows, LANES), f32),
            ],
        ),
        out_shape=jax.ShapeDtypeStruct((rows, 2 * GROUP), bf16),
        compiler_params=params(),
        cost_estimate=cost(14),
        name="attend_back",
    )(sel, query, key, value, logs, *tables, seg_col, seg_row, low_grad, wo)


def project_kernel(
    final, fresh, sel_ref, back_ref, att_ref, low_t_ref, first_t_ref, wq_ref, wk_ref, wv_ref, *rest
):
    if not fresh:
        before_ref, *rest = rest
    if final:
        x_ref, gain_ref, grad_ref, group_ref, token_ref, norm_ref = rest
    else:
        group_ref, sum_ref = rest
    step = pl.program_id(0)
    block = first_t_ref.shape[0]
    group_ref[:, : 2 * GROUP] = nn(first_t_ref[...], back_ref[...]).astype(bf16)
    group_ref[:, 2 * GROUP :] = nn(low_t_ref[...], att_ref[...]).astype(bf16)
    back = back_ref[pl.ds(pl.multiple_of(step * block, block), block), :]
    first_grad = nt(back[:, :GROUP], wq_ref[...])
    first_grad = first_grad + nt(back[:, GROUP : GROUP + LANES], wk_ref[...])
    first_grad = first_grad + nt(back[:, GROUP + LANES :], wv_ref[...])
    if not fresh:
        first_grad = before_ref[...] + first_grad
    if final:
        inputs = x_ref[...].astype(f32)
        gain = gain_ref[...].astype(f32)
        scale = lax.rsqrt(jnp.mean(inputs * inputs, axis=-1, keepdims=True) + EPS)
        norm = jnp.broadcast_to(jnp.sum(first_grad * inputs * scale, axis=0, keepdims=True), norm_ref.shape)

        @pl.when(step == 0)
        def _():
            norm_ref[...] = norm

        @pl.when(step > 0)
        def _():
            norm_ref[...] += norm

        inner = jnp.mean(gain * first_grad * inputs, axis=-1, keepdims=True)
        grad = scale * gain * first_grad - inputs * (scale * scale * scale) * inner
        token_ref[...] = (grad + grad_ref[...]).astype(bf16)
    else:
        sum_ref[...] = first_grad


def project(sel, back, att, low_t, first_t, weights, before=None, final=None):
    width, rows = low_t.shape
    packed = len(weights) == 1
    wq, wk, wv = weights * 3 if packed else weights
    steps = 4
    block = rows // steps
    assert rows == width

    def fixed(shape):
        return pl.BlockSpec(shape, lambda i, s: (0,) * len(shape))

    wide_w = pl.BlockSpec((width, GROUP), lambda i, s: (0, s[0]))
    key_w = pl.BlockSpec((width, LANES), lambda i, s: (0, 2 if packed else s[0]))
    value_w = pl.BlockSpec((width, LANES), lambda i, s: (0, 3 if packed else s[0]))
    strip = pl.BlockSpec((block, width), lambda i, s: (i, 0))
    in_specs = [
        fixed((rows, 2 * GROUP)), pl.BlockSpec((rows, GROUP), lambda i, s: (0, s[0])),
        strip, strip, wide_w, key_w, value_w,
    ]
    out_specs = [pl.BlockSpec((block, 3 * GROUP), lambda i, s: (i, 0))]
    out_shape = [jax.ShapeDtypeStruct((width, 3 * GROUP), bf16)]
    extra = ()
    if before is not None:
        in_specs.append(strip)
        extra = (before,)
    if final is None:
        out_specs.append(strip)
        out_shape.append(jax.ShapeDtypeStruct((rows, width), f32))
    else:
        extra = (*extra, *final)
        in_specs += [pl.BlockSpec((block, width), lambda i, s: (s[1] * steps + i, 0)), fixed((1, width)), strip]
        out_specs += [strip, fixed((8, width))]
        out_shape += [
            jax.ShapeDtypeStruct((rows, width), bf16),
            jax.ShapeDtypeStruct((8, width), f32),
        ]
    return pl.pallas_call(
        partial(project_kernel, final is not None, before is None),
        grid_spec=pltpu.PrefetchScalarGridSpec(
            num_scalar_prefetch=1, grid=(steps,), in_specs=in_specs, out_specs=out_specs
        ),
        out_shape=tuple(out_shape),
        compiler_params=params(),
        cost_estimate=cost(7),
        name="project_final" if final is not None else "project",
    )(sel, back, att, low_t, first_t, wq, wk, wv, *extra)


def plain_order(piece, place, count):
    shape = piece.shape
    bit = 1
    while bit < count:
        pairs = piece.reshape(-1, 2, bit * shape[0] // count, shape[1])
        flipped = jnp.concatenate([pairs[:, 1:], pairs[:, :1]], axis=1)
        piece = jnp.where((place // bit) % 2 == 1, flipped, pairs)
        bit *= 2
    return piece.reshape(shape)


def add_split(colors, sides):
    rows = [terms[0][0].shape[1] for terms in colors]
    half = rows[0] // 2
    if half % 16:
        out = []
        for terms, side in zip(colors, sides):
            cutouts = [lax.slice_in_dim(t, i * n, (i + 1) * n, axis=0) for t, n, i in terms]
            both = []
            for at in (side, 1 - side):
                pieces = [lax.dynamic_slice_in_dim(t, at * half, half, 1).astype(f32) for t in cutouts]
                both.append(sum(pieces[1:], pieces[0]).astype(bf16))
            out.append(tuple(both))
        return out
    steps = 4 if half % 64 == 0 else (2 if half % 32 == 0 else 1)
    block = half // steps
    in_specs, operands, out_specs, shapes, counts = [], [], [], [], []
    for number, terms in enumerate(colors):
        counts.append(len(terms))
        for other in (0, 1):
            for array, lead, index in terms:

                def place(j, s, number=number, index=index, other=other):
                    return (index, (s[number] ^ other) * steps + j, 0)

                in_specs.append(pl.BlockSpec((lead, block, array.shape[2]), place))
                operands.append(array)
        array, lead, _ = terms[0]
        for _ in range(2):
            out_specs.append(pl.BlockSpec((lead, block, array.shape[2]), lambda j, s: (0, j, 0)))
            shapes.append(jax.ShapeDtypeStruct((lead, half, array.shape[2]), bf16))

    def kernel(side_ref, *refs):
        ins, outs = refs[: len(operands)], refs[len(operands) :]
        at = 0
        for number, count in enumerate(counts):
            for other in range(2):
                value = ins[at][...].astype(f32)
                for term in range(1, count):
                    value = value + ins[at + term][...].astype(f32)
                outs[2 * number + other][...] = value.astype(bf16)
                at += count

    out = pl.pallas_call(
        kernel,
        grid_spec=pltpu.PrefetchScalarGridSpec(
            num_scalar_prefetch=1, grid=(steps,), in_specs=in_specs, out_specs=out_specs
        ),
        out_shape=tuple(shapes),
        compiler_params=params(),
        cost_estimate=cost(4),
        name="add_split",
    )(jnp.stack(sides), *operands)
    return [(out[2 * i], out[2 * i + 1]) for i in range(len(colors))]


def add_halves(colors):
    count = len(colors)
    _, rows, columns = colors[0][0].shape

    def kernel(*refs):
        ins, (mine_ref, theirs_ref) = refs[:-2], refs[-2:]
        for i in range(count):
            value = (ins[2 * i][...].astype(f32) + ins[2 * i + 1][...].astype(f32)).astype(bf16)
            mine_ref[i] = value[0]
            theirs_ref[i] = value[1]

    shape = jax.ShapeDtypeStruct((count, rows, columns), bf16)
    return pl.pallas_call(
        kernel,
        out_shape=(shape, shape),
        compiler_params=params(0),
        cost_estimate=cost(3),
        name="add_halves",
    )(*[a for pair in colors for a in pair])


def straighten(pieces, places, count):
    if (pieces[0].shape[0] // count) % 16:
        return [plain_order(p, at, count) for p, at in zip(pieces, places)], [jnp.int32(0)] * len(places), 1
    return pieces, places, count


def unpack_experts(own, other, places, core, count):
    pairs = len(own)
    flat, places, count = straighten([*own, *other], [*places, *places], count)
    rows, width = flat[0].shape
    block, hidden = rows // count, rows // 3

    def kernel(place_ref, *refs):
        ins, (gate_ref, up_ref, down_ref, plain_ref) = refs[: 2 * pairs], refs[2 * pairs :]
        e = pl.program_id(0)
        for pair in range(pairs):
            for far in range(2):
                ref = ins[far * pairs + pair]

                @pl.when(e == 2 * pair + (place_ref[pairs] ^ far))
                def _(ref=ref, pair=pair):
                    for i in range(count):
                        start = pl.multiple_of((i ^ place_ref[pair]) * block, block)
                        plain_ref[i * block : (i + 1) * block, :] = ref[pl.ds(start, block), :].astype(f32)

        gate_ref[0] = plain_ref[:hidden, :].T
        up_ref[0] = plain_ref[hidden : 2 * hidden, :].T
        down_ref[0] = plain_ref[2 * hidden :, :]

    wide = jax.ShapeDtypeStruct((2 * pairs, width, hidden), f32)
    tall = jax.ShapeDtypeStruct((2 * pairs, hidden, width), f32)
    return pl.pallas_call(
        kernel,
        grid_spec=pltpu.PrefetchScalarGridSpec(
            num_scalar_prefetch=1,
            grid=(2 * pairs,),
            in_specs=[pl.BlockSpec((rows, width), lambda e, s: (0, 0))] * (2 * pairs),
            out_specs=[
                pl.BlockSpec((1, width, hidden), lambda e, s: (e, 0, 0)),
                pl.BlockSpec((1, width, hidden), lambda e, s: (e, 0, 0)),
                pl.BlockSpec((1, hidden, width), lambda e, s: (e, 0, 0)),
            ],
            scratch_shapes=[pltpu.VMEM((rows, width), f32)],
        ),
        out_shape=(wide, wide, tall),
        compiler_params=params(),
        cost_estimate=cost(10),
        name="unpack_experts",
    )(jnp.stack([*places[:pairs], core]), *flat)


def unpack(own, other, places, core, count):
    colors = len(own)
    flat, places, count = straighten([*own, *other], [*places, *places], count)
    rows, columns = flat[0].shape
    block = rows // count
    shapes = (
        jax.ShapeDtypeStruct((colors * rows, 2 * GROUP), f32),
        jax.ShapeDtypeStruct((colors * rows, 2 * LANES), f32),
        jax.ShapeDtypeStruct((colors * rows, 2 * LANES), f32),
        jax.ShapeDtypeStruct((2 * GROUP, colors * rows), f32),
    )

    def kernel(place_ref, *refs):
        ins, (query_ref, key_ref, value_ref, output_ref, plain_ref) = refs[: 2 * colors], refs[2 * colors :]
        for group in range(2):
            for color in range(colors):
                for i in range(count):
                    start = pl.multiple_of((i ^ place_ref[color]) * block, block)
                    one = ins[color][pl.ds(start, block), :].astype(f32)
                    two = ins[colors + color][pl.ds(start, block), :].astype(f32)
                    plain_ref[i * block : (i + 1) * block, :] = jnp.where(place_ref[colors] == group, one, two)
                here = slice(color * rows, (color + 1) * rows)
                wide = slice(group * GROUP, (group + 1) * GROUP)
                thin = slice(group * LANES, (group + 1) * LANES)
                query_ref[here, wide] = plain_ref[:, :GROUP]
                key_ref[here, thin] = plain_ref[:, GROUP : GROUP + LANES]
                value_ref[here, thin] = plain_ref[:, GROUP + LANES : 2 * GROUP]
                output_ref[wide, here] = plain_ref[:, 2 * GROUP :].T

    return pl.pallas_call(
        kernel,
        grid_spec=pltpu.PrefetchScalarGridSpec(
            num_scalar_prefetch=1,
            grid=(1,),
            in_specs=[pl.BlockSpec((rows, columns), lambda i, s: (0, 0))] * (2 * colors),
            out_specs=[pl.BlockSpec(o.shape, lambda i, s: (0, 0)) for o in shapes],
            scratch_shapes=[pltpu.VMEM((rows, columns), f32)],
        ),
        out_shape=shapes,
        compiler_params=params(),
        cost_estimate=cost(6),
        name="unpack",
    )(jnp.stack([*places[:colors], core]), *flat)


def swap_tensor(values):
    return lax.ppermute(values, "tensor", [(0, 1), (1, 0)])


def swap_dp(values, bit):
    count = lax.axis_size("dp")
    return lax.ppermute(values, "dp", [(i, i ^ bit) for i in range(count)])


def after(values, earlier):
    return lax.optimization_barrier((values, earlier))[0]


def bit_of(bit):
    return (lax.axis_index("dp") // bit) % 2


def cut(values, index, axis, count=2):
    size = values.shape[axis] // count
    return lax.dynamic_slice_in_dim(values, index * size, size, axis)


def total(terms):
    out = terms[0].astype(f32)
    for term in terms[1:]:
        out = out + term.astype(f32)
    return out.astype(bf16)


def swap(values, bit):
    return swap_tensor(values) if bit == 0 else swap_dp(values, bit)


def place_of(order):
    place = 0
    for bit in order:
        if bit:
            place = 2 * place + bit_of(bit)
    return place


def gather_back(pieces, orders):
    for bits in zip(*(reversed(order) for order in orders)):
        got = yield list(zip(pieces, bits))
        pieces = [jnp.concatenate([p, g], 0) for p, g in zip(pieces, got)]
    got = yield [(p, 1) for p in pieces]
    return pieces, got


def sum_all(values):
    for bit in [0] + [1 << i for i in range(30) if (1 << i) < lax.axis_size("dp")]:
        (got,) = yield [(values, bit)]
        values = values + got
    return values


def experts_sum(kept, sent, orders, far):
    flat = kept.reshape(-1, *kept.shape[2:])
    (got,) = yield [(sent.reshape(flat.shape), 1)]
    colors = [[(flat, 2, i), (got, 2, i)] for i in range(len(orders))]
    for bits in zip(*orders):
        split = add_split(colors, [bit_of(b) for b in bits])
        got = yield [(s, b) for (_, s), b in zip(split, bits)]
        colors = [[(k, 2, 0), (g, 2, 0)] for (k, _), g in zip(split, got)]
    mine, theirs = add_halves([[t for t, _, _ in terms] for terms in colors])
    (got,) = yield [(theirs, 0)]
    count = len(orders)
    for bit in far:
        ((mine, theirs),) = add_split([[(mine, count, 0), (got, count, 0)]], [bit_of(bit)])
        (got,) = yield [(theirs, bit)]
    piece = total([mine, got])
    for bit in reversed(far):
        (got,) = yield [(piece, bit)]
        piece = jnp.concatenate([piece, got], 1)
    return (yield from gather_back([piece[i] for i in range(count)], orders))


def attention_sum(terms, orders, far):
    count = len(orders)
    parts = [t.reshape(count, t.shape[0] // count, t.shape[1]) for t in terms]
    colors = [[(p, 1, i) for p in parts] for i in range(count)]
    for bits in zip(*orders):
        split = add_split(colors, [bit_of(b) for b in bits])
        got = yield [(s, b) for (_, s), b in zip(split, bits)]
        colors = [[(k, 1, 0), (g, 1, 0)] for (k, _), g in zip(split, got)]
    for bit in far:
        split = add_split(colors, [bit_of(bit)] * count)
        (got,) = yield [(jnp.concatenate([s for _, s in split], 0), bit)]
        colors = [[(k, 1, 0), (got, 1, i)] for i, (k, _) in enumerate(split)]
    piece = jnp.concatenate(
        [total([lax.slice_in_dim(t, i, i + n, axis=0) for t, n, i in terms]) for terms in colors], 0
    )
    for bit in reversed(far):
        (got,) = yield [(piece, bit)]
        piece = jnp.concatenate([piece, got], 1)
    return (yield from gather_back([piece[i] for i in range(count)], orders))


class Chains:
    def __init__(self):
        self.live = {}
        self.done = {}

    def advance(self, names=None, fence=None):
        names = [n for n in (names or list(self.live)) if n in self.live]
        requests = {}
        waiting = {n: self.live[n][1] for n in names}
        if fence is not None:
            fence, waiting = lax.optimization_barrier((fence, waiting))
        for n in names:
            chain = self.live[n][0]
            try:
                requests[n] = chain.send(waiting[n])
            except StopIteration as stop:
                self.done[n] = stop.value
                del self.live[n]
        sends = {n: [v for v, _ in r] for n, r in requests.items()}
        if fence is not None:
            fence, sends = lax.optimization_barrier((fence, sends))
        for n, r in requests.items():
            self.live[n] = (self.live[n][0], [swap(v, bit) for v, (_, bit) in zip(sends[n], r)])
        return fence

    def add(self, name, chain):
        self.live[name] = (chain, None)


def per_device(
    tokens, cotangent, segments, routes, slot_index,
    w_query, w_key, w_value, w_output, norm_attn, norm_ffn, w_router, w_gate, w_up, w_down,
):
    length, width = tokens.shape
    side = lax.axis_index("tensor")
    dp_size = lax.axis_size("dp")
    core = lax.axis_index("dp") % 2
    rows = SEQ_LEN
    far = [8 << i for i in range(20) if (8 << i) < dp_size]

    def own(values):
        return lax.dynamic_slice_in_dim(values, side * rows, rows, 0)

    seg = own(segments)
    seg_row, seg_col = seg[None, :], seg[:, None]
    routes_t = own(routes).T
    slots_t = own(slot_index).T
    wr_t = w_router.T
    gain_one, gain_two = norm_attn[None, :], norm_ffn[None, :]
    half_dim = HEAD_DIM // 2
    frequency = THETA ** (-(2.0 * jnp.arange(half_dim, dtype=f32)) / HEAD_DIM)
    freq = jnp.broadcast_to(frequency[:, None], (half_dim, LANES))

    near = swap_tensor(jnp.concatenate([cut(w, core, 1) for w in (w_query, w_key, w_value)], 1))
    order_index = lax.axis_index("dp") % 4
    experts_own = [lax.dynamic_slice_in_dim(w, order_index, 1, 0) for w in (w_gate, w_up, w_down)]
    got = [swap_tensor(experts_own[0])]

    first, first_t, *tables = prologue(side[None], tokens, gain_one, seg_row, freq)
    saved_a = attend(first, (w_query, w_key, w_value), tables, seg_col, seg_row)
    (near, got[0]), (first, saved_a) = lax.optimization_barrier(((near, got[0]), (first, saved_a)))
    far_qkv = swap_dp(near, 1)
    near_out = swap_tensor(after(cut(w_output, core, 0), near))
    got.append(swap_tensor(after(experts_own[1], near)))
    across = [swap_dp(got[0], 2)]
    beside = [swap_dp(got[0], 1)]
    saved_b = attend(first, (near,), tables, seg_col, seg_row)
    (near_out, got[1], across[0]), (first, saved_b) = lax.optimization_barrier(
        ((near_out, got[1], across[0]), (first, saved_b))
    )
    far_out = swap_dp(near_out, 1)
    got.append(swap_tensor(after(experts_own[2], near_out)))
    across.append(swap_dp(got[1], 2))
    beside.append(swap_dp(got[1], 1))
    corner = [swap_dp(across[0], 1)]
    saved_c = attend(first, (far_qkv,), tables, seg_col, seg_row)
    (across[1], got[2]), saved_c = lax.optimization_barrier(((across[1], got[2]), saved_c))
    across.append(swap_dp(got[2], 2))
    beside.append(swap_dp(got[2], 1))
    corner.append(swap_dp(across[1], 1))
    resid, second, gates, places = router(
        side[None], tokens, (saved_a[3], saved_b[3], saved_c[3]), (w_output, near_out, far_out), gain_two, wr_t, routes_t, slots_t
    )
    across[2], second = lax.optimization_barrier((across[2], second))
    corner.append(swap_dp(across[2], 1))
    r_gate, r_up, r_down = (jnp.concatenate(parts, axis=0) for parts in zip(got, beside, across, corner))
    out, low_t, low_grad, resid_grad, small, kept, sent = experts_layer(
        jnp.stack([order_index, side]), second, cotangent, resid, gates, places, gain_two, wr_t,
        (w_gate, r_gate, w_up, r_up, w_down, r_down),
    )

    chains = Chains()
    orders = ([2, 4], [4, 2])

    def piece_swaps(values, count, bit=0):
        size = values.shape[0] // count
        received = []
        for i in range(count):
            (got,) = yield [(values[i * size : (i + 1) * size], bit)]
            received.append(got)
        return received[0] if count == 1 else jnp.concatenate(received, 0)

    chains.add("grads", experts_sum(kept, sent, orders, far))
    chains.add("out", piece_swaps(out, 2))
    zero = jnp.zeros((1,), jnp.int32)
    one_minus = 1 - core[None]
    shared = (tables, seg_col, seg_row)

    low_grad = chains.advance(fence=low_grad)
    back = attend_back(zero, saved_c, *shared, low_grad, far_out)
    back = chains.advance(["grads"], fence=back)
    group_d, partial_sum = project(zero, back, saved_c[3], low_t, first_t, (far_qkv,))
    chains.add("other", piece_swaps(group_d, 1, 1))
    low_grad, partial_sum = chains.advance(["other", "out"], fence=(low_grad, partial_sum))
    back = attend_back(zero, saved_b, *shared, low_grad, near_out)
    back = chains.advance(["other"], fence=back)
    group_c, partial_sum = project(zero, back, saved_b[3], low_t, first_t, (near,), before=partial_sum)
    chains.add("theirs", piece_swaps(total([group_c, chains.done["other"]]), 1))
    low_grad, partial_sum = chains.advance(["grads", "out", "theirs"], fence=(low_grad, partial_sum))
    back = attend_back(one_minus, saved_a, *shared, low_grad, w_output)
    back = chains.advance(["grads"], fence=back)
    group_b, partial_sum = project(
        one_minus, back, saved_a[3], low_t, first_t, (w_query, w_key, w_value), before=partial_sum
    )
    chains.add("mine", piece_swaps(group_b, 1, 1))
    low_grad, partial_sum = chains.advance(["mine"], fence=(low_grad, partial_sum))
    back = attend_back(core[None], saved_a, *shared, low_grad, w_output)
    back = chains.advance(["grads", "mine", "theirs"], fence=back)
    group_a, token, norm_one = project(
        jnp.stack([core, side]), back, saved_a[3], low_t, first_t, (w_query, w_key, w_value),
        before=partial_sum, final=(tokens, gain_one, resid_grad),
    )
    chains.add("token", piece_swaps(token, 4))
    chains.add("tail", attention_sum((group_a, chains.done["mine"], chains.done["theirs"]), orders, far))
    chains.add("small", sum_all(jnp.concatenate([small, norm_one], 0)))

    def both(mine, other):
        return jnp.where(side == 0, jnp.concatenate([mine, other], 0), jnp.concatenate([other, mine], 0))

    place_far = place_of(far)
    size_far = 2 ** len(far)
    places = [place_of(order) * size_far + place_far for order in orders]
    done = chains.done
    finishers = {
        "out": lambda got: both(out, got),
        "token": lambda got: both(token, got).astype(f32),
        "grads": lambda got: unpack_experts(*got, places, core, dp_size // 2),
    }
    results = {}
    chains.advance(["token", "tail", "small"], fence=())
    while chains.live:
        ready = {n: f(done[n]) for n, f in finishers.items() if n in done and n not in results}
        results.update(chains.advance(fence=ready))
    for name, finisher in finishers.items():
        if name not in results:
            results[name] = finisher(done[name])
    grad_gate, grad_up, grad_down = results["grads"]
    own_tail, other_tail = done["tail"]
    grad_query, grad_key, grad_value, grad_output = unpack(own_tail, other_tail, places, core, dp_size // 2)
    small = done["small"]
    experts = w_router.shape[1]

    return (
        results["out"],
        results["token"],
        grad_query,
        grad_key,
        grad_value,
        grad_output,
        small[experts + 8],
        small[experts],
        small[:experts].T,
        grad_gate,
        grad_up,
        grad_down,
    )


def solution(mesh):
    placed = (
        P("dp", None), P("dp", None), P("dp"), P("dp", None), P("dp", None),
        P(None, "tensor"), P(None, "tensor"), P(None, "tensor"), P("tensor", None),
        P(), P(), P(),
        P(None, None, "tensor"), P(None, None, "tensor"), P(None, "tensor", None),
    )
    return jax.shard_map(
        per_device,
        mesh=mesh,
        in_specs=placed,
        out_specs=(
            P("dp", None), P("dp", None),
            P(None, "tensor"), P(None, "tensor"), P(None, "tensor"), P("tensor", None),
            P(), P(), P(),
            P(None, None, "tensor"), P(None, None, "tensor"), P(None, "tensor", None),
        ),
        check_vma=False,
    )
```
